128 devices in a mesh: row: 8 (over y_hi, x), col: 8 (over z, y_lo), layer: 2 (over core).
Axes of the slice: x: 4, y: 4 (y_hi: 2, y_lo: 2; y = y_hi * 2 + y_lo), z: 4, core: 2. Of those that a mesh axis runs over, the one named last changes fastest.
Arguments:
- similarity: bfloat16 [12288, 12288], P('row', ('col', 'layer')), may hold values from 0.049804688 to 1
- block_mask: int32 [96, 96], P('row', ('col', 'layer')), may hold values from 0 to 1, as said below
Outputs:
- normalized: float32 [12288, 12288], P('row', ('col', 'layer'))
The draws below stay inside these ranges and needn't reach their ends.
Inputs may be any that keep to these rules, and one draw needn't show every extreme that they name: Entries are 0 or 1; every diagonal block is 1; each device's share of block_mask holds at most 18 ones, and some device's share holds exactly 18.
All inputs are finite; a program needn't handle non-finite values.
Results may differ from the reference program's by a relative error of at most 0.0003.
Values may be sent and summed in bfloat16 or wider, within the bound.
A program may use at most 256 MiB of HBM per device.

```python
import jax
import jax.numpy as jnp

BLK = 128
NB_DEV = 6
NBLK = 96
N = 12288
MAXNZ = 18
N_ROW = 8


def draw_block_mask(key, part):
    key = jax.random.fold_in(key, 7)
    first_key, second_key, third_key = jax.random.split(key, 3)
    tile_rows = NBLK // N_ROW
    tile_cols = NBLK // NB_DEV
    tile_size = tile_rows * NB_DEV
    tile_keys = jax.random.split(first_key, N_ROW * tile_cols)
    ranks = jax.vmap(lambda k: jax.random.permutation(k, tile_size))(tile_keys)
    ranks = ranks.reshape(N_ROW, tile_cols, tile_size).astype(jnp.int32)
    diagonal = jnp.arange(NBLK)[:, None] == jnp.arange(NBLK)[None, :]
    diag_tiles = diagonal.reshape(N_ROW, tile_rows, tile_cols, NB_DEV).transpose(0, 2, 1, 3).reshape(N_ROW, tile_cols, tile_size)
    shifted = jnp.where(diag_tiles, ranks - tile_size, ranks)
    order = jnp.argsort(jnp.argsort(shifted, axis=-1, stable=True), axis=-1, stable=True).astype(jnp.int32)
    lowest = jnp.where(jnp.any(diag_tiles, axis=-1), NB_DEV, 1).astype(jnp.int32)
    spread = jax.random.randint(second_key, (N_ROW, tile_cols), 0, 4096)
    counts = lowest + spread % (MAXNZ + 1 - lowest)
    special = jax.random.randint(third_key, (), 0, N_ROW * tile_cols)
    places = jnp.arange(N_ROW * tile_cols).reshape(N_ROW, tile_cols)
    counts = jnp.where(places == special, MAXNZ, counts)
    chosen = order < counts[:, :, None]
    back = chosen.reshape(N_ROW, tile_cols, tile_rows, NB_DEV).transpose(0, 2, 1, 3).reshape(NBLK, NBLK)
    return jnp.where(back, 1, 0).astype(jnp.int32)


def steps_of(key, extent, cuts, low, top_value):
    def one(axis_at, shards_of):
        draws = jax.random.uniform(jax.random.fold_in(jax.random.fold_in(key, 6), axis_at), (shards_of,), jnp.float32, low / len(cuts), top_value / len(cuts))
        return jnp.repeat(jnp.exp(draws), extent[axis_at] // shards_of).reshape((-1,) + (1,) * (len(extent) - axis_at - 1))

    loudness = one(*cuts[0])
    for cut in cuts[1:]:
        loudness = loudness * one(*cut)
    return loudness


def setup_inputs(seed: int = 0) -> dict:
    splits = jax.random.split(jax.random.key(seed), 3)
    similarity = jnp.clip(0.049804688 + 0.9501953 * jax.random.uniform(splits[0], (N, N), jnp.float32) ** steps_of(splits[0], (N, N), ((0, 8), (1, 16)), -0.2, 0.2), 0.049804688, 1.0).astype(jnp.bfloat16)
    block_mask = draw_block_mask(jax.random.fold_in(splits[2], 71), 0)
    return {"similarity": similarity, "block_mask": block_mask}


def reference(similarity, block_mask):
    expanded = jnp.repeat(jnp.repeat(block_mask, BLK, 0), BLK, 1).astype(jnp.bfloat16)
    masked = similarity * expanded
    product = jnp.dot(masked, masked, preferred_element_type=jnp.float32)
    inflated = product * product
    totals = jnp.sum(inflated, axis=0)
    return (NBLK * BLK) * inflated / totals
```

```python
import functools

import jax
import jax.numpy as jnp
from jax import lax
from jax.experimental import pallas as pl
from jax.experimental.pallas import tpu as pltpu
from jax.sharding import PartitionSpec as P

BLK = 128
MAXNZ = 18
HEAD = 16
HALF = MAXNZ // 2
SHARE = HEAD + MAXNZ * BLK
CUT = HEAD + HALF * BLK
MIB = 1 << 20
MESH = pl.DeviceIdType.MESH


def pack_kernel(mask_ref, x_ref, share_ref, sems):
    rows, cols = mask_ref.shape
    base = (2 * lax.axis_index("col") + lax.axis_index("layer")) * cols
    sub = lax.broadcasted_iota(jnp.int32, (HEAD, BLK), 0)
    lane = lax.broadcasted_iota(jnp.int32, (HEAD, BLK), 1)

    def one_row(i, carry):
        count, head = carry
        for j in range(cols):
            here = mask_ref[i, j]

            @pl.when(here > 0)
            def _():
                pltpu.make_async_copy(
                    x_ref.at[pl.ds(i * BLK, BLK), pl.ds(j * BLK, BLK)],
                    share_ref.at[pl.ds(pl.multiple_of(HEAD + count * BLK, HEAD), BLK)],
                    sems.at[count],
                ).start()

            cell = (sub == i) & (lane == base + j)
            place = (sub == rows) & (lane == count)
            head = jnp.where(cell & (here > 0), count + 1, head)
            head = jnp.where(place & (here > 0), i * cols + j + 1, head)
            count = count + here
        return count, head

    count, head = lax.fori_loop(
        0, rows, one_row, (jnp.int32(0), jnp.zeros((HEAD, BLK), jnp.int32))
    )
    share_ref[pl.ds(0, HEAD), :] = head.astype(jnp.float32).astype(share_ref.dtype)
    for s in range(MAXNZ):

        @pl.when(s < count)
        def _():
            pltpu.make_async_copy(
                x_ref.at[pl.ds(0, BLK), pl.ds(0, BLK)],
                share_ref.at[pl.ds(HEAD + s * BLK, BLK)],
                sems.at[s],
            ).wait()


def pack(block_mask, similarity):
    return pl.pallas_call(
        pack_kernel,
        out_shape=pltpu.VMEM((SHARE, BLK), similarity.dtype),
        in_specs=[
            pl.BlockSpec(memory_space=pltpu.SMEM),
            pl.BlockSpec(memory_space=pltpu.HBM),
        ],
        out_specs=pl.BlockSpec(memory_space=pltpu.VMEM),
        scratch_shapes=[pltpu.SemaphoreType.DMA((MAXNZ,))],
        compiler_params=pltpu.CompilerParams(vmem_limit_bytes=4 * MIB),
        name="pack",
    )(block_mask, similarity)


def gather_kernel(share_ref, rows_ref, cols_ref, send_sems, recv_sems, own_sems):
    row, col, layer = (lax.axis_index(a) for a in ("row", "col", "layer"))
    high, x = row // 4, row % 4
    z, low = col // 2, col % 2

    def along_z(step):
        return 2 * ((z + step) % 4) + low

    def along_x(step):
        return 4 * high + (x + step) % 4

    mate = 2 * z + 1 - low
    far = 4 * (1 - high) + x

    zp, zm = (row, along_z(1), layer), (row, along_z(3), layer)
    xp, xm = (along_x(1), col, layer), (along_x(3), col, layer)
    lo, hi = (row, mate, layer), (far, mate, layer)
    sib = (row, col, 1 - layer)

    barrier = pltpu.get_barrier_semaphore()
    for peer in (zp, zm, xp, xm, lo, hi, sib):
        pl.semaphore_signal(barrier, inc=1, device_id=peer, device_id_type=MESH)
    pl.semaphore_wait(barrier, 7)

    mine = 2 * col + layer
    keep = [
        pltpu.make_async_copy(share_ref, rows_ref.at[mine], own_sems.at[0]),
        pltpu.make_async_copy(share_ref, cols_ref.at[row], own_sems.at[1]),
    ]
    for copy in keep:
        copy.start()

    H1, H2, ALL = pl.ds(0, CUT), pl.ds(CUT, SHARE - CUT), pl.ds(0, SHARE)
    n = [0]
    started = []

    def send(src, dst, part, peer):
        k = n[0]
        n[0] += 1
        copy = pltpu.make_async_remote_copy(
            src_ref=src.at[part],
            dst_ref=dst.at[part],
            send_sem=send_sems.at[k],
            recv_sem=recv_sems.at[k],
            device_id=peer,
            device_id_type=MESH,
        )
        copy.start()
        started.append(copy)
        return k

    waited = set()

    def arrived(k, dst, part, peer):
        waited.add(k)
        pltpu.make_async_remote_copy(
            src_ref=dst.at[part],
            dst_ref=dst.at[part],
            send_sem=send_sems.at[k],
            recv_sem=recv_sems.at[k],
            device_id=peer,
            device_id_type=MESH,
        ).wait_recv()

    def r(c):
        return rows_ref.at[2 * c + layer]

    def rsib(c):
        return rows_ref.at[2 * c + 1 - layer]

    def c(q):
        return cols_ref.at[q]

    own_r, own_c = r(col), c(row)
    lo1 = send(share_ref, own_r, H1, lo)
    zp1 = send(share_ref, own_r, H1, zp)
    zm2 = send(share_ref, own_r, H2, zm)
    xp1 = send(share_ref, own_c, H1, xp)
    xm2 = send(share_ref, own_c, H2, xm)
    lo2 = send(share_ref, own_r, H2, lo)
    zp2 = send(share_ref, own_r, H2, zp)
    zm1 = send(share_ref, own_r, H1, zm)
    xp2 = send(share_ref, own_c, H2, xp)
    xm1 = send(share_ref, own_c, H1, xm)
    sb0 = send(share_ref, own_r, ALL, sib)

    y_r = r(mate)
    arrived(lo1, y_r, H1, lo)
    hi1 = send(y_r, c(row), H1, hi)
    yzp1 = send(y_r, y_r, H1, zp)
    arrived(lo2, y_r, H2, lo)
    hi2 = send(y_r, c(row), H2, hi)
    yzm2 = send(y_r, y_r, H2, zm)

    zm_r, zp_r, zz_r = r(along_z(3)), r(along_z(1)), r(along_z(2))
    xm_c, xp_c, xx_c = c(along_x(3)), c(along_x(1)), c(along_x(2))
    arrived(zp1, zm_r, H1, zm)
    fzp = send(zm_r, zm_r, H1, zp)
    arrived(zm2, zp_r, H2, zp)
    fzm = send(zp_r, zp_r, H2, zm)
    arrived(xp1, xm_c, H1, xm)
    fxp = send(xm_c, xm_c, H1, xp)
    arrived(xm2, xp_c, H2, xp)
    fxm = send(xp_c, xp_c, H2, xm)
    yzp2 = send(y_r, y_r, H2, zp)
    yzm1 = send(y_r, y_r, H1, zm)
    sb1 = send(y_r, y_r, ALL, sib)

    y_c = c(far)
    arrived(hi1, y_c, H1, hi)
    yxp1 = send(y_c, y_c, H1, xp)
    arrived(hi2, y_c, H2, hi)
    yxm2 = send(y_c, y_c, H2, xm)
    yxp2 = send(y_c, y_c, H2, xp)
    yxm1 = send(y_c, y_c, H1, xm)

    def other(q):
        return q + 1 - 2 * (q % 2)

    ym_r, yp_r, yy_r = (r(other(along_z(s))) for s in (3, 1, 2))
    arrived(yzp1, ym_r, H1, zm)
    gzp = send(ym_r, ym_r, H1, zp)
    arrived(yzm2, yp_r, H2, zp)
    gzm = send(yp_r, yp_r, H2, zm)

    def across(q):
        return c((q + 4) % 8)

    ym_c, yp_c, yy_c = (across(along_x(s)) for s in (3, 1, 2))
    arrived(yxp1, ym_c, H1, xm)
    gxp = send(ym_c, ym_c, H1, xp)
    arrived(yxm2, yp_c, H2, xp)
    gxm = send(yp_c, yp_c, H2, xm)

    arrived(zp2, zm_r, H2, zm)
    sb2 = send(zm_r, zm_r, ALL, sib)
    arrived(zm1, zp_r, H1, zp)
    sb3 = send(zp_r, zp_r, ALL, sib)
    arrived(fzp, zz_r, H1, zm)
    arrived(fzm, zz_r, H2, zp)
    sb4 = send(zz_r, zz_r, ALL, sib)
    arrived(yzp2, ym_r, H2, zm)
    sb5 = send(ym_r, ym_r, ALL, sib)
    arrived(yzm1, yp_r, H1, zp)
    sb6 = send(yp_r, yp_r, ALL, sib)
    arrived(gzp, yy_r, H1, zm)
    sb7 = send(yy_r, yy_r, H1, sib)
    arrived(gzm, yy_r, H2, zp)
    sb8 = send(yy_r, yy_r, H2, sib)

    arrived(xp2, xm_c, H2, xm)
    arrived(xm1, xp_c, H1, xp)
    arrived(fxp, xx_c, H1, xm)
    arrived(fxm, xx_c, H2, xp)
    arrived(yxp2, ym_c, H2, xm)
    arrived(yxm1, yp_c, H1, xp)
    arrived(gxp, yy_c, H1, xm)
    arrived(gxm, yy_c, H2, xp)

    arrived(sb0, rsib(col), ALL, sib)
    arrived(sb1, rsib(mate), ALL, sib)
    arrived(sb2, rsib(along_z(3)), ALL, sib)
    arrived(sb3, rsib(along_z(1)), ALL, sib)
    arrived(sb4, rsib(along_z(2)), ALL, sib)
    arrived(sb5, rsib(other(along_z(3))), ALL, sib)
    arrived(sb6, rsib(other(along_z(1))), ALL, sib)
    arrived(sb7, rsib(other(along_z(2))), H1, sib)
    arrived(sb8, rsib(other(along_z(2))), H2, sib)
    assert waited == set(range(n[0])) and n[0] == COPIES
    for copy in started:
        copy.wait_send()
    for copy in keep:
        copy.wait()


COPIES = 37


def gather(share):
    return pl.pallas_call(
        gather_kernel,
        out_shape=[
            pltpu.VMEM((16, SHARE, BLK), share.dtype),
            pltpu.VMEM((8, SHARE, BLK), share.dtype),
        ],
        in_specs=[pl.BlockSpec(memory_space=pltpu.VMEM)],
        out_specs=[pl.BlockSpec(memory_space=pltpu.VMEM)] * 2,
        scratch_shapes=[
            pltpu.SemaphoreType.DMA((COPIES,)),
            pltpu.SemaphoreType.DMA((COPIES,)),
            pltpu.SemaphoreType.DMA((2,)),
        ],
        compiler_params=pltpu.CompilerParams(
            collective_id=0, has_side_effects=True, vmem_limit_bytes=32 * MIB
        ),
        name="gather",
    )(share)


GROUP = 4


def product_kernel(
    r_ref, c_ref, out_ref, sums_ref, dense, head_v, head_s, place_v, place_s, lists, sems
):
    tiles, lanes = out_ref.shape[0] // BLK, out_ref.shape[1]
    wide = lanes // BLK
    head = r_ref[0, pl.ds(0, HEAD), :].astype(jnp.float32)
    for s in range(1, 16):
        head = head + r_ref[s, pl.ds(0, HEAD), :].astype(jnp.float32)
    head_v[...] = head.astype(jnp.int32)
    for q in range(8):
        top = c_ref[q, pl.ds(0, HEAD), :].astype(jnp.float32).astype(jnp.int32)
        place_v[pl.ds(q, 1), :] = top[tiles : tiles + 1, :]
    copies = [
        pltpu.make_async_copy(head_v, head_s, sems.at[0]),
        pltpu.make_async_copy(place_v, place_s, sems.at[1]),
    ]
    for copy in copies:
        copy.start()

    @pl.loop(0, dense.shape[0] // 256)
    def _(t):
        dense[pl.ds(pl.multiple_of(t * 256, 256), 256), :] = jnp.zeros((256, lanes), dense.dtype)

    for copy in copies:
        copy.wait()

    @pl.loop(0, 8)
    def _(q):
        @pl.loop(0, MAXNZ)
        def _(s):
            v = place_s[q, s] - 1

            @pl.when(v >= 0)
            def _():
                k = q * tiles + v // wide
                j = v % wide
                dense[
                    pl.ds(pl.multiple_of(k * BLK, BLK), BLK),
                    pl.ds(pl.multiple_of(j * BLK, BLK), BLK),
                ] = c_ref[q, pl.ds(pl.multiple_of(HEAD + s * BLK, HEAD), BLK), :]

    sums_ref[...] = jnp.zeros(sums_ref.shape, jnp.float32)

    @pl.loop(0, tiles)
    def _(i):
        def look(k, count):
            v = head_s[i, k]
            lists[0, count] = k
            lists[1, count] = v - 1
            return count + jnp.where(v > 0, 1, 0)

        count = lax.fori_loop(0, 8 * tiles, look, jnp.int32(0), unroll=8)
        for t in range(GROUP):
            lists[0, count + t] = 0
            lists[1, count + t] = 0
        here = pl.ds(pl.multiple_of(i * BLK, BLK), BLK)

        def part(g):
            left, right = [], []
            for t in range(GROUP):
                p = g * GROUP + t
                k, v = lists[0, p], lists[1, p]
                a = r_ref[k // wide, pl.ds(pl.multiple_of(HEAD + v * BLK, HEAD), BLK), :]
                left.append(jnp.where(p < count, a, jnp.zeros_like(a)))
                right.append(dense[pl.ds(pl.multiple_of(k * BLK, BLK), BLK), :])
            return jnp.dot(
                jnp.concatenate(left, 1),
                jnp.concatenate(right, 0),
                preferred_element_type=jnp.float32,
            )

        out_ref[here, :] = part(0)

        @pl.loop(1, (count + GROUP - 1) // GROUP)
        def _(g):
            out_ref[here, :] += part(g)

        value = out_ref[here, :]
        value = value * value
        out_ref[here, :] = value
        sums_ref[...] += jnp.sum(value.reshape(BLK // 8, 8, lanes), axis=0)


def product(rows, cols, out_rows, lanes):
    return pl.pallas_call(
        product_kernel,
        out_shape=[
            pltpu.VMEM((out_rows, lanes), jnp.float32),
            pltpu.VMEM((8, lanes), jnp.float32),
        ],
        in_specs=[pl.BlockSpec(memory_space=pltpu.VMEM)] * 2,
        out_specs=[pl.BlockSpec(memory_space=pltpu.VMEM)] * 2,
        scratch_shapes=[
            pltpu.VMEM((8 * out_rows, lanes), rows.dtype),
            pltpu.VMEM((HEAD, BLK), jnp.int32),
            pltpu.SMEM((HEAD, BLK), jnp.int32),
            pltpu.VMEM((8, BLK), jnp.int32),
            pltpu.SMEM((8, BLK), jnp.int32),
            pltpu.SMEM((2, BLK), jnp.int32),
            pltpu.SemaphoreType.DMA((2,)),
        ],
        compiler_params=pltpu.CompilerParams(vmem_limit_bytes=24 * MIB),
        name="product",
    )(rows, cols)


def totals_kernel(sums_ref, out_ref, slots, send_sems, recv_sems):
    row, col, layer = (lax.axis_index(a) for a in ("row", "col", "layer"))
    barrier = pltpu.get_barrier_semaphore()
    peers = [((row + s) % 8, col, layer) for s in range(1, 8)]
    for peer in peers:
        pl.semaphore_signal(barrier, inc=1, device_id=peer, device_id_type=MESH)
    slots[row] = sums_ref[...]
    pl.semaphore_wait(barrier, 7)
    copies = [
        pltpu.make_async_remote_copy(
            src_ref=slots.at[row],
            dst_ref=slots.at[row],
            send_sem=send_sems.at[s],
            recv_sem=recv_sems.at[s],
            device_id=peer,
            device_id_type=MESH,
        )
        for s, peer in enumerate(peers)
    ]
    for copy in copies:
        copy.start()
    for copy in copies:
        copy.wait()
    total = slots[0]
    for q in range(1, 8):
        total = total + slots[q]
    out_ref[...] = jnp.sum(total, axis=0, keepdims=True)


def reduce_totals(sums):
    return pl.pallas_call(
        totals_kernel,
        out_shape=jax.ShapeDtypeStruct((1, sums.shape[1]), jnp.float32),
        in_specs=[pl.BlockSpec(memory_space=pltpu.VMEM)],
        out_specs=pl.BlockSpec(memory_space=pltpu.VMEM),
        scratch_shapes=[
            pltpu.VMEM((8,) + sums.shape, jnp.float32),
            pltpu.SemaphoreType.DMA((7,)),
            pltpu.SemaphoreType.DMA((7,)),
        ],
        compiler_params=pltpu.CompilerParams(
            collective_id=1, has_side_effects=True, vmem_limit_bytes=4 * MIB
        ),
        name="totals",
    )(sums)


def scale_kernel(scaling, value_ref, total_ref, out_ref):
    out_ref[...] = scaling * value_ref[...] / total_ref[...]


def scale(value, total, scaling, steps=6):
    rows, lanes = value.shape
    return pl.pallas_call(
        functools.partial(scale_kernel, scaling),
        grid=(steps,),
        out_shape=jax.ShapeDtypeStruct(value.shape, jnp.float32),
        in_specs=[
            pl.BlockSpec((rows // steps, lanes), lambda i: (i, 0)),
            pl.BlockSpec((1, lanes), lambda i: (0, 0)),
        ],
        out_specs=pl.BlockSpec((rows // steps, lanes), lambda i: (i, 0)),
        compiler_params=pltpu.CompilerParams(vmem_limit_bytes=16 * MIB),
        name="scale",
    )(value, total)


def body(similarity, block_mask):
    share = pack(block_mask, similarity)
    rows, cols = gather(share)
    value, sums = product(rows, cols, *similarity.shape)
    total = reduce_totals(sums)
    scaling = similarity.shape[0] * lax.axis_size("row")
    return scale(value, total, float(scaling))


def solution(mesh):
    return jax.shard_map(
        body,
        mesh=mesh,
        in_specs=(P("row", ("col", "layer")), P("row", ("col", "layer"))),
        out_specs=P("row", ("col", "layer")),
        check_vma=False,
    )
```

```python
import functools

import jax
import jax.numpy as jnp
from jax import lax
from jax.experimental import pallas as pl
from jax.experimental.pallas import tpu as pltpu
from jax.sharding import PartitionSpec as P

BLK = 128
MAXNZ = 18
HEAD = 32
HALF = MAXNZ // 2
SHARE = HEAD + MAXNZ * BLK
CUT = HEAD + HALF * BLK
MIB = 1 << 20
MESH = pl.DeviceIdType.MESH


def pack_kernel(mask_ref, x_ref, share_ref, sems):
    cols, rows = mask_ref.shape
    sub = lax.broadcasted_iota(jnp.int32, (HEAD, BLK), 0)
    lane = lax.broadcasted_iota(jnp.int32, (HEAD, BLK), 1)
    lane_row = (lane * 43) >> 8
    lane_col = lane - lane_row * cols

    def one_row(i, carry):
        count, head = carry
        below = 8 + jnp.where(i < cols, i, i - cols + 8)
        for j in range(cols):
            here = mask_ref[j, i]

            @pl.when(here > 0)
            def _():
                pltpu.make_async_copy(
                    x_ref.at[pl.ds(i * BLK, BLK), pl.ds(j * BLK, BLK)],
                    share_ref.at[pl.ds(pl.multiple_of(HEAD + count * BLK, HEAD), BLK)],
                    sems.at[count],
                ).start()

            cell = ((sub == j) & (lane_row == i)) | ((sub == below) & (lane_col == j))
            head = jnp.where(cell & (here > 0), count + 1, head)
            count = count + here
        return count, head

    count, head = lax.fori_loop(
        0, rows, one_row, (jnp.int32(0), jnp.zeros((HEAD, BLK), jnp.int32))
    )
    head = jnp.where(lane < rows * cols, head, 0)
    share_ref[pl.ds(0, HEAD), :] = head.astype(jnp.float32).astype(share_ref.dtype)
    for s in range(MAXNZ):

        @pl.when(s < count)
        def _():
            pltpu.make_async_copy(
                x_ref.at[pl.ds(0, BLK), pl.ds(0, BLK)],
                share_ref.at[pl.ds(HEAD + s * BLK, BLK)],
                sems.at[s],
            ).wait()


def pack(block_mask, similarity):
    return pl.pallas_call(
        pack_kernel,
        out_shape=pltpu.VMEM((SHARE, BLK), similarity.dtype),
        in_specs=[
            pl.BlockSpec(memory_space=pltpu.SMEM),
            pl.BlockSpec(memory_space=pl.ANY),
        ],
        out_specs=pl.BlockSpec(memory_space=pltpu.VMEM),
        scratch_shapes=[pltpu.SemaphoreType.DMA((MAXNZ,))],
        compiler_params=pltpu.CompilerParams(vmem_limit_bytes=56 * MIB),
        name="pack",
    )(block_mask.T, similarity)


def gather_kernel(share_ref, rows_ref, cols_ref, send_sems, recv_sems, own_sems):
    row, col, layer = (lax.axis_index(a) for a in ("row", "col", "layer"))
    high, x = row // 4, row % 4
    z, low = col // 2, col % 2

    def along_z(step):
        return 2 * ((z + step) % 4) + low

    def along_x(step):
        return 4 * high + (x + step) % 4

    mate = 2 * z + 1 - low
    far = 4 * (1 - high) + x

    zp, zm = (row, along_z(1), layer), (row, along_z(3), layer)
    xp, xm = (along_x(1), col, layer), (along_x(3), col, layer)
    lo, hi = (row, mate, layer), (far, mate, layer)
    sib = (row, col, 1 - layer)

    barrier = pltpu.get_barrier_semaphore()
    for peer in (zp, zm, xp, xm, lo, hi, sib):
        pl.semaphore_signal(barrier, inc=1, device_id=peer, device_id_type=MESH)
    pl.semaphore_wait(barrier, 7)

    mine = 2 * col + layer
    keep = [
        pltpu.make_async_copy(share_ref, rows_ref.at[mine], own_sems.at[0]),
        pltpu.make_async_copy(share_ref, cols_ref.at[row], own_sems.at[1]),
    ]
    for copy in keep:
        copy.start()

    H1, H2, ALL = pl.ds(0, CUT), pl.ds(CUT, SHARE - CUT), pl.ds(0, SHARE)
    n = [0]
    started = []

    def send(src, dst, part, peer):
        k = n[0]
        n[0] += 1
        copy = pltpu.make_async_remote_copy(
            src_ref=src.at[part],
            dst_ref=dst.at[part],
            send_sem=send_sems.at[k],
            recv_sem=recv_sems.at[k],
            device_id=peer,
            device_id_type=MESH,
        )
        copy.start()
        started.append(copy)
        return k

    waited = set()

    def arrived(k, dst, part, peer):
        waited.add(k)
        pltpu.make_async_remote_copy(
            src_ref=dst.at[part],
            dst_ref=dst.at[part],
            send_sem=send_sems.at[k],
            recv_sem=recv_sems.at[k],
            device_id=peer,
            device_id_type=MESH,
        ).wait_recv()

    def r(c):
        return rows_ref.at[2 * c + layer]

    def rsib(c):
        return rows_ref.at[2 * c + 1 - layer]

    def c(q):
        return cols_ref.at[q]

    own_r, own_c = r(col), c(row)
    lo1 = send(share_ref, own_r, H1, lo)
    zp1 = send(share_ref, own_r, H1, zp)
    zm2 = send(share_ref, own_r, H2, zm)
    xp1 = send(share_ref, own_c, H1, xp)
    xm2 = send(share_ref, own_c, H2, xm)
    lo2 = send(share_ref, own_r, H2, lo)
    zp2 = send(share_ref, own_r, H2, zp)
    zm1 = send(share_ref, own_r, H1, zm)
    xp2 = send(share_ref, own_c, H2, xp)
    xm1 = send(share_ref, own_c, H1, xm)
    sb0 = send(share_ref, own_r, ALL, sib)

    y_r = r(mate)
    arrived(lo1, y_r, H1, lo)
    hi1 = send(y_r, c(row), H1, hi)
    yzp1 = send(y_r, y_r, H1, zp)
    arrived(lo2, y_r, H2, lo)
    hi2 = send(y_r, c(row), H2, hi)
    yzm2 = send(y_r, y_r, H2, zm)

    zm_r, zp_r, zz_r = r(along_z(3)), r(along_z(1)), r(along_z(2))
    xm_c, xp_c, xx_c = c(along_x(3)), c(along_x(1)), c(along_x(2))
    arrived(zp1, zm_r, H1, zm)
    fzp = send(zm_r, zm_r, H1, zp)
    arrived(zm2, zp_r, H2, zp)
    fzm = send(zp_r, zp_r, H2, zm)
    arrived(xp1, xm_c, H1, xm)
    fxp = send(xm_c, xm_c, H1, xp)
    arrived(xm2, xp_c, H2, xp)
    fxm = send(xp_c, xp_c, H2, xm)
    yzp2 = send(y_r, y_r, H2, zp)
    yzm1 = send(y_r, y_r, H1, zm)
    sb1 = send(y_r, y_r, ALL, sib)

    y_c = c(far)
    arrived(hi1, y_c, H1, hi)
    yxp1 = send(y_c, y_c, H1, xp)
    arrived(hi2, y_c, H2, hi)
    yxm2 = send(y_c, y_c, H2, xm)
    yxp2 = send(y_c, y_c, H2, xp)
    yxm1 = send(y_c, y_c, H1, xm)

    def other(q):
        return q + 1 - 2 * (q % 2)

    ym_r, yp_r, yy_r = (r(other(along_z(s))) for s in (3, 1, 2))
    arrived(yzp1, ym_r, H1, zm)
    gzp = send(ym_r, ym_r, H1, zp)
    arrived(yzm2, yp_r, H2, zp)
    gzm = send(yp_r, yp_r, H2, zm)

    def across(q):
        return c((q + 4) % 8)

    ym_c, yp_c, yy_c = (across(along_x(s)) for s in (3, 1, 2))
    arrived(yxp1, ym_c, H1, xm)
    gxp = send(ym_c, ym_c, H1, xp)
    arrived(yxm2, yp_c, H2, xp)
    gxm = send(yp_c, yp_c, H2, xm)

    arrived(zp2, zm_r, H2, zm)
    sb2 = send(zm_r, zm_r, ALL, sib)
    arrived(zm1, zp_r, H1, zp)
    sb3 = send(zp_r, zp_r, ALL, sib)
    arrived(fzp, zz_r, H1, zm)
    arrived(fzm, zz_r, H2, zp)
    sb4 = send(zz_r, zz_r, ALL, sib)
    arrived(yzp2, ym_r, H2, zm)
    sb5 = send(ym_r, ym_r, ALL, sib)
    arrived(yzm1, yp_r, H1, zp)
    sb6 = send(yp_r, yp_r, ALL, sib)
    arrived(gzp, yy_r, H1, zm)
    sb7 = send(yy_r, yy_r, H1, sib)
    arrived(gzm, yy_r, H2, zp)
    sb8 = send(yy_r, yy_r, H2, sib)

    arrived(xp2, xm_c, H2, xm)
    arrived(xm1, xp_c, H1, xp)
    arrived(fxp, xx_c, H1, xm)
    arrived(fxm, xx_c, H2, xp)
    arrived(yxp2, ym_c, H2, xm)
    arrived(yxm1, yp_c, H1, xp)
    arrived(gxp, yy_c, H1, xm)
    arrived(gxm, yy_c, H2, xp)

    arrived(sb0, rsib(col), ALL, sib)
    arrived(sb1, rsib(mate), ALL, sib)
    arrived(sb2, rsib(along_z(3)), ALL, sib)
    arrived(sb3, rsib(along_z(1)), ALL, sib)
    arrived(sb4, rsib(along_z(2)), ALL, sib)
    arrived(sb5, rsib(other(along_z(3))), ALL, sib)
    arrived(sb6, rsib(other(along_z(1))), ALL, sib)
    arrived(sb7, rsib(other(along_z(2))), H1, sib)
    arrived(sb8, rsib(other(along_z(2))), H2, sib)
    assert waited == set(range(n[0])) and n[0] == COPIES
    for copy in started:
        copy.wait_send()
    for copy in keep:
        copy.wait()


COPIES = 37


def gather(share):
    return pl.pallas_call(
        gather_kernel,
        out_shape=[
            pltpu.VMEM((16, SHARE, BLK), share.dtype),
            pltpu.VMEM((8, SHARE, BLK), share.dtype),
        ],
        in_specs=[pl.BlockSpec(memory_space=pltpu.VMEM)],
        out_specs=[pl.BlockSpec(memory_space=pltpu.VMEM)] * 2,
        scratch_shapes=[
            pltpu.SemaphoreType.DMA((COPIES,)),
            pltpu.SemaphoreType.DMA((COPIES,)),
            pltpu.SemaphoreType.DMA((2,)),
        ],
        compiler_params=pltpu.CompilerParams(
            collective_id=0, has_side_effects=True, vmem_limit_bytes=32 * MIB
        ),
        name="gather",
    )(share)


GROUP = 4
DEPTH = 16


def product_kernel(r_ref, c_ref, out_ref, sums_ref, table_v, table_s, sem):
    tiles, lanes = out_ref.shape[0] // BLK, out_ref.shape[1]
    wide = lanes // BLK
    col = lax.axis_index("col")

    hr, hc = [], []
    for q in range(16):
        hr.append(r_ref[q, pl.ds(0, HEAD), :].astype(jnp.float32)[0:8])
    for q in range(8):
        top = c_ref[q, pl.ds(0, HEAD), :].astype(jnp.float32)
        hc += [top[8:16], top[16:24]]
    hr, hc = jnp.concatenate(hr, 0), jnp.concatenate(hc, 0)
    both = (hr > 0) & (hc > 0)
    line = lax.broadcasted_iota(jnp.int32, (BLK, BLK), 0)
    rank = jnp.dot(
        (line > lax.broadcasted_iota(jnp.int32, (BLK, BLK), 1)).astype(jnp.bfloat16),
        both.astype(jnp.float32).astype(jnp.bfloat16),
        preferred_element_type=jnp.float32,
    )
    rank = jnp.where(both, rank, -1.0).astype(jnp.int32)
    place_r = (line >> 3) * SHARE + (HEAD - BLK) + hr.astype(jnp.int32) * BLK
    place_c = (line >> 4) * SHARE + (HEAD - BLK) + hc.astype(jnp.int32) * BLK
    count = jnp.sum(both.astype(jnp.int32), axis=0, keepdims=True)
    most = jnp.max(count)
    idle_c = col * SHARE + HEAD

    def fill(done):
        for p in range(DEPTH):
            at = rank == done + p
            some = count > done + p
            first = jnp.sum(jnp.where(at, place_r, 0), axis=0, keepdims=True)
            second = jnp.sum(jnp.where(at, place_c, 0), axis=0, keepdims=True)
            table_v[pl.ds(p, 1), :] = jnp.where(some, first, HEAD)
            table_v[pl.ds(DEPTH + p, 1), :] = jnp.where(some, second, idle_c)
        table_v[pl.ds(2 * DEPTH, 1), :] = jnp.clip(count - done, 0, DEPTH)
        copy = pltpu.make_async_copy(table_v, table_s, sem)
        copy.start()
        copy.wait()

    def part(i, j, g):
        cell = i * wide + j
        left, right = [], []
        have = table_s[2 * DEPTH, cell]
        for t in range(GROUP):
            p = g * GROUP + t
            a = r_ref[pl.ds(pl.multiple_of(table_s[p, cell], HEAD), BLK), :]
            left.append(jnp.where(p < have, a, jnp.zeros_like(a)))
            right.append(c_ref[pl.ds(pl.multiple_of(table_s[DEPTH + p, cell], HEAD), BLK), :])
        return jnp.dot(
            jnp.concatenate(left, 1),
            jnp.concatenate(right, 0),
            preferred_element_type=jnp.float32,
        )

    def more(i, j, first):
        here = pl.ds(pl.multiple_of(i * BLK, BLK), BLK)

        @pl.loop(first, (table_s[2 * DEPTH, i * wide + j] + GROUP - 1) // GROUP)
        def _(g):
            out_ref[here, pl.ds(j * BLK, BLK)] += part(i, j, g)

    fill(0)
    r_ref = r_ref.reshape(16 * SHARE, BLK)
    c_ref = c_ref.reshape(8 * SHARE, BLK)

    @pl.loop(0, tiles)
    def _(i):
        here = pl.ds(pl.multiple_of(i * BLK, BLK), BLK)
        for j in range(wide):
            out_ref[here, pl.ds(j * BLK, BLK)] = part(i, j, 0)
        for j in range(wide):
            more(i, j, 1)

    @pl.loop(1, (most + DEPTH - 1) // DEPTH)
    def _(d):
        fill(d * DEPTH)

        @pl.loop(0, tiles)
        def _(i):
            for j in range(wide):
                more(i, j, 0)

    def square(t, total):
        here = pl.ds(pl.multiple_of(t * 64, 64), 64)
        value = out_ref[here, :]
        value = value * value
        out_ref[here, :] = value
        return total + jnp.sum(value.reshape(8, 8, lanes), axis=0)

    sums_ref[...] = lax.fori_loop(
        0, tiles * BLK // 64, square, jnp.zeros((8, lanes), jnp.float32)
    )


def product(rows, cols, out_rows, lanes):
    return pl.pallas_call(
        product_kernel,
        out_shape=[
            pltpu.VMEM((out_rows, lanes), jnp.float32),
            pltpu.VMEM((8, lanes), jnp.float32),
        ],
        in_specs=[pl.BlockSpec(memory_space=pltpu.VMEM)] * 2,
        out_specs=[pl.BlockSpec(memory_space=pltpu.VMEM)] * 2,
        scratch_shapes=[
            pltpu.VMEM((2 * DEPTH + 8, BLK), jnp.int32),
            pltpu.SMEM((2 * DEPTH + 8, BLK), jnp.int32),
            pltpu.SemaphoreType.DMA(()),
        ],
        compiler_params=pltpu.CompilerParams(vmem_limit_bytes=8 * MIB),
        name="product",
    )(rows, cols)


def totals_kernel(sums_ref, out_ref, slots, send_sems, recv_sems):
    row, col, layer = (lax.axis_index(a) for a in ("row", "col", "layer"))
    barrier = pltpu.get_barrier_semaphore()
    peers = [((row + s) % 8, col, layer) for s in range(1, 8)]
    for peer in peers:
        pl.semaphore_signal(barrier, inc=1, device_id=peer, device_id_type=MESH)
    slots[row] = sums_ref[...]
    pl.semaphore_wait(barrier, 7)
    copies = [
        pltpu.make_async_remote_copy(
            src_ref=slots.at[row],
            dst_ref=slots.at[row],
            send_sem=send_sems.at[s],
            recv_sem=recv_sems.at[s],
            device_id=peer,
            device_id_type=MESH,
        )
        for s, peer in enumerate(peers)
    ]
    for copy in copies:
        copy.start()
    for copy in copies:
        copy.wait()
    total = slots[0]
    for q in range(1, 8):
        total = total + slots[q]
    out_ref[...] = jnp.sum(total, axis=0, keepdims=True)


def reduce_totals(sums):
    return pl.pallas_call(
        totals_kernel,
        out_shape=jax.ShapeDtypeStruct((1, sums.shape[1]), jnp.float32),
        in_specs=[pl.BlockSpec(memory_space=pltpu.VMEM)],
        out_specs=pl.BlockSpec(memory_space=pltpu.VMEM),
        scratch_shapes=[
            pltpu.VMEM((8,) + sums.shape, jnp.float32),
            pltpu.SemaphoreType.DMA((7,)),
            pltpu.SemaphoreType.DMA((7,)),
        ],
        compiler_params=pltpu.CompilerParams(
            collective_id=1, has_side_effects=True, vmem_limit_bytes=4 * MIB
        ),
        name="totals",
    )(sums)


STEPS = 6


def scale_kernel(scaling, value_ref, total_ref, out_ref, staged, sems):
    step = staged.shape[1]
    total = total_ref[...]
    copies = []
    for t in range(STEPS):
        here = pl.ds(t * step, step)
        staged[t] = scaling * value_ref[here, :] / total
        copy = pltpu.make_async_copy(staged.at[t], out_ref.at[here], sems.at[t])
        copy.start()
        copies.append(copy)
    for copy in copies:
        copy.wait()


def scale(value, total, scaling):
    rows, lanes = value.shape
    return pl.pallas_call(
        functools.partial(scale_kernel, scaling),
        out_shape=jax.ShapeDtypeStruct(value.shape, jnp.float32),
        in_specs=[pl.BlockSpec(memory_space=pltpu.VMEM)] * 2,
        out_specs=pl.BlockSpec(memory_space=pltpu.HBM),
        scratch_shapes=[
            pltpu.VMEM((STEPS, rows // STEPS, lanes), jnp.float32),
            pltpu.SemaphoreType.DMA((STEPS,)),
        ],
        compiler_params=pltpu.CompilerParams(vmem_limit_bytes=16 * MIB),
        name="scale",
    )(value, total)


def body(similarity, block_mask):
    share = pack(block_mask, similarity)
    rows, cols = gather(share)
    value, sums = product(rows, cols, *similarity.shape)
    total = reduce_totals(sums)
    scaling = similarity.shape[0] * lax.axis_size("row")
    return scale(value, total, float(scaling))


def solution(mesh):
    return jax.shard_map(
        body,
        mesh=mesh,
        in_specs=(P("row", ("col", "layer")), P("row", ("col", "layer"))),
        out_specs=P("row", ("col", "layer")),
        check_vma=False,
    )
```

```python
import functools

import jax
import jax.numpy as jnp
from jax import lax
from jax.experimental import pallas as pl
from jax.experimental.pallas import tpu as pltpu
from jax.sharding import PartitionSpec as P

BLK = 128
MAXNZ = 18
HEAD = 32
HALF = MAXNZ // 2
SHARE = HEAD + MAXNZ * BLK
MIB = 1 << 20
MESH = pl.DeviceIdType.MESH


def pack_kernel(mask_ref, x_ref, share_ref, sems):
    cols, rows = mask_ref.shape
    sub = lax.broadcasted_iota(jnp.int32, (HEAD, BLK), 0)
    lane = lax.broadcasted_iota(jnp.int32, (HEAD, BLK), 1)
    lane_row = (lane * 43) >> 8
    lane_col = lane - lane_row * cols

    def one_row(i, carry):
        count, head = carry
        below = 8 + jnp.where(i < cols, i, i - cols + 8)
        for j in range(cols):
            here = mask_ref[j, i]

            @pl.when(here > 0)
            def _():
                pltpu.make_async_copy(
                    x_ref.at[pl.ds(i * BLK, BLK), pl.ds(j * BLK, BLK)],
                    share_ref.at[pl.ds(pl.multiple_of(HEAD + count * BLK, HEAD), BLK)],
                    sems.at[count],
                ).start()

            cell = ((sub == j) & (lane_row == i)) | ((sub == below) & (lane_col == j))
            head = jnp.where(cell & (here > 0), count + 1, head)
            count = count + here
        return count, head

    count, head = lax.fori_loop(
        0, rows, one_row, (jnp.int32(0), jnp.zeros((HEAD, BLK), jnp.int32))
    )
    head = jnp.where(lane < rows * cols, head, 0)
    share_ref[pl.ds(0, HEAD), :] = head.astype(jnp.float32).astype(share_ref.dtype)
    for s in range(MAXNZ):

        @pl.when(s < count)
        def _():
            pltpu.make_async_copy(
                x_ref.at[pl.ds(0, BLK), pl.ds(0, BLK)],
                share_ref.at[pl.ds(HEAD + s * BLK, BLK)],
                sems.at[s],
            ).wait()


def pack(block_mask, similarity):
    return pl.pallas_call(
        pack_kernel,
        out_shape=pltpu.VMEM((SHARE, BLK), similarity.dtype),
        in_specs=[
            pl.BlockSpec(memory_space=pltpu.SMEM),
            pl.BlockSpec(memory_space=pl.ANY),
        ],
        out_specs=pl.BlockSpec(memory_space=pltpu.VMEM),
        scratch_shapes=[pltpu.SemaphoreType.DMA((MAXNZ,))],
        compiler_params=pltpu.CompilerParams(vmem_limit_bytes=56 * MIB),
        name="pack",
    )(block_mask.T, similarity)


LAST = 5
SPLIT = 7


def span(first, last):
    low = HEAD + first * BLK if first else 0
    return pl.ds(low, HEAD + last * BLK - low)


def gather_kernel(
    share_ref, rows_ref, cols_ref, relay, send_sems, recv_sems, own_sems
):
    row, col, layer = (lax.axis_index(a) for a in ("row", "col", "layer"))
    high, x = row // 4, row % 4
    z, low = col // 2, col % 2

    def along_z(step):
        return 2 * ((z + step) % 4) + low

    def along_x(step):
        return 4 * high + (x + step) % 4

    mate = 2 * z + 1 - low
    far = 4 * (1 - high) + x

    zp, zm = (row, along_z(1), layer), (row, along_z(3), layer)
    xp, xm = (along_x(1), col, layer), (along_x(3), col, layer)
    lo, hi = (row, mate, layer), (far, mate, layer)
    sib = (row, col, 1 - layer)

    barrier = pltpu.get_barrier_semaphore()
    for peer in (zp, zm, xp, xm, lo, hi, sib):
        pl.semaphore_signal(barrier, inc=1, device_id=peer, device_id_type=MESH)
    pl.semaphore_wait(barrier, 7)

    mine = 2 * col + layer
    keep = [
        pltpu.make_async_copy(share_ref, rows_ref.at[mine], own_sems.at[0]),
        pltpu.make_async_copy(share_ref, cols_ref.at[row], own_sems.at[1]),
    ]

    EARLY = MAXNZ - LAST
    ALL = span(0, MAXNZ)
    H1, H2 = span(0, HALF), span(HALF, MAXNZ)
    U1, U2, U, L = span(0, SPLIT), span(SPLIT, EARLY), span(0, EARLY), span(EARLY, MAXNZ)
    T = pl.ds(0, LAST * BLK)
    started = []
    waited = set()

    def send(src, dst, part, peer, into=None):
        k = len(started)
        copy = pltpu.make_async_remote_copy(
            src_ref=src.at[part],
            dst_ref=dst.at[part if into is None else into],
            send_sem=send_sems.at[k],
            recv_sem=recv_sems.at[k],
            device_id=peer,
            device_id_type=MESH,
        )
        copy.start()
        started.append(copy)
        return k

    def arrived(k, dst, part, peer):
        waited.add(k)
        pltpu.make_async_remote_copy(
            src_ref=dst.at[part],
            dst_ref=dst.at[part],
            send_sem=send_sems.at[k],
            recv_sem=recv_sems.at[k],
            device_id=peer,
            device_id_type=MESH,
        ).wait_recv()

    def other(q):
        return q + 1 - 2 * (q % 2)

    def r(q):
        return rows_ref.at[2 * q + layer]

    def rsib(q):
        return rows_ref.at[2 * q + 1 - layer]

    def c(q):
        return cols_ref.at[q]

    def across(q):
        return c((q + 4) % 8)

    own_r, own_c = r(col), c(row)
    y_r, y_c = r(mate), c(far)
    zm_r, zp_r, zz_r = (r(along_z(s)) for s in (3, 1, 2))
    ym_r, yp_r, yy_r = (r(other(along_z(s))) for s in (3, 1, 2))
    xm_c, xp_c, xx_c = (c(along_x(s)) for s in (3, 1, 2))
    ym_c, yp_c, yy_c = (across(along_x(s)) for s in (3, 1, 2))

    lo1 = send(share_ref, own_r, U1, lo)
    zp1 = send(share_ref, own_r, H1, zp)
    zm2 = send(share_ref, own_r, H2, zm)
    xp1 = send(share_ref, own_c, H1, xp)
    xm2 = send(share_ref, own_c, H2, xm)
    lo2 = send(share_ref, own_r, U2, lo)
    zp2 = send(share_ref, own_r, H2, zp)
    zm1 = send(share_ref, own_r, H1, zm)
    xp2 = send(share_ref, own_c, H2, xp)
    xm1 = send(share_ref, own_c, H1, xm)
    lo3 = send(share_ref, own_r, L, lo)
    sb0 = send(share_ref, own_r, ALL, sib)
    for copy in keep:
        copy.start()

    arrived(lo1, y_r, U1, lo)
    hi1 = send(y_r, own_c, U1, hi)
    arrived(zp1, zm_r, H1, zm)
    fzp = send(zm_r, zm_r, H1, zp)
    arrived(zm2, zp_r, H2, zp)
    fzm = send(zp_r, zp_r, H2, zm)
    arrived(xp1, xm_c, H1, xm)
    fxp = send(xm_c, xm_c, H1, xp)
    arrived(xm2, xp_c, H2, xp)
    fxm = send(xp_c, xp_c, H2, xm)
    lzp = send(zp_r, zp_r, L, lo)
    txp = send(xp_c, relay.at[0], L, lo, T)
    yzp1 = send(y_r, y_r, U1, zp)
    arrived(lo2, y_r, U2, lo)
    hi2 = send(y_r, own_c, U2, hi)
    yzm2 = send(y_r, y_r, U2, zm)
    yzp2 = send(y_r, y_r, U2, zp)
    yzm1 = send(y_r, y_r, U1, zm)
    arrived(hi1, y_c, U1, hi)
    yxp1 = send(y_c, y_c, U1, xp)
    arrived(lo3, y_r, L, lo)
    hi3 = send(y_r, own_c, L, hi)
    sb1 = send(y_r, y_r, ALL, sib)

    arrived(zp2, zm_r, H2, zm)
    lzm = send(zm_r, zm_r, L, lo)
    sb2 = send(zm_r, zm_r, ALL, sib)
    arrived(xp2, xm_c, H2, xm)
    txm = send(xm_c, relay.at[1], L, lo, T)
    arrived(zm1, zp_r, H1, zp)
    sb3 = send(zp_r, zp_r, ALL, sib)
    arrived(hi2, y_c, U2, hi)
    yxm2 = send(y_c, y_c, U2, xm)
    yxp2 = send(y_c, y_c, U2, xp)
    yxm1 = send(y_c, y_c, U1, xm)
    arrived(txp, relay.at[0], T, lo)
    uxp = send(relay.at[0], xp_c, T, hi, L)
    arrived(fzm, zz_r, H2, zp)
    lzz = send(zz_r, zz_r, L, lo)
    arrived(fxm, xx_c, H2, xp)
    txx = send(xx_c, relay.at[2], L, lo, T)
    arrived(fzp, zz_r, H1, zm)
    sb4 = send(zz_r, zz_r, ALL, sib)
    arrived(txm, relay.at[1], T, lo)
    uxm = send(relay.at[1], xm_c, T, hi, L)

    arrived(yzp1, ym_r, U1, zm)
    gzp = send(ym_r, ym_r, U1, zp)
    arrived(yzm2, yp_r, U2, zp)
    gzm = send(yp_r, yp_r, U2, zm)
    arrived(yxp1, ym_c, U1, xm)
    gxp = send(ym_c, ym_c, U1, xp)
    arrived(yxm2, yp_c, U2, xp)
    gxm = send(yp_c, yp_c, U2, xm)
    arrived(lzp, yp_r, L, lo)
    arrived(yzm1, yp_r, U1, zp)
    sb5 = send(yp_r, yp_r, ALL, sib)
    arrived(txx, relay.at[2], T, lo)
    uxx = send(relay.at[2], xx_c, T, hi, L)
    arrived(yzp2, ym_r, U2, zm)
    arrived(lzm, ym_r, L, lo)
    sb6 = send(ym_r, ym_r, ALL, sib)
    arrived(lzz, yy_r, L, lo)
    sb7 = send(yy_r, yy_r, L, sib)
    arrived(gzp, yy_r, U1, zm)
    sb8 = send(yy_r, yy_r, U1, sib)
    arrived(gzm, yy_r, U2, zp)
    sb9 = send(yy_r, yy_r, U2, sib)

    arrived(hi3, y_c, L, hi)
    arrived(xm1, xp_c, H1, xp)
    arrived(fxp, xx_c, H1, xm)
    arrived(yxp2, ym_c, U2, xm)
    arrived(yxm1, yp_c, U1, xp)
    arrived(uxp, yp_c, L, hi)
    arrived(uxm, ym_c, L, hi)
    arrived(uxx, yy_c, L, hi)
    arrived(gxp, yy_c, U1, xm)
    arrived(gxm, yy_c, U2, xp)

    arrived(sb0, rsib(col), ALL, sib)
    arrived(sb1, rsib(mate), ALL, sib)
    arrived(sb2, rsib(along_z(3)), ALL, sib)
    arrived(sb3, rsib(along_z(1)), ALL, sib)
    arrived(sb4, rsib(along_z(2)), ALL, sib)
    arrived(sb5, rsib(other(along_z(1))), ALL, sib)
    arrived(sb6, rsib(other(along_z(3))), ALL, sib)
    arrived(sb7, rsib(other(along_z(2))), L, sib)
    arrived(sb8, rsib(other(along_z(2))), U1, sib)
    arrived(sb9, rsib(other(along_z(2))), U2, sib)
    assert waited == set(range(len(started))) and len(started) == COPIES
    for copy in started:
        copy.wait_send()
    for copy in keep:
        copy.wait()


COPIES = 49


def gather(share):
    return pl.pallas_call(
        gather_kernel,
        out_shape=[
            pltpu.VMEM((16, SHARE, BLK), share.dtype),
            pltpu.VMEM((8, SHARE, BLK), share.dtype),
        ],
        in_specs=[pl.BlockSpec(memory_space=pltpu.VMEM)],
        out_specs=[pl.BlockSpec(memory_space=pltpu.VMEM)] * 2,
        scratch_shapes=[
            pltpu.VMEM((3, LAST * BLK, BLK), share.dtype),
            pltpu.SemaphoreType.DMA((COPIES,)),
            pltpu.SemaphoreType.DMA((COPIES,)),
            pltpu.SemaphoreType.DMA((2,)),
        ],
        compiler_params=pltpu.CompilerParams(
            collective_id=0, has_side_effects=True, vmem_limit_bytes=32 * MIB
        ),
        name="gather",
    )(share)


GROUP = 4
DEPTH = 16


def product_kernel(r_ref, c_ref, out_ref, sums_ref, table_v, table_s, sem):
    tiles, lanes = out_ref.shape[0] // BLK, out_ref.shape[1]
    wide = lanes // BLK
    col = lax.axis_index("col")

    hr, hc = [], []
    for q in range(16):
        hr.append(r_ref[q, pl.ds(0, HEAD), :].astype(jnp.float32)[0:8])
    for q in range(8):
        top = c_ref[q, pl.ds(0, HEAD), :].astype(jnp.float32)
        hc += [top[8:16], top[16:24]]
    hr, hc = jnp.concatenate(hr, 0), jnp.concatenate(hc, 0)
    both = (hr > 0) & (hc > 0)
    line = lax.broadcasted_iota(jnp.int32, (BLK, BLK), 0)
    rank = jnp.dot(
        (line > lax.broadcasted_iota(jnp.int32, (BLK, BLK), 1)).astype(jnp.bfloat16),
        both.astype(jnp.float32).astype(jnp.bfloat16),
        preferred_element_type=jnp.float32,
    )
    rank = jnp.where(both, rank, -1.0).astype(jnp.int32)
    place_r = (line >> 3) * SHARE + (HEAD - BLK) + hr.astype(jnp.int32) * BLK
    place_c = (line >> 4) * SHARE + (HEAD - BLK) + hc.astype(jnp.int32) * BLK
    count = jnp.sum(both.astype(jnp.int32), axis=0, keepdims=True)
    most = jnp.max(count)
    idle_c = col * SHARE + HEAD

    def fill(done):
        for p in range(DEPTH):
            at = rank == done + p
            some = count > done + p
            first = jnp.sum(jnp.where(at, place_r, 0), axis=0, keepdims=True)
            second = jnp.sum(jnp.where(at, place_c, 0), axis=0, keepdims=True)
            table_v[pl.ds(p, 1), :] = jnp.where(some, first, HEAD)
            table_v[pl.ds(DEPTH + p, 1), :] = jnp.where(some, second, idle_c)
        table_v[pl.ds(2 * DEPTH, 1), :] = jnp.clip(count - done, 0, DEPTH)
        copy = pltpu.make_async_copy(table_v, table_s, sem)
        copy.start()
        copy.wait()

    def part(i, j, g):
        cell = i * wide + j
        left, right = [], []
        have = table_s[2 * DEPTH, cell]
        for t in range(GROUP):
            p = g * GROUP + t
            a = r_ref[pl.ds(pl.multiple_of(table_s[p, cell], HEAD), BLK), :]
            left.append(jnp.where(p < have, a, jnp.zeros_like(a)))
            right.append(c_ref[pl.ds(pl.multiple_of(table_s[DEPTH + p, cell], HEAD), BLK), :])
        return jnp.dot(
            jnp.concatenate(left, 1),
            jnp.concatenate(right, 0),
            preferred_element_type=jnp.float32,
        )

    def more(i, j, first):
        here = pl.ds(pl.multiple_of(i * BLK, BLK), BLK)

        @pl.loop(first, (table_s[2 * DEPTH, i * wide + j] + GROUP - 1) // GROUP)
        def _(g):
            out_ref[here, pl.ds(j * BLK, BLK)] += part(i, j, g)

    fill(0)
    r_ref = r_ref.reshape(16 * SHARE, BLK)
    c_ref = c_ref.reshape(8 * SHARE, BLK)

    @pl.loop(0, tiles)
    def _(i):
        here = pl.ds(pl.multiple_of(i * BLK, BLK), BLK)
        for j in range(wide):
            out_ref[here, pl.ds(j * BLK, BLK)] = part(i, j, 0)
        for j in range(wide):
            more(i, j, 1)

    @pl.loop(1, (most + DEPTH - 1) // DEPTH)
    def _(d):
        fill(d * DEPTH)

        @pl.loop(0, tiles)
        def _(i):
            for j in range(wide):
                more(i, j, 0)

    def square(t, total):
        here = pl.ds(pl.multiple_of(t * 64, 64), 64)
        value = out_ref[here, :]
        value = value * value
        out_ref[here, :] = value
        return total + jnp.sum(value.reshape(8, 8, lanes), axis=0)

    sums_ref[...] = lax.fori_loop(
        0, tiles * BLK // 64, square, jnp.zeros((8, lanes), jnp.float32)
    )


def product(rows, cols, out_rows, lanes):
    return pl.pallas_call(
        product_kernel,
        out_shape=[
            pltpu.VMEM((out_rows, lanes), jnp.float32),
            pltpu.VMEM((8, lanes), jnp.float32),
        ],
        in_specs=[pl.BlockSpec(memory_space=pltpu.VMEM)] * 2,
        out_specs=[pl.BlockSpec(memory_space=pltpu.VMEM)] * 2,
        scratch_shapes=[
            pltpu.VMEM((2 * DEPTH + 8, BLK), jnp.int32),
            pltpu.SMEM((2 * DEPTH + 8, BLK), jnp.int32),
            pltpu.SemaphoreType.DMA(()),
        ],
        compiler_params=pltpu.CompilerParams(vmem_limit_bytes=8 * MIB),
        name="product",
    )(rows, cols)


def totals_kernel(sums_ref, out_ref, slots, send_sems, recv_sems):
    row, col, layer = (lax.axis_index(a) for a in ("row", "col", "layer"))
    barrier = pltpu.get_barrier_semaphore()
    peers = [((row + s) % 8, col, layer) for s in range(1, 8)]
    for peer in peers:
        pl.semaphore_signal(barrier, inc=1, device_id=peer, device_id_type=MESH)
    slots[row] = sums_ref[...]
    pl.semaphore_wait(barrier, 7)
    copies = [
        pltpu.make_async_remote_copy(
            src_ref=slots.at[row],
            dst_ref=slots.at[row],
            send_sem=send_sems.at[s],
            recv_sem=recv_sems.at[s],
            device_id=peer,
            device_id_type=MESH,
        )
        for s, peer in enumerate(peers)
    ]
    for copy in copies:
        copy.start()
    for copy in copies:
        copy.wait()
    total = slots[0]
    for q in range(1, 8):
        total = total + slots[q]
    out_ref[...] = jnp.sum(total, axis=0, keepdims=True)


def reduce_totals(sums):
    return pl.pallas_call(
        totals_kernel,
        out_shape=jax.ShapeDtypeStruct((1, sums.shape[1]), jnp.float32),
        in_specs=[pl.BlockSpec(memory_space=pltpu.VMEM)],
        out_specs=pl.BlockSpec(memory_space=pltpu.VMEM),
        scratch_shapes=[
            pltpu.VMEM((8,) + sums.shape, jnp.float32),
            pltpu.SemaphoreType.DMA((7,)),
            pltpu.SemaphoreType.DMA((7,)),
        ],
        compiler_params=pltpu.CompilerParams(
            collective_id=1, has_side_effects=True, vmem_limit_bytes=4 * MIB
        ),
        name="totals",
    )(sums)


STEPS = 6


def scale_kernel(scaling, value_ref, total_ref, out_ref, staged, sems):
    step = staged.shape[1]
    total = total_ref[...]
    copies = []
    for t in range(STEPS):
        here = pl.ds(t * step, step)
        staged[t] = scaling * value_ref[here, :] / total
        copy = pltpu.make_async_copy(staged.at[t], out_ref.at[here], sems.at[t])
        copy.start()
        copies.append(copy)
    for copy in copies:
        copy.wait()


def scale(value, total, scaling):
    rows, lanes = value.shape
    return pl.pallas_call(
        functools.partial(scale_kernel, scaling),
        out_shape=jax.ShapeDtypeStruct(value.shape, jnp.float32),
        in_specs=[pl.BlockSpec(memory_space=pltpu.VMEM)] * 2,
        out_specs=pl.BlockSpec(memory_space=pltpu.HBM),
        scratch_shapes=[
            pltpu.VMEM((STEPS, rows // STEPS, lanes), jnp.float32),
            pltpu.SemaphoreType.DMA((STEPS,)),
        ],
        compiler_params=pltpu.CompilerParams(vmem_limit_bytes=16 * MIB),
        name="scale",
    )(value, total)


def body(similarity, block_mask):
    rows, cols = gather(pack(block_mask, similarity))
    value, sums = product(rows, cols, *similarity.shape)
    total = reduce_totals(sums)
    scaling = similarity.shape[0] * lax.axis_size("row")
    return scale(value, total, float(scaling))


def solution(mesh):
    return jax.shard_map(
        body,
        mesh=mesh,
        in_specs=(P("row", ("col", "layer")), P("row", ("col", "layer"))),
        out_specs=P("row", ("col", "layer")),
        check_vma=False,
    )
```

```python
import functools

import jax
import jax.numpy as jnp
from jax import lax
from jax.experimental import pallas as pl
from jax.experimental.pallas import tpu as pltpu
from jax.sharding import PartitionSpec as P

BLK = 128
MAXNZ = 18
HEAD = 32
HALF = MAXNZ // 2
SHARE = HEAD + MAXNZ * BLK
MIB = 1 << 20
MESH = pl.DeviceIdType.MESH


def pack_kernel(mask_ref, x_ref, share_ref, sems):
    cols, rows = mask_ref.shape
    sub = lax.broadcasted_iota(jnp.int32, (HEAD, BLK), 0)
    lane = lax.broadcasted_iota(jnp.int32, (HEAD, BLK), 1)
    lane_row = (lane * 43) >> 8
    lane_col = lane - lane_row * cols

    def one_row(i, carry):
        count, head = carry
        below = 8 + jnp.where(i < cols, i, i - cols + 8)
        for j in range(cols):
            here = mask_ref[j, i]

            @pl.when(here > 0)
            def _():
                pltpu.make_async_copy(
                    x_ref.at[pl.ds(i * BLK, BLK), pl.ds(j * BLK, BLK)],
                    share_ref.at[pl.ds(pl.multiple_of(HEAD + count * BLK, HEAD), BLK)],
                    sems.at[count],
                ).start()

            cell = ((sub == j) & (lane_row == i)) | ((sub == below) & (lane_col == j))
            head = jnp.where(cell & (here > 0), count + 1, head)
            count = count + here
        return count, head

    count, head = lax.fori_loop(
        0, rows, one_row, (jnp.int32(0), jnp.zeros((HEAD, BLK), jnp.int32))
    )
    head = jnp.where(lane < rows * cols, head, 0)
    share_ref[pl.ds(0, HEAD), :] = head.astype(jnp.float32).astype(share_ref.dtype)
    for s in range(MAXNZ):

        @pl.when(s < count)
        def _():
            pltpu.make_async_copy(
                x_ref.at[pl.ds(0, BLK), pl.ds(0, BLK)],
                share_ref.at[pl.ds(HEAD + s * BLK, BLK)],
                sems.at[s],
            ).wait()


def pack(block_mask, similarity):
    return pl.pallas_call(
        pack_kernel,
        out_shape=pltpu.VMEM((SHARE, BLK), similarity.dtype),
        in_specs=[
            pl.BlockSpec(memory_space=pltpu.SMEM),
            pl.BlockSpec(memory_space=pl.ANY),
        ],
        out_specs=pl.BlockSpec(memory_space=pltpu.VMEM),
        scratch_shapes=[pltpu.SemaphoreType.DMA((MAXNZ,))],
        compiler_params=pltpu.CompilerParams(vmem_limit_bytes=56 * MIB),
        name="pack",
    )(block_mask.T, similarity)


LAST = 5
SPLIT = 7


def span(first, last):
    low = HEAD + first * BLK if first else 0
    return pl.ds(low, HEAD + last * BLK - low)


def gather_kernel(
    share_ref, rows_ref, cols_ref, relay, send_sems, recv_sems, own_sems
):
    row, col, layer = (lax.axis_index(a) for a in ("row", "col", "layer"))
    high, x = row // 4, row % 4
    z, low = col // 2, col % 2

    def along_z(step):
        return 2 * ((z + step) % 4) + low

    def along_x(step):
        return 4 * high + (x + step) % 4

    mate = 2 * z + 1 - low
    far = 4 * (1 - high) + x

    zp, zm = (row, along_z(1), layer), (row, along_z(3), layer)
    xp, xm = (along_x(1), col, layer), (along_x(3), col, layer)
    lo, hi = (row, mate, layer), (far, mate, layer)
    sib = (row, col, 1 - layer)

    barrier = pltpu.get_barrier_semaphore()
    for peer in (zp, zm, xp, xm, lo, hi, sib):
        pl.semaphore_signal(barrier, inc=1, device_id=peer, device_id_type=MESH)
    pl.semaphore_wait(barrier, 7)

    mine = 2 * col + layer
    keep = [
        pltpu.make_async_copy(share_ref, rows_ref.at[mine], own_sems.at[0]),
        pltpu.make_async_copy(share_ref, cols_ref.at[row], own_sems.at[1]),
    ]

    EARLY = MAXNZ - LAST
    ALL = span(0, MAXNZ)
    H1, H2 = span(0, HALF), span(HALF, MAXNZ)
    U1, U2, L = span(0, SPLIT), span(SPLIT, EARLY), span(EARLY, MAXNZ)
    V1, V2, V3, V4 = span(0, 4), span(4, SPLIT), span(SPLIT, 10), span(10, EARLY)
    T = pl.ds(0, LAST * BLK)
    started = []
    waited = set()

    def send(src, dst, part, peer, into=None):
        k = len(started)
        copy = pltpu.make_async_remote_copy(
            src_ref=src.at[part],
            dst_ref=dst.at[part if into is None else into],
            send_sem=send_sems.at[k],
            recv_sem=recv_sems.at[k],
            device_id=peer,
            device_id_type=MESH,
        )
        copy.start()
        started.append(copy)
        return k

    def arrived(k, dst, part, peer):
        waited.add(k)
        pltpu.make_async_remote_copy(
            src_ref=dst.at[part],
            dst_ref=dst.at[part],
            send_sem=send_sems.at[k],
            recv_sem=recv_sems.at[k],
            device_id=peer,
            device_id_type=MESH,
        ).wait_recv()

    def other(q):
        return q + 1 - 2 * (q % 2)

    def r(q):
        return rows_ref.at[2 * q + layer]

    def rsib(q):
        return rows_ref.at[2 * q + 1 - layer]

    def c(q):
        return cols_ref.at[q]

    def across(q):
        return c((q + 4) % 8)

    own_r, own_c = r(col), c(row)
    y_r, y_c = r(mate), c(far)
    zm_r, zp_r, zz_r = (r(along_z(s)) for s in (3, 1, 2))
    ym_r, yp_r, yy_r = (r(other(along_z(s))) for s in (3, 1, 2))
    xm_c, xp_c, xx_c = (c(along_x(s)) for s in (3, 1, 2))
    ym_c, yp_c, yy_c = (across(along_x(s)) for s in (3, 1, 2))

    lo1 = send(share_ref, own_r, U1, lo)
    zp1 = send(share_ref, own_r, H1, zp)
    zm2 = send(share_ref, own_r, H2, zm)
    xp1 = send(share_ref, own_c, H1, xp)
    xm2 = send(share_ref, own_c, H2, xm)
    lo2 = send(share_ref, own_r, U2, lo)
    zp2 = send(share_ref, own_r, H2, zp)
    zm1 = send(share_ref, own_r, H1, zm)
    xp2 = send(share_ref, own_c, H2, xp)
    xm1 = send(share_ref, own_c, H1, xm)
    lo3 = send(share_ref, own_r, L, lo)
    sb0 = send(share_ref, own_r, ALL, sib)
    for copy in keep:
        copy.start()

    arrived(lo1, y_r, U1, lo)
    hi1 = send(y_r, own_c, U1, hi)
    yzp1 = send(y_r, y_r, U1, zp)
    arrived(zp1, zm_r, H1, zm)
    fzp = send(zm_r, zm_r, H1, zp)
    arrived(zm2, zp_r, H2, zp)
    fzm = send(zp_r, zp_r, H2, zm)
    arrived(xp1, xm_c, H1, xm)
    fxp = send(xm_c, xm_c, H1, xp)
    arrived(xm2, xp_c, H2, xp)
    fxm = send(xp_c, xp_c, H2, xm)
    txp = send(xp_c, relay.at[0], L, lo, T)
    lzp = send(zp_r, zp_r, L, lo)
    arrived(lo2, y_r, U2, lo)
    hi2 = send(y_r, own_c, U2, hi)
    yzm2 = send(y_r, y_r, U2, zm)
    yzp2 = send(y_r, y_r, U2, zp)
    yzm1 = send(y_r, y_r, U1, zm)
    arrived(hi1, y_c, U1, hi)
    yxp1 = send(y_c, y_c, U1, xp)
    arrived(lo3, y_r, L, lo)
    hi3 = send(y_r, own_c, L, hi)
    sb1 = send(y_r, y_r, ALL, sib)

    arrived(zp2, zm_r, H2, zm)
    arrived(xp2, xm_c, H2, xm)
    txm = send(xm_c, relay.at[1], L, lo, T)
    lzm = send(zm_r, zm_r, L, lo)
    sb2 = send(zm_r, zm_r, ALL, sib)
    arrived(zm1, zp_r, H1, zp)
    sb3 = send(zp_r, zp_r, ALL, sib)
    arrived(hi2, y_c, U2, hi)
    yxm2 = send(y_c, y_c, U2, xm)
    yxp2 = send(y_c, y_c, U2, xp)
    yxm1 = send(y_c, y_c, U1, xm)
    arrived(txp, relay.at[0], T, lo)
    uxp = send(relay.at[0], xp_c, T, hi, L)
    arrived(fxm, xx_c, H2, xp)
    txx = send(xx_c, relay.at[2], L, lo, T)
    arrived(fzm, zz_r, H2, zp)
    lzz = send(zz_r, zz_r, L, lo)
    arrived(fzp, zz_r, H1, zm)
    sb4 = send(zz_r, zz_r, ALL, sib)
    arrived(txm, relay.at[1], T, lo)
    uxm = send(relay.at[1], xm_c, T, hi, L)

    arrived(yzp1, ym_r, U1, zm)
    gzp = send(ym_r, ym_r, V1, zp)
    gzq = send(ym_r, ym_r, V2, zp)
    arrived(yzm2, yp_r, U2, zp)
    gzm = send(yp_r, yp_r, V3, zm)
    gzn = send(yp_r, yp_r, V4, zm)
    arrived(yxp1, ym_c, U1, xm)
    gxp = send(ym_c, ym_c, U1, xp)
    arrived(yxm2, yp_c, U2, xp)
    gxm = send(yp_c, yp_c, U2, xm)
    arrived(lzp, yp_r, L, lo)
    arrived(yzm1, yp_r, U1, zp)
    sb5 = send(yp_r, yp_r, ALL, sib)
    arrived(txx, relay.at[2], T, lo)
    uxx = send(relay.at[2], xx_c, T, hi, L)
    arrived(yzp2, ym_r, U2, zm)
    arrived(lzm, ym_r, L, lo)
    sb6 = send(ym_r, ym_r, ALL, sib)
    arrived(lzz, yy_r, L, lo)
    sb7 = send(yy_r, yy_r, L, sib)
    arrived(gzp, yy_r, V1, zm)
    sb8 = send(yy_r, yy_r, V1, sib)
    arrived(gzm, yy_r, V3, zp)
    sb9 = send(yy_r, yy_r, V3, sib)
    arrived(gzn, yy_r, V4, zp)
    sb10 = send(yy_r, yy_r, V4, sib)
    arrived(gzq, yy_r, V2, zm)
    sb11 = send(yy_r, yy_r, V2, sib)

    arrived(hi3, y_c, L, hi)
    arrived(xm1, xp_c, H1, xp)
    arrived(fxp, xx_c, H1, xm)
    arrived(yxp2, ym_c, U2, xm)
    arrived(yxm1, yp_c, U1, xp)
    arrived(uxp, yp_c, L, hi)
    arrived(uxm, ym_c, L, hi)
    arrived(uxx, yy_c, L, hi)
    arrived(gxp, yy_c, U1, xm)
    arrived(gxm, yy_c, U2, xp)

    arrived(sb0, rsib(col), ALL, sib)
    arrived(sb1, rsib(mate), ALL, sib)
    arrived(sb2, rsib(along_z(3)), ALL, sib)
    arrived(sb3, rsib(along_z(1)), ALL, sib)
    arrived(sb4, rsib(along_z(2)), ALL, sib)
    arrived(sb5, rsib(other(along_z(1))), ALL, sib)
    arrived(sb6, rsib(other(along_z(3))), ALL, sib)
    arrived(sb7, rsib(other(along_z(2))), L, sib)
    arrived(sb8, rsib(other(along_z(2))), V1, sib)
    arrived(sb9, rsib(other(along_z(2))), V3, sib)
    arrived(sb10, rsib(other(along_z(2))), V4, sib)
    arrived(sb11, rsib(other(along_z(2))), V2, sib)
    assert waited == set(range(len(started))) and len(started) == COPIES
    for copy in started:
        copy.wait_send()
    for copy in keep:
        copy.wait()


COPIES = 53


def gather(share):
    return pl.pallas_call(
        gather_kernel,
        out_shape=[
            pltpu.VMEM((16, SHARE, BLK), share.dtype),
            pltpu.VMEM((8, SHARE, BLK), share.dtype),
        ],
        in_specs=[pl.BlockSpec(memory_space=pltpu.VMEM)],
        out_specs=[pl.BlockSpec(memory_space=pltpu.VMEM)] * 2,
        scratch_shapes=[
            pltpu.VMEM((3, LAST * BLK, BLK), share.dtype),
            pltpu.SemaphoreType.DMA((COPIES,)),
            pltpu.SemaphoreType.DMA((COPIES,)),
            pltpu.SemaphoreType.DMA((2,)),
        ],
        compiler_params=pltpu.CompilerParams(
            collective_id=0, has_side_effects=True, vmem_limit_bytes=32 * MIB
        ),
        name="gather",
    )(share)


GROUP = 4
DEPTH = 16


def product_kernel(r_ref, c_ref, out_ref, sums_ref, table_v, table_s, sem):
    tiles, lanes = out_ref.shape[0] // BLK, out_ref.shape[1]
    wide = lanes // BLK
    col = lax.axis_index("col")

    hr, hc = [], []
    for q in range(16):
        hr.append(r_ref[q, pl.ds(0, HEAD), :].astype(jnp.float32)[0:8])
    for q in range(8):
        top = c_ref[q, pl.ds(0, HEAD), :].astype(jnp.float32)
        hc += [top[8:16], top[16:24]]
    hr, hc = jnp.concatenate(hr, 0), jnp.concatenate(hc, 0)
    both = (hr > 0) & (hc > 0)
    line = lax.broadcasted_iota(jnp.int32, (BLK, BLK), 0)
    rank = jnp.dot(
        (line > lax.broadcasted_iota(jnp.int32, (BLK, BLK), 1)).astype(jnp.bfloat16),
        both.astype(jnp.float32).astype(jnp.bfloat16),
        preferred_element_type=jnp.float32,
    )
    rank = jnp.where(both, rank, -1.0).astype(jnp.int32)
    place_r = (line >> 3) * SHARE + (HEAD - BLK) + hr.astype(jnp.int32) * BLK
    place_c = (line >> 4) * SHARE + (HEAD - BLK) + hc.astype(jnp.int32) * BLK
    count = jnp.sum(both.astype(jnp.int32), axis=0, keepdims=True)
    most = jnp.max(count)
    idle_c = col * SHARE + HEAD

    def fill(done):
        for p in range(DEPTH):
            at = rank == done + p
            some = count > done + p
            first = jnp.sum(jnp.where(at, place_r, 0), axis=0, keepdims=True)
            second = jnp.sum(jnp.where(at, place_c, 0), axis=0, keepdims=True)
            table_v[pl.ds(p, 1), :] = jnp.where(some, first, HEAD)
            table_v[pl.ds(DEPTH + p, 1), :] = jnp.where(some, second, idle_c)
        table_v[pl.ds(2 * DEPTH, 1), :] = jnp.clip(count - done, 0, DEPTH)
        copy = pltpu.make_async_copy(table_v, table_s, sem)
        copy.start()
        copy.wait()

    def part(i, j, g):
        cell = i * wide + j
        left, right = [], []
        have = table_s[2 * DEPTH, cell]
        for t in range(GROUP):
            p = g * GROUP + t
            a = r_ref[pl.ds(pl.multiple_of(table_s[p, cell], HEAD), BLK), :]
            left.append(jnp.where(p < have, a, jnp.zeros_like(a)))
            right.append(c_ref[pl.ds(pl.multiple_of(table_s[DEPTH + p, cell], HEAD), BLK), :])
        return sum(
            jnp.dot(a, b, preferred_element_type=jnp.float32) for a, b in zip(left, right)
        )

    def more(i, j, first):
        here = pl.ds(pl.multiple_of(i * BLK, BLK), BLK)

        @pl.loop(first, (table_s[2 * DEPTH, i * wide + j] + GROUP - 1) // GROUP)
        def _(g):
            out_ref[here, pl.ds(j * BLK, BLK)] += part(i, j, g)

    fill(0)
    r_ref = r_ref.reshape(16 * SHARE, BLK)
    c_ref = c_ref.reshape(8 * SHARE, BLK)

    @pl.loop(0, tiles, unroll=3)
    def _(i):
        here = pl.ds(pl.multiple_of(i * BLK, BLK), BLK)
        for j in range(wide):
            out_ref[here, pl.ds(j * BLK, BLK)] = part(i, j, 0)

    @pl.loop(0, tiles)
    def _(i):
        top = table_s[2 * DEPTH, i * wide]
        for j in range(1, wide):
            top = jnp.maximum(top, table_s[2 * DEPTH, i * wide + j])

        @pl.when(top > GROUP)
        def _():
            for j in range(wide):
                more(i, j, 1)

    @pl.loop(1, (most + DEPTH - 1) // DEPTH)
    def _(d):
        fill(d * DEPTH)

        @pl.loop(0, tiles)
        def _(i):
            for j in range(wide):
                more(i, j, 0)

    def square(t, total):
        here = pl.ds(pl.multiple_of(t * 64, 64), 64)
        value = out_ref[here, :]
        value = value * value
        out_ref[here, :] = value
        return total + jnp.sum(value.reshape(8, 8, lanes), axis=0)

    total = lax.fori_loop(
        0, tiles * BLK // 64, square, jnp.zeros((8, lanes), jnp.float32)
    )
    sums_ref[...] = jnp.sum(total, axis=0, keepdims=True)


def product(rows, cols, out_rows, lanes):
    return pl.pallas_call(
        product_kernel,
        out_shape=[
            pltpu.VMEM((out_rows, lanes), jnp.float32),
            pltpu.VMEM((1, lanes), jnp.float32),
        ],
        in_specs=[pl.BlockSpec(memory_space=pltpu.VMEM)] * 2,
        out_specs=[pl.BlockSpec(memory_space=pltpu.VMEM)] * 2,
        scratch_shapes=[
            pltpu.VMEM((2 * DEPTH + 8, BLK), jnp.int32),
            pltpu.SMEM((2 * DEPTH + 8, BLK), jnp.int32),
            pltpu.SemaphoreType.DMA(()),
        ],
        compiler_params=pltpu.CompilerParams(vmem_limit_bytes=8 * MIB),
        name="product",
    )(rows, cols)


def totals_kernel(sums_ref, out_ref, slots, send_sems, recv_sems):
    row, col, layer = (lax.axis_index(a) for a in ("row", "col", "layer"))
    high, x = row // 4, row % 4
    near = [(4 * high + (x + s) % 4, col, layer) for s in range(1, 4)]
    far = (4 * (1 - high) + x, col, layer)
    barrier = pltpu.get_barrier_semaphore()
    for peer in near + [far]:
        pl.semaphore_signal(barrier, inc=1, device_id=peer, device_id_type=MESH)
    slots[x] = sums_ref[...]
    pl.semaphore_wait(barrier, 4)

    def swap(k, src, dst, peer):
        return pltpu.make_async_remote_copy(
            src_ref=slots.at[src],
            dst_ref=slots.at[dst],
            send_sem=send_sems.at[k],
            recv_sem=recv_sems.at[k],
            device_id=peer,
            device_id_type=MESH,
        )

    copies = [swap(k, x, x, peer) for k, peer in enumerate(near)]
    for copy in copies:
        copy.start()
    for copy in copies:
        copy.wait()
    slots[4] = (slots[0] + slots[1]) + (slots[2] + slots[3])
    copy = swap(3, 4, 5, far)
    copy.start()
    copy.wait()
    out_ref[...] = slots[4] + slots[5]


def reduce_totals(sums):
    return pl.pallas_call(
        totals_kernel,
        out_shape=pltpu.VMEM(sums.shape, jnp.float32),
        in_specs=[pl.BlockSpec(memory_space=pltpu.VMEM)],
        out_specs=pl.BlockSpec(memory_space=pltpu.VMEM),
        scratch_shapes=[
            pltpu.VMEM((6,) + sums.shape, jnp.float32),
            pltpu.SemaphoreType.DMA((4,)),
            pltpu.SemaphoreType.DMA((4,)),
        ],
        compiler_params=pltpu.CompilerParams(
            collective_id=1, has_side_effects=True, vmem_limit_bytes=4 * MIB
        ),
        name="totals",
    )(sums)


STEPS = 6


def scale_kernel(scaling, value_ref, total_ref, out_ref, staged, sems):
    step = staged.shape[1]
    total = total_ref[...]
    copies = []
    for t in range(STEPS):
        here = pl.ds(t * step, step)
        staged[t] = scaling * value_ref[here, :] / total
        copy = pltpu.make_async_copy(staged.at[t], out_ref.at[here], sems.at[t])
        copy.start()
        copies.append(copy)
    for copy in copies:
        copy.wait()


def scale(value, total, scaling):
    rows, lanes = value.shape
    return pl.pallas_call(
        functools.partial(scale_kernel, scaling),
        out_shape=jax.ShapeDtypeStruct(value.shape, jnp.float32),
        in_specs=[pl.BlockSpec(memory_space=pltpu.VMEM)] * 2,
        out_specs=pl.BlockSpec(memory_space=pltpu.HBM),
        scratch_shapes=[
            pltpu.VMEM((STEPS, rows // STEPS, lanes), jnp.float32),
            pltpu.SemaphoreType.DMA((STEPS,)),
        ],
        compiler_params=pltpu.CompilerParams(vmem_limit_bytes=16 * MIB),
        name="scale",
    )(value, total)


def body(similarity, block_mask):
    rows, cols = gather(pack(block_mask, similarity))
    value, sums = product(rows, cols, *similarity.shape)
    total = reduce_totals(sums)
    scaling = similarity.shape[0] * lax.axis_size("row")
    return scale(value, total, float(scaling))


def solution(mesh):
    return jax.shard_map(
        body,
        mesh=mesh,
        in_specs=(P("row", ("col", "layer")), P("row", ("col", "layer"))),
        out_specs=P("row", ("col", "layer")),
        check_vma=False,
    )
```

```python
import functools

import jax
import jax.numpy as jnp
from jax import lax
from jax.experimental import pallas as pl
from jax.experimental.pallas import tpu as pltpu
from jax.sharding import PartitionSpec as P

BLK = 128
MAXNZ = 18
HEAD = 32
HALF = MAXNZ // 2
SHARE = HEAD + MAXNZ * BLK
MIB = 1 << 20
MESH = pl.DeviceIdType.MESH


def pack_share(mask_ref, x_ref, x_v, share, place_v, place_s, sems):
    cols, rows = mask_ref.shape
    strips = x_v.reshape(cols * rows * BLK, BLK)
    loads = [
        pltpu.make_async_copy(
            x_ref.at[:, pl.ds(j * BLK, BLK)],
            strips.at[pl.ds(j * rows * BLK, rows * BLK)],
            sems.at[j],
        )
        for j in range(cols)
    ]
    for load in loads:
        load.start()
    sub = lax.broadcasted_iota(jnp.int32, (HEAD, BLK), 0)
    lane = lax.broadcasted_iota(jnp.int32, (HEAD, BLK), 1)
    lane_row = (lane * 43) >> 8
    lane_col = lane - lane_row * cols
    lane8 = lane[:8]

    def one_row(i, carry):
        count, head, place = carry
        below = 8 + jnp.where(i < cols, i, i - cols + 8)
        for j in range(cols):
            here = mask_ref[j, i]
            cell = ((sub == j) & (lane_row == i)) | ((sub == below) & (lane_col == j))
            head = head + jnp.where(cell, here * (count + 1), 0)
            place = place + jnp.where(lane8 == count, here * (j * rows + i), 0)
            count = count + here
        return count, head, place

    _, head, place = lax.fori_loop(
        0,
        rows,
        one_row,
        (jnp.int32(0), jnp.zeros((HEAD, BLK), jnp.int32), jnp.zeros((8, BLK), jnp.int32)),
    )
    place_v[...] = place
    move = pltpu.make_async_copy(place_v, place_s, sems.at[cols])
    move.start()
    head = jnp.where(lane < rows * cols, head, 0)
    share[pl.ds(0, HEAD), :] = head.astype(jnp.float32).astype(share.dtype)
    move.wait()
    for load in loads:
        load.wait()
    for s in range(MAXNZ):
        share[pl.ds(HEAD + s * BLK, BLK), :] = x_v[place_s[0, s]]


LAST = 5
SPLIT = 7


def span(first, last):
    low = HEAD + first * BLK if first else 0
    return pl.ds(low, HEAD + last * BLK - low)


def gather_kernel(
    mask_ref,
    x_ref,
    rows_ref,
    cols_ref,
    x_v,
    share_ref,
    relay,
    place_v,
    place_s,
    send_sems,
    recv_sems,
    own_sems,
    pack_sems,
):
    row, col, layer = (lax.axis_index(a) for a in ("row", "col", "layer"))
    high, x = row // 4, row % 4
    z, low = col // 2, col % 2

    def along_z(step):
        return 2 * ((z + step) % 4) + low

    def along_x(step):
        return 4 * high + (x + step) % 4

    mate = 2 * z + 1 - low
    far = 4 * (1 - high) + x

    zp, zm = (row, along_z(1), layer), (row, along_z(3), layer)
    xp, xm = (along_x(1), col, layer), (along_x(3), col, layer)
    lo, hi = (row, mate, layer), (far, mate, layer)
    sib = (row, col, 1 - layer)

    barrier = pltpu.get_barrier_semaphore()
    for peer in (zp, zm, xp, xm, lo, hi, sib):
        pl.semaphore_signal(barrier, inc=1, device_id=peer, device_id_type=MESH)
    pack_share(mask_ref, x_ref, x_v, share_ref, place_v, place_s, pack_sems)
    pl.semaphore_wait(barrier, 7)

    mine = 2 * col + layer
    keep = [
        pltpu.make_async_copy(share_ref, rows_ref.at[mine], own_sems.at[0]),
        pltpu.make_async_copy(share_ref, cols_ref.at[row], own_sems.at[1]),
    ]

    EARLY = MAXNZ - LAST
    ALL = span(0, MAXNZ)
    H1, H2 = span(0, HALF), span(HALF, MAXNZ)
    U1, U2, L = span(0, SPLIT), span(SPLIT, EARLY), span(EARLY, MAXNZ)
    V1, V2, V3, V4 = span(0, 4), span(4, SPLIT), span(SPLIT, 10), span(10, EARLY)
    T = pl.ds(0, LAST * BLK)
    started = []
    waited = set()

    def send(src, dst, part, peer, into=None):
        k = len(started)
        copy = pltpu.make_async_remote_copy(
            src_ref=src.at[part],
            dst_ref=dst.at[part if into is None else into],
            send_sem=send_sems.at[k],
            recv_sem=recv_sems.at[k],
            device_id=peer,
            device_id_type=MESH,
        )
        copy.start()
        started.append(copy)
        return k

    def arrived(k, dst, part, peer):
        waited.add(k)
        pltpu.make_async_remote_copy(
            src_ref=dst.at[part],
            dst_ref=dst.at[part],
            send_sem=send_sems.at[k],
            recv_sem=recv_sems.at[k],
            device_id=peer,
            device_id_type=MESH,
        ).wait_recv()

    def other(q):
        return q + 1 - 2 * (q % 2)

    def r(q):
        return rows_ref.at[2 * q + layer]

    def rsib(q):
        return rows_ref.at[2 * q + 1 - layer]

    def c(q):
        return cols_ref.at[q]

    def across(q):
        return c((q + 4) % 8)

    own_r, own_c = r(col), c(row)
    y_r, y_c = r(mate), c(far)
    zm_r, zp_r, zz_r = (r(along_z(s)) for s in (3, 1, 2))
    ym_r, yp_r, yy_r = (r(other(along_z(s))) for s in (3, 1, 2))
    xm_c, xp_c, xx_c = (c(along_x(s)) for s in (3, 1, 2))
    ym_c, yp_c, yy_c = (across(along_x(s)) for s in (3, 1, 2))

    lo1 = send(share_ref, own_r, U1, lo)
    zp1 = send(share_ref, own_r, H1, zp)
    zm2 = send(share_ref, own_r, H2, zm)
    xp1 = send(share_ref, own_c, H1, xp)
    xm2 = send(share_ref, own_c, H2, xm)
    lo2 = send(share_ref, own_r, U2, lo)
    zp2 = send(share_ref, own_r, H2, zp)
    zm1 = send(share_ref, own_r, H1, zm)
    xp2 = send(share_ref, own_c, H2, xp)
    xm1 = send(share_ref, own_c, H1, xm)
    lo3 = send(share_ref, own_r, L, lo)
    sb0 = send(share_ref, own_r, ALL, sib)
    for copy in keep:
        copy.start()

    arrived(lo1, y_r, U1, lo)
    hi1 = send(y_r, own_c, U1, hi)
    yzp1 = send(y_r, y_r, U1, zp)
    arrived(zp1, zm_r, H1, zm)
    fzp = send(zm_r, zm_r, H1, zp)
    arrived(zm2, zp_r, H2, zp)
    fzm = send(zp_r, zp_r, H2, zm)
    arrived(xp1, xm_c, H1, xm)
    fxp = send(xm_c, xm_c, H1, xp)
    arrived(xm2, xp_c, H2, xp)
    fxm = send(xp_c, xp_c, H2, xm)
    txp = send(xp_c, relay.at[0], L, lo, T)
    lzp = send(zp_r, zp_r, L, lo)
    arrived(lo2, y_r, U2, lo)
    hi2 = send(y_r, own_c, U2, hi)
    yzm2 = send(y_r, y_r, U2, zm)
    yzp2 = send(y_r, y_r, U2, zp)
    yzm1 = send(y_r, y_r, U1, zm)
    arrived(hi1, y_c, U1, hi)
    yxp1 = send(y_c, y_c, U1, xp)
    arrived(lo3, y_r, L, lo)
    hi3 = send(y_r, own_c, L, hi)
    sb1 = send(y_r, y_r, ALL, sib)

    arrived(zp2, zm_r, H2, zm)
    arrived(xp2, xm_c, H2, xm)
    txm = send(xm_c, relay.at[1], L, lo, T)
    lzm = send(zm_r, zm_r, L, lo)
    sb2 = send(zm_r, zm_r, ALL, sib)
    arrived(zm1, zp_r, H1, zp)
    sb3 = send(zp_r, zp_r, ALL, sib)
    arrived(hi2, y_c, U2, hi)
    yxm2 = send(y_c, y_c, U2, xm)
    yxp2 = send(y_c, y_c, U2, xp)
    yxm1 = send(y_c, y_c, U1, xm)
    arrived(txp, relay.at[0], T, lo)
    uxp = send(relay.at[0], xp_c, T, hi, L)
    arrived(fxm, xx_c, H2, xp)
    txx = send(xx_c, relay.at[2], L, lo, T)
    arrived(fzm, zz_r, H2, zp)
    lzz = send(zz_r, zz_r, L, lo)
    arrived(fzp, zz_r, H1, zm)
    sb4 = send(zz_r, zz_r, ALL, sib)
    arrived(txm, relay.at[1], T, lo)
    uxm = send(relay.at[1], xm_c, T, hi, L)

    arrived(yzp1, ym_r, U1, zm)
    gzp = send(ym_r, ym_r, V1, zp)
    gzq = send(ym_r, ym_r, V2, zp)
    arrived(yzm2, yp_r, U2, zp)
    gzm = send(yp_r, yp_r, V3, zm)
    gzn = send(yp_r, yp_r, V4, zm)
    arrived(yxp1, ym_c, U1, xm)
    gxp = send(ym_c, ym_c, U1, xp)
    arrived(yxm2, yp_c, U2, xp)
    gxm = send(yp_c, yp_c, U2, xm)
    arrived(lzp, yp_r, L, lo)
    arrived(yzm1, yp_r, U1, zp)
    sb5 = send(yp_r, yp_r, ALL, sib)
    arrived(txx, relay.at[2], T, lo)
    uxx = send(relay.at[2], xx_c, T, hi, L)
    arrived(yzp2, ym_r, U2, zm)
    arrived(lzm, ym_r, L, lo)
    sb6 = send(ym_r, ym_r, ALL, sib)
    arrived(lzz, yy_r, L, lo)
    sb7 = send(yy_r, yy_r, L, sib)
    arrived(gzp, yy_r, V1, zm)
    sb8 = send(yy_r, yy_r, V1, sib)
    arrived(gzm, yy_r, V3, zp)
    sb9 = send(yy_r, yy_r, V3, sib)
    arrived(gzn, yy_r, V4, zp)
    sb10 = send(yy_r, yy_r, V4, sib)
    arrived(gzq, yy_r, V2, zm)
    sb11 = send(yy_r, yy_r, V2, sib)

    arrived(hi3, y_c, L, hi)
    arrived(xm1, xp_c, H1, xp)
    arrived(fxp, xx_c, H1, xm)
    arrived(yxp2, ym_c, U2, xm)
    arrived(yxm1, yp_c, U1, xp)
    arrived(uxp, yp_c, L, hi)
    arrived(uxm, ym_c, L, hi)
    arrived(uxx, yy_c, L, hi)
    arrived(gxp, yy_c, U1, xm)
    arrived(gxm, yy_c, U2, xp)

    arrived(sb0, rsib(col), ALL, sib)
    arrived(sb1, rsib(mate), ALL, sib)
    arrived(sb2, rsib(along_z(3)), ALL, sib)
    arrived(sb3, rsib(along_z(1)), ALL, sib)
    arrived(sb4, rsib(along_z(2)), ALL, sib)
    arrived(sb5, rsib(other(along_z(1))), ALL, sib)
    arrived(sb6, rsib(other(along_z(3))), ALL, sib)
    arrived(sb7, rsib(other(along_z(2))), L, sib)
    arrived(sb8, rsib(other(along_z(2))), V1, sib)
    arrived(sb9, rsib(other(along_z(2))), V3, sib)
    arrived(sb10, rsib(other(along_z(2))), V4, sib)
    arrived(sb11, rsib(other(along_z(2))), V2, sib)
    assert waited == set(range(len(started))) and len(started) == COPIES
    for copy in started:
        copy.wait_send()
    for copy in keep:
        copy.wait()


COPIES = 53


def gather(block_mask, similarity):
    dtype = similarity.dtype
    cells = block_mask.size
    return pl.pallas_call(
        gather_kernel,
        out_shape=[
            pltpu.VMEM((16, SHARE, BLK), dtype),
            pltpu.VMEM((8, SHARE, BLK), dtype),
        ],
        in_specs=[
            pl.BlockSpec(memory_space=pltpu.SMEM),
            pl.BlockSpec(memory_space=pl.ANY),
        ],
        out_specs=[pl.BlockSpec(memory_space=pltpu.VMEM)] * 2,
        scratch_shapes=[
            pltpu.VMEM((cells, BLK, BLK), dtype),
            pltpu.VMEM((SHARE, BLK), dtype),
            pltpu.VMEM((3, LAST * BLK, BLK), dtype),
            pltpu.VMEM((8, BLK), jnp.int32),
            pltpu.SMEM((8, BLK), jnp.int32),
            pltpu.SemaphoreType.DMA((COPIES,)),
            pltpu.SemaphoreType.DMA((COPIES,)),
            pltpu.SemaphoreType.DMA((2,)),
            pltpu.SemaphoreType.DMA((7,)),
        ],
        compiler_params=pltpu.CompilerParams(
            collective_id=0, has_side_effects=True, vmem_limit_bytes=44 * MIB
        ),
        name="gather",
    )(block_mask.T, similarity)


GROUP = 4
DEPTH = 16


def product_kernel(r_ref, c_ref, out_ref, sums_ref, table_v, table_s, sem):
    tiles, lanes = out_ref.shape[0] // BLK, out_ref.shape[1]
    wide = lanes // BLK
    col = lax.axis_index("col")

    hr, hc = [], []
    for q in range(16):
        hr.append(r_ref[q, pl.ds(0, HEAD), :].astype(jnp.float32)[0:8])
    for q in range(8):
        top = c_ref[q, pl.ds(0, HEAD), :].astype(jnp.float32)
        hc += [top[8:16], top[16:24]]
    hr, hc = jnp.concatenate(hr, 0), jnp.concatenate(hc, 0)
    both = (hr > 0) & (hc > 0)
    line = lax.broadcasted_iota(jnp.int32, (BLK, BLK), 0)
    rank = jnp.dot(
        (line > lax.broadcasted_iota(jnp.int32, (BLK, BLK), 1)).astype(jnp.bfloat16),
        both.astype(jnp.float32).astype(jnp.bfloat16),
        preferred_element_type=jnp.float32,
    )
    rank = jnp.where(both, rank, -1.0).astype(jnp.int32)
    place_r = (line >> 3) * SHARE + (HEAD - BLK) + hr.astype(jnp.int32) * BLK
    place_c = (line >> 4) * SHARE + (HEAD - BLK) + hc.astype(jnp.int32) * BLK
    count = jnp.sum(both.astype(jnp.int32), axis=0, keepdims=True)
    most = jnp.max(count)
    idle_c = col * SHARE + HEAD

    def fill(done):
        for p in range(DEPTH):
            at = rank == done + p
            some = count > done + p
            first = jnp.sum(jnp.where(at, place_r, 0), axis=0, keepdims=True)
            second = jnp.sum(jnp.where(at, place_c, 0), axis=0, keepdims=True)
            table_v[pl.ds(p, 1), :] = jnp.where(some, first, HEAD)
            table_v[pl.ds(DEPTH + p, 1), :] = jnp.where(some, second, idle_c)
        table_v[pl.ds(2 * DEPTH, 1), :] = jnp.clip(count - done, 0, DEPTH)
        copy = pltpu.make_async_copy(table_v, table_s, sem)
        copy.start()
        copy.wait()

    def part(i, j, g):
        cell = i * wide + j
        left, right = [], []
        have = table_s[2 * DEPTH, cell]
        for t in range(GROUP):
            p = g * GROUP + t
            a = r_ref[pl.ds(pl.multiple_of(table_s[p, cell], HEAD), BLK), :]
            left.append(jnp.where(p < have, a, jnp.zeros_like(a)))
            right.append(c_ref[pl.ds(pl.multiple_of(table_s[DEPTH + p, cell], HEAD), BLK), :])
        return sum(
            jnp.dot(a, b, preferred_element_type=jnp.float32) for a, b in zip(left, right)
        )

    def more(i, j, first):
        here = pl.ds(pl.multiple_of(i * BLK, BLK), BLK)

        @pl.loop(first, (table_s[2 * DEPTH, i * wide + j] + GROUP - 1) // GROUP)
        def _(g):
            out_ref[here, pl.ds(j * BLK, BLK)] += part(i, j, g)

    fill(0)
    r_ref = r_ref.reshape(16 * SHARE, BLK)
    c_ref = c_ref.reshape(8 * SHARE, BLK)

    @pl.loop(0, tiles, unroll=3)
    def _(i):
        here = pl.ds(pl.multiple_of(i * BLK, BLK), BLK)
        for j in range(wide):
            out_ref[here, pl.ds(j * BLK, BLK)] = part(i, j, 0)

    @pl.loop(0, tiles)
    def _(i):
        top = table_s[2 * DEPTH, i * wide]
        for j in range(1, wide):
            top = jnp.maximum(top, table_s[2 * DEPTH, i * wide + j])

        @pl.when(top > GROUP)
        def _():
            for j in range(wide):
                more(i, j, 1)

    @pl.loop(1, (most + DEPTH - 1) // DEPTH)
    def _(d):
        fill(d * DEPTH)

        @pl.loop(0, tiles)
        def _(i):
            for j in range(wide):
                more(i, j, 0)

    def square(t, total):
        here = pl.ds(pl.multiple_of(t * 64, 64), 64)
        value = out_ref[here, :]
        value = value * value
        out_ref[here, :] = value
        return total + jnp.sum(value.reshape(8, 8, lanes), axis=0)

    total = lax.fori_loop(
        0, tiles * BLK // 64, square, jnp.zeros((8, lanes), jnp.float32)
    )
    sums_ref[...] = jnp.sum(total, axis=0, keepdims=True)


def product(rows, cols, out_rows, lanes):
    return pl.pallas_call(
        product_kernel,
        out_shape=[
            pltpu.VMEM((out_rows, lanes), jnp.float32),
            pltpu.VMEM((1, lanes), jnp.float32),
        ],
        in_specs=[pl.BlockSpec(memory_space=pltpu.VMEM)] * 2,
        out_specs=[pl.BlockSpec(memory_space=pltpu.VMEM)] * 2,
        scratch_shapes=[
            pltpu.VMEM((2 * DEPTH + 8, BLK), jnp.int32),
            pltpu.SMEM((2 * DEPTH + 8, BLK), jnp.int32),
            pltpu.SemaphoreType.DMA(()),
        ],
        compiler_params=pltpu.CompilerParams(vmem_limit_bytes=8 * MIB),
        name="product",
    )(rows, cols)


def totals_kernel(sums_ref, out_ref, slots, send_sems, recv_sems):
    row, col, layer = (lax.axis_index(a) for a in ("row", "col", "layer"))
    high, x = row // 4, row % 4
    near = [(4 * high + (x + s) % 4, col, layer) for s in range(1, 4)]
    far = (4 * (1 - high) + x, col, layer)
    barrier = pltpu.get_barrier_semaphore()
    for peer in near + [far]:
        pl.semaphore_signal(barrier, inc=1, device_id=peer, device_id_type=MESH)
    slots[x] = sums_ref[...]
    pl.semaphore_wait(barrier, 4)

    def swap(k, src, dst, peer):
        return pltpu.make_async_remote_copy(
            src_ref=slots.at[src],
            dst_ref=slots.at[dst],
            send_sem=send_sems.at[k],
            recv_sem=recv_sems.at[k],
            device_id=peer,
            device_id_type=MESH,
        )

    copies = [swap(k, x, x, peer) for k, peer in enumerate(near)]
    for copy in copies:
        copy.start()
    for copy in copies:
        copy.wait()
    slots[4] = (slots[0] + slots[1]) + (slots[2] + slots[3])
    copy = swap(3, 4, 5, far)
    copy.start()
    copy.wait()
    out_ref[...] = slots[4] + slots[5]


def reduce_totals(sums):
    return pl.pallas_call(
        totals_kernel,
        out_shape=pltpu.VMEM(sums.shape, jnp.float32),
        in_specs=[pl.BlockSpec(memory_space=pltpu.VMEM)],
        out_specs=pl.BlockSpec(memory_space=pltpu.VMEM),
        scratch_shapes=[
            pltpu.VMEM((6,) + sums.shape, jnp.float32),
            pltpu.SemaphoreType.DMA((4,)),
            pltpu.SemaphoreType.DMA((4,)),
        ],
        compiler_params=pltpu.CompilerParams(
            collective_id=1, has_side_effects=True, vmem_limit_bytes=4 * MIB
        ),
        name="totals",
    )(sums)


STEPS = 6


def scale_kernel(scaling, value_ref, total_ref, out_ref, staged, sems):
    step = staged.shape[1]
    total = total_ref[...]
    copies = []
    for t in range(STEPS):
        here = pl.ds(t * step, step)
        staged[t] = scaling * value_ref[here, :] / total
        copy = pltpu.make_async_copy(staged.at[t], out_ref.at[here], sems.at[t])
        copy.start()
        copies.append(copy)
    for copy in copies:
        copy.wait()


def scale(value, total, scaling):
    rows, lanes = value.shape
    return pl.pallas_call(
        functools.partial(scale_kernel, scaling),
        out_shape=jax.ShapeDtypeStruct(value.shape, jnp.float32),
        in_specs=[pl.BlockSpec(memory_space=pltpu.VMEM)] * 2,
        out_specs=pl.BlockSpec(memory_space=pltpu.HBM),
        scratch_shapes=[
            pltpu.VMEM((STEPS, rows // STEPS, lanes), jnp.float32),
            pltpu.SemaphoreType.DMA((STEPS,)),
        ],
        compiler_params=pltpu.CompilerParams(vmem_limit_bytes=16 * MIB),
        name="scale",
    )(value, total)


def body(similarity, block_mask):
    rows, cols = gather(block_mask, similarity)
    value, sums = product(rows, cols, *similarity.shape)
    total = reduce_totals(sums)
    scaling = similarity.shape[0] * lax.axis_size("row")
    return scale(value, total, float(scaling))


def solution(mesh):
    return jax.shard_map(
        body,
        mesh=mesh,
        in_specs=(P("row", ("col", "layer")), P("row", ("col", "layer"))),
        out_specs=P("row", ("col", "layer")),
        check_vma=False,
    )
```

```python
import functools

import jax
import jax.numpy as jnp
from jax import lax
from jax.experimental import pallas as pl
from jax.experimental.pallas import tpu as pltpu
from jax.sharding import PartitionSpec as P

BLK = 128
MAXNZ = 18
HEAD = 32
HALF = MAXNZ // 2
SLOTS = MAXNZ + 1
SHARE = SLOTS * BLK
TOP = BLK - HEAD
GROUP = 4
DEPTH = 16
MIB = 1 << 20
MESH = pl.DeviceIdType.MESH


def pack_share(mask_ref, x_ref, x_v, share, place_v, place_s, sems):
    cols, rows = mask_ref.shape
    strips = x_v.reshape(cols * rows * BLK, BLK)
    loads = [
        pltpu.make_async_copy(
            x_ref.at[:, pl.ds(j * BLK, BLK)],
            strips.at[pl.ds(j * rows * BLK, rows * BLK)],
            sems.at[j],
        )
        for j in range(cols)
    ]
    for load in loads:
        load.start()
    sub = lax.broadcasted_iota(jnp.int32, (HEAD, BLK), 0)
    lane = lax.broadcasted_iota(jnp.int32, (HEAD, BLK), 1)
    lane_row = (lane * 43) >> 8
    lane_col = lane - lane_row * cols
    lane8 = lane[:8]

    def find(i, carry):
        count, place = carry
        for j in range(cols):
            here = mask_ref[j, i]
            place = place + jnp.where(lane8 == count, here * (j * rows + i), 0)
            count = count + here
        return count, place

    zero = jnp.int32(0)
    _, place = lax.fori_loop(0, rows, find, (zero, jnp.zeros((8, BLK), jnp.int32)), unroll=3)
    place_v[...] = place
    move = pltpu.make_async_copy(place_v, place_s, sems.at[cols])
    move.start()

    def mark(i, carry):
        count, head = carry
        below = 8 + jnp.where(i < cols, i, i - cols + 8)
        for j in range(cols):
            here = mask_ref[j, i]
            cell = ((sub == j) & (lane_row == i)) | ((sub == below) & (lane_col == j))
            head = head + jnp.where(cell, here * (count + 1), 0)
            count = count + here
        return count, head

    _, head = lax.fori_loop(0, rows, mark, (zero, jnp.zeros((HEAD, BLK), jnp.int32)))
    head = jnp.where(lane < rows * cols, head, 0)
    share[pl.ds(TOP, HEAD), :] = head.astype(jnp.float32).astype(share.dtype)
    move.wait()
    for load in loads:
        load.wait()
    for s in range(MAXNZ):
        share[pl.ds((s + 1) * BLK, BLK), :] = x_v[place_s[0, s]]


def pair_lists(rows_ref, cols_ref):
    hr, hc = [], []
    for q in range(16):
        hr.append(rows_ref[q, pl.ds(TOP, HEAD), :].astype(jnp.float32)[0:8])
    for q in range(8):
        top = cols_ref[q, pl.ds(TOP, HEAD), :].astype(jnp.float32)
        hc += [top[8:16], top[16:24]]
    hr, hc = jnp.concatenate(hr, 0), jnp.concatenate(hc, 0)
    both = jnp.where((hr > 0) & (hc > 0), 1.0, 0.0)
    line = lax.broadcasted_iota(jnp.int32, (BLK, BLK), 0)
    before = line > lax.broadcasted_iota(jnp.int32, (BLK, BLK), 1)
    rank = jnp.dot(
        jnp.where(before, 1.0, 0.0).astype(jnp.bfloat16),
        both.astype(jnp.bfloat16),
        preferred_element_type=jnp.float32,
    )
    rank = jnp.where(both > 0, rank, -1.0).astype(jnp.int32)
    place_r = (line >> 3) * SLOTS + hr.astype(jnp.int32)
    place_c = (line >> 4) * SLOTS + hc.astype(jnp.int32)
    count = jnp.sum(both, axis=0, keepdims=True).astype(jnp.int32)
    return rank, place_r, place_c, count


def write_lists(table_v, lists, done):
    rank, place_r, place_c, count = lists
    for p in range(DEPTH):
        at = rank == done + p
        some = count > done + p
        first = jnp.sum(jnp.where(at, place_r, 0), axis=0, keepdims=True)
        second = jnp.sum(jnp.where(at, place_c, 0), axis=0, keepdims=True)
        table_v[pl.ds(p, 1), :] = jnp.where(some, first, 16 * SLOTS)
        table_v[pl.ds(DEPTH + p, 1), :] = jnp.where(some, second, 1)
    most = jnp.max(count, axis=1, keepdims=True)
    table_v[pl.ds(2 * DEPTH, 1), :] = count - done
    table_v[pl.ds(2 * DEPTH + 1, 1), :] = jnp.broadcast_to(most, count.shape)


LAST = 5
SPLIT = 7


def span(first, last):
    low = (first + 1) * BLK if first else TOP
    return pl.ds(low, (last + 1) * BLK - low)


def gather_kernel(
    mask_ref,
    x_ref,
    rows_ref,
    cols_ref,
    table_ref,
    x_v,
    share_ref,
    relay,
    place_v,
    place_s,
    send_sems,
    recv_sems,
    own_sems,
    pack_sems,
    table_v,
):
    row, col, layer = (lax.axis_index(a) for a in ("row", "col", "layer"))
    high, x = row // 4, row % 4
    z, low = col // 2, col % 2

    def along_z(step):
        return 2 * ((z + step) % 4) + low

    def along_x(step):
        return 4 * high + (x + step) % 4

    mate = 2 * z + 1 - low
    far = 4 * (1 - high) + x

    zp, zm = (row, along_z(1), layer), (row, along_z(3), layer)
    xp, xm = (along_x(1), col, layer), (along_x(3), col, layer)
    lo, hi = (row, mate, layer), (far, mate, layer)
    sib = (row, col, 1 - layer)

    barrier = pltpu.get_barrier_semaphore()
    for peer in (zp, zm, xp, xm, lo, hi, sib):
        pl.semaphore_signal(barrier, inc=1, device_id=peer, device_id_type=MESH)
    pack_share(mask_ref, x_ref, x_v, share_ref, place_v, place_s, pack_sems)
    pl.semaphore_wait(barrier, 7)

    ALL = span(0, MAXNZ)
    mine = 2 * col + layer
    keep = [
        pltpu.make_async_copy(share_ref.at[ALL], rows_ref.at[mine].at[ALL], own_sems.at[0]),
        pltpu.make_async_copy(share_ref.at[ALL], cols_ref.at[row].at[ALL], own_sems.at[1]),
    ]

    EARLY = MAXNZ - LAST
    H1, H2 = span(0, HALF), span(HALF, MAXNZ)
    U1, U2, L = span(0, SPLIT), span(SPLIT, EARLY), span(EARLY, MAXNZ)
    V1, V2, V3, V4 = span(0, 4), span(4, SPLIT), span(SPLIT, 10), span(10, EARLY)
    T = pl.ds(0, LAST * BLK)
    started = []
    waited = set()

    def send(src, dst, part, peer, into=None):
        k = len(started)
        copy = pltpu.make_async_remote_copy(
            src_ref=src.at[part],
            dst_ref=dst.at[part if into is None else into],
            send_sem=send_sems.at[k],
            recv_sem=recv_sems.at[k],
            device_id=peer,
            device_id_type=MESH,
        )
        copy.start()
        started.append(copy)
        return k

    def arrived(k, dst, part, peer):
        waited.add(k)
        pltpu.make_async_remote_copy(
            src_ref=dst.at[part],
            dst_ref=dst.at[part],
            send_sem=send_sems.at[k],
            recv_sem=recv_sems.at[k],
            device_id=peer,
            device_id_type=MESH,
        ).wait_recv()

    def other(q):
        return q + 1 - 2 * (q % 2)

    def r(q):
        return rows_ref.at[2 * q + layer]

    def rsib(q):
        return rows_ref.at[2 * q + 1 - layer]

    def c(q):
        return cols_ref.at[q]

    def across(q):
        return c((q + 4) % 8)

    own_r, own_c = r(col), c(row)
    y_r, y_c = r(mate), c(far)
    zm_r, zp_r, zz_r = (r(along_z(s)) for s in (3, 1, 2))
    ym_r, yp_r, yy_r = (r(other(along_z(s))) for s in (3, 1, 2))
    xm_c, xp_c, xx_c = (c(along_x(s)) for s in (3, 1, 2))
    ym_c, yp_c, yy_c = (across(along_x(s)) for s in (3, 1, 2))

    lo1 = send(share_ref, own_r, U1, lo)
    zp1 = send(share_ref, own_r, H1, zp)
    zm2 = send(share_ref, own_r, H2, zm)
    xp1 = send(share_ref, own_c, H1, xp)
    xm2 = send(share_ref, own_c, H2, xm)
    lo2 = send(share_ref, own_r, U2, lo)
    zp2 = send(share_ref, own_r, H2, zp)
    zm1 = send(share_ref, own_r, H1, zm)
    xp2 = send(share_ref, own_c, H2, xp)
    xm1 = send(share_ref, own_c, H1, xm)
    lo3 = send(share_ref, own_r, L, lo)
    sb0 = send(share_ref, own_r, ALL, sib)
    for copy in keep:
        copy.start()
    rows_ref[16, pl.ds(0, BLK), :] = jnp.zeros((BLK, BLK), rows_ref.dtype)

    arrived(lo1, y_r, U1, lo)
    hi1 = send(y_r, own_c, U1, hi)
    yzp1 = send(y_r, y_r, U1, zp)
    arrived(zp1, zm_r, H1, zm)
    fzp = send(zm_r, zm_r, H1, zp)
    arrived(zm2, zp_r, H2, zp)
    fzm = send(zp_r, zp_r, H2, zm)
    arrived(xp1, xm_c, H1, xm)
    fxp = send(xm_c, xm_c, H1, xp)
    arrived(xm2, xp_c, H2, xp)
    fxm = send(xp_c, xp_c, H2, xm)
    txp = send(xp_c, relay.at[0], L, lo, T)
    lzp = send(zp_r, zp_r, L, lo)
    arrived(lo2, y_r, U2, lo)
    hi2 = send(y_r, own_c, U2, hi)
    yzm2 = send(y_r, y_r, U2, zm)
    yzp2 = send(y_r, y_r, U2, zp)
    yzm1 = send(y_r, y_r, U1, zm)
    arrived(hi1, y_c, U1, hi)
    yxp1 = send(y_c, y_c, U1, xp)
    arrived(lo3, y_r, L, lo)
    hi3 = send(y_r, own_c, L, hi)
    sb1 = send(y_r, y_r, ALL, sib)

    arrived(zp2, zm_r, H2, zm)
    arrived(xp2, xm_c, H2, xm)
    txm = send(xm_c, relay.at[1], L, lo, T)
    lzm = send(zm_r, zm_r, L, lo)
    sb2 = send(zm_r, zm_r, ALL, sib)
    arrived(zm1, zp_r, H1, zp)
    sb3 = send(zp_r, zp_r, ALL, sib)
    arrived(hi2, y_c, U2, hi)
    yxm2 = send(y_c, y_c, U2, xm)
    yxp2 = send(y_c, y_c, U2, xp)
    yxm1 = send(y_c, y_c, U1, xm)
    arrived(txp, relay.at[0], T, lo)
    uxp = send(relay.at[0], xp_c, T, hi, L)
    arrived(fxm, xx_c, H2, xp)
    txx = send(xx_c, relay.at[2], L, lo, T)
    arrived(fzm, zz_r, H2, zp)
    lzz = send(zz_r, zz_r, L, lo)
    arrived(fzp, zz_r, H1, zm)
    sb4 = send(zz_r, zz_r, ALL, sib)
    arrived(txm, relay.at[1], T, lo)
    uxm = send(relay.at[1], xm_c, T, hi, L)

    arrived(yzp1, ym_r, U1, zm)
    gzp = send(ym_r, ym_r, V1, zp)
    gzq = send(ym_r, ym_r, V2, zp)
    arrived(yzm2, yp_r, U2, zp)
    gzm = send(yp_r, yp_r, V3, zm)
    gzn = send(yp_r, yp_r, V4, zm)
    arrived(yxp1, ym_c, U1, xm)
    gxp = send(ym_c, ym_c, U1, xp)
    arrived(yxm2, yp_c, U2, xp)
    gxm = send(yp_c, yp_c, U2, xm)
    arrived(lzp, yp_r, L, lo)
    arrived(yzm1, yp_r, U1, zp)
    sb5 = send(yp_r, yp_r, ALL, sib)
    arrived(txx, relay.at[2], T, lo)
    uxx = send(relay.at[2], xx_c, T, hi, L)
    arrived(yzp2, ym_r, U2, zm)
    arrived(lzm, ym_r, L, lo)
    sb6 = send(ym_r, ym_r, ALL, sib)
    arrived(lzz, yy_r, L, lo)
    sb7 = send(yy_r, yy_r, L, sib)
    arrived(gzp, yy_r, V1, zm)
    sb8 = send(yy_r, yy_r, V1, sib)
    arrived(gzm, yy_r, V3, zp)
    sb9 = send(yy_r, yy_r, V3, sib)
    arrived(gzn, yy_r, V4, zp)
    sb10 = send(yy_r, yy_r, V4, sib)
    arrived(gzq, yy_r, V2, zm)
    sb11 = send(yy_r, yy_r, V2, sib)

    for copy in keep:
        copy.wait()
    arrived(xm1, xp_c, H1, xp)
    arrived(fxp, xx_c, H1, xm)
    arrived(yxm1, yp_c, U1, xp)
    arrived(gxp, yy_c, U1, xm)
    arrived(sb0, rsib(col), ALL, sib)
    arrived(sb1, rsib(mate), ALL, sib)
    arrived(sb2, rsib(along_z(3)), ALL, sib)
    arrived(sb3, rsib(along_z(1)), ALL, sib)
    arrived(sb4, rsib(along_z(2)), ALL, sib)
    arrived(sb5, rsib(other(along_z(1))), ALL, sib)
    arrived(sb6, rsib(other(along_z(3))), ALL, sib)
    arrived(sb8, rsib(other(along_z(2))), V1, sib)
    write_lists(table_v, pair_lists(rows_ref, cols_ref), 0)
    hand = pltpu.make_async_copy(table_v, table_ref, own_sems.at[2])
    hand.start()

    arrived(hi3, y_c, L, hi)
    arrived(yxp2, ym_c, U2, xm)
    arrived(uxp, yp_c, L, hi)
    arrived(uxm, ym_c, L, hi)
    arrived(uxx, yy_c, L, hi)
    arrived(gxm, yy_c, U2, xp)
    arrived(sb7, rsib(other(along_z(2))), L, sib)
    arrived(sb9, rsib(other(along_z(2))), V3, sib)
    arrived(sb10, rsib(other(along_z(2))), V4, sib)
    arrived(sb11, rsib(other(along_z(2))), V2, sib)
    assert waited == set(range(len(started))) and len(started) == COPIES
    for copy in started:
        copy.wait_send()
    hand.wait()


COPIES = 53


def gather(block_mask, similarity):
    dtype = similarity.dtype
    cells = block_mask.size
    return pl.pallas_call(
        gather_kernel,
        out_shape=[
            pltpu.VMEM((17, SHARE, BLK), dtype),
            pltpu.VMEM((8, SHARE, BLK), dtype),
            pltpu.SMEM((2 * DEPTH + 8, BLK), jnp.int32),
        ],
        in_specs=[
            pl.BlockSpec(memory_space=pltpu.SMEM),
            pl.BlockSpec(memory_space=pl.ANY),
        ],
        out_specs=[
            pl.BlockSpec(memory_space=pltpu.VMEM),
            pl.BlockSpec(memory_space=pltpu.VMEM),
            pl.BlockSpec(memory_space=pltpu.SMEM),
        ],
        scratch_shapes=[
            pltpu.VMEM((cells, BLK, BLK), dtype),
            pltpu.VMEM((SHARE, BLK), dtype),
            pltpu.VMEM((3, LAST * BLK, BLK), dtype),
            pltpu.VMEM((8, BLK), jnp.int32),
            pltpu.SMEM((8, BLK), jnp.int32),
            pltpu.SemaphoreType.DMA((COPIES,)),
            pltpu.SemaphoreType.DMA((COPIES,)),
            pltpu.SemaphoreType.DMA((3,)),
            pltpu.SemaphoreType.DMA((7,)),
            pltpu.VMEM((2 * DEPTH + 8, BLK), jnp.int32),
        ],
        compiler_params=pltpu.CompilerParams(
            collective_id=0, has_side_effects=True, vmem_limit_bytes=44 * MIB
        ),
        name="gather",
    )(block_mask.T, similarity)


def group_product(r_ref, c_ref, table, cell, g):
    return sum(
        jnp.dot(
            r_ref[table[p, cell]],
            c_ref[table[DEPTH + p, cell]],
            preferred_element_type=jnp.float32,
        )
        for p in [g * GROUP + t for t in range(GROUP)]
    )


def as_blocks(ref):
    return ref.reshape(ref.shape[0] * SLOTS, BLK, BLK)


def later_kernel(rows_ref, cols_ref, table_ref, extra_ref, table_v, table_s, sem):
    r_ref, c_ref = as_blocks(rows_ref), as_blocks(cols_ref)
    tiles, wide = extra_ref.shape[0] // BLK, extra_ref.shape[1] // BLK

    def here(i, j):
        return pl.ds(pl.multiple_of(i * BLK, BLK), BLK), pl.ds(j * BLK, BLK)

    def groups(table, cell):
        return (jnp.minimum(table[2 * DEPTH, cell], DEPTH) + GROUP - 1) // GROUP

    def add(table, i, j, first):
        cell = i * wide + j

        @pl.loop(first, groups(table, cell))
        def _(g):
            extra_ref[here(i, j)] += group_product(r_ref, c_ref, table, cell, g)

    @pl.loop(0, tiles)
    def _(i):
        top = table_ref[2 * DEPTH, i * wide]
        for j in range(1, wide):
            top = jnp.maximum(top, table_ref[2 * DEPTH, i * wide + j])

        @pl.when(top > GROUP)
        def _():
            for j in range(wide):
                cell = i * wide + j

                @pl.when(table_ref[2 * DEPTH, cell] > GROUP)
                def _():
                    extra_ref[here(i, j)] = group_product(r_ref, c_ref, table_ref, cell, 1)
                    add(table_ref, i, j, 2)

    most = table_ref[2 * DEPTH + 1, 0]

    @pl.loop(1, (most + DEPTH - 1) // DEPTH)
    def _(d):
        write_lists(table_v, pair_lists(rows_ref, cols_ref), d * DEPTH)
        copy = pltpu.make_async_copy(table_v, table_s, sem)
        copy.start()
        copy.wait()

        @pl.loop(0, tiles)
        def _(i):
            for j in range(wide):
                add(table_s, i, j, 0)


VMEM, SMEM = pl.BlockSpec(memory_space=pltpu.VMEM), pl.BlockSpec(memory_space=pltpu.SMEM)


def later(rows, cols, table, shape):
    return pl.pallas_call(
        later_kernel,
        out_shape=pltpu.VMEM(shape, jnp.float32),
        in_specs=[VMEM, VMEM, SMEM],
        out_specs=VMEM,
        scratch_shapes=[
            pltpu.VMEM(table.shape, jnp.int32),
            pltpu.SMEM(table.shape, jnp.int32),
            pltpu.SemaphoreType.DMA(()),
        ],
        compiler_params=pltpu.CompilerParams(vmem_limit_bytes=8 * MIB),
        name="later",
    )(rows, cols, table)


def product_kernel(
    rows_ref, cols_ref, table_ref, extra_ref, out_ref, total_ref, slots, send_sems, recv_sems
):
    row, col, layer = (lax.axis_index(a) for a in ("row", "col", "layer"))
    high, x = row // 4, row % 4
    near = [(4 * high + (x + s) % 4, col, layer) for s in range(1, 4)]
    far = (4 * (1 - high) + x, col, layer)
    barrier = pltpu.get_barrier_semaphore()
    for peer in near + [far]:
        pl.semaphore_signal(barrier, inc=1, device_id=peer, device_id_type=MESH)

    r_ref, c_ref = as_blocks(rows_ref), as_blocks(cols_ref)
    tiles, wide = out_ref.shape[0] // BLK, out_ref.shape[1] // BLK

    def one_row(i, sums):
        lines = pl.ds(pl.multiple_of(i * BLK, BLK), BLK)
        out = []
        for j in range(wide):
            cell = i * wide + j
            value = group_product(r_ref, c_ref, table_ref, cell, 0)
            has_more = jnp.full((BLK, BLK), table_ref[2 * DEPTH, cell], jnp.int32) > GROUP
            value = value + jnp.where(has_more, extra_ref[lines, pl.ds(j * BLK, BLK)], 0.0)
            value = value * value
            out_ref[lines, pl.ds(j * BLK, BLK)] = value
            out.append(sums[j] + jnp.sum(value.reshape(BLK // 8, 8, BLK), axis=0))
        return tuple(out)

    sums = tuple(jnp.zeros((8, BLK), jnp.float32) for _ in range(wide))
    sums = lax.fori_loop(0, tiles, one_row, sums, unroll=3)
    slots[x] = jnp.concatenate([jnp.sum(v, axis=0, keepdims=True) for v in sums], 1)
    pl.semaphore_wait(barrier, 4)

    def swap(k, src, dst, peer):
        return pltpu.make_async_remote_copy(
            src_ref=slots.at[src],
            dst_ref=slots.at[dst],
            send_sem=send_sems.at[k],
            recv_sem=recv_sems.at[k],
            device_id=peer,
            device_id_type=MESH,
        )

    copies = [swap(k, x, x, peer) for k, peer in enumerate(near)]
    for copy in copies:
        copy.start()
    for copy in copies:
        copy.wait()
    slots[4] = (slots[0] + slots[1]) + (slots[2] + slots[3])
    copy = swap(3, 4, 5, far)
    copy.start()
    copy.wait()
    total_ref[...] = slots[4] + slots[5]


def product(rows, cols, table, extra):
    lanes = extra.shape[1]
    return pl.pallas_call(
        product_kernel,
        out_shape=[pltpu.VMEM(extra.shape, jnp.float32), pltpu.VMEM((1, lanes), jnp.float32)],
        in_specs=[VMEM, VMEM, SMEM, VMEM],
        out_specs=[VMEM, VMEM],
        scratch_shapes=[
            pltpu.VMEM((6, 1, lanes), jnp.float32),
            pltpu.SemaphoreType.DMA((4,)),
            pltpu.SemaphoreType.DMA((4,)),
        ],
        compiler_params=pltpu.CompilerParams(
            collective_id=1, has_side_effects=True, vmem_limit_bytes=8 * MIB
        ),
        name="product",
    )(rows, cols, table, extra)


STEPS = 6


def scale_kernel(scaling, value_ref, total_ref, out_ref, staged, sems):
    step = staged.shape[1]
    total = total_ref[...]
    copies = []
    for t in range(STEPS):
        here = pl.ds(t * step, step)
        staged[t] = scaling * value_ref[here, :] / total
        copy = pltpu.make_async_copy(staged.at[t], out_ref.at[here], sems.at[t])
        copy.start()
        copies.append(copy)
    for copy in copies:
        copy.wait()


def scale(value, total, scaling):
    rows, lanes = value.shape
    return pl.pallas_call(
        functools.partial(scale_kernel, scaling),
        out_shape=jax.ShapeDtypeStruct(value.shape, jnp.float32),
        in_specs=[pl.BlockSpec(memory_space=pltpu.VMEM)] * 2,
        out_specs=pl.BlockSpec(memory_space=pltpu.HBM),
        scratch_shapes=[
            pltpu.VMEM((STEPS, rows // STEPS, lanes), jnp.float32),
            pltpu.SemaphoreType.DMA((STEPS,)),
        ],
        compiler_params=pltpu.CompilerParams(vmem_limit_bytes=16 * MIB),
        name="scale",
    )(value, total)


def body(similarity, block_mask):
    rows, cols, table = gather(block_mask, similarity)
    extra = later(rows, cols, table, similarity.shape)
    value, total = product(rows, cols, table, extra)
    scaling = similarity.shape[0] * lax.axis_size("row")
    return scale(value, total, float(scaling))


def solution(mesh):
    return jax.shard_map(
        body,
        mesh=mesh,
        in_specs=(P("row", ("col", "layer")), P("row", ("col", "layer"))),
        out_specs=P("row", ("col", "layer")),
        check_vma=False,
    )
```

```python
import functools

import jax
import jax.numpy as jnp
from jax import lax
from jax.experimental import pallas as pl
from jax.experimental.pallas import tpu as pltpu
from jax.sharding import PartitionSpec as P

BLK = 128
MAXNZ = 18
HEAD = 32
HALF = MAXNZ // 2
SLOTS = MAXNZ + 1
SHARE = SLOTS * BLK
TOP = BLK - HEAD
GROUP = 4
DEPTH = 16
MIB = 1 << 20
MESH = pl.DeviceIdType.MESH


def pack_share(mask_ref, x_ref, x_v, share, place_v, place_s, sems):
    cols, rows = mask_ref.shape
    strips = x_v.reshape(cols * rows * BLK, BLK)
    loads = [
        pltpu.make_async_copy(
            x_ref.at[:, pl.ds(j * BLK, BLK)],
            strips.at[pl.ds(j * rows * BLK, rows * BLK)],
            sems.at[j],
        )
        for j in range(cols)
    ]
    for load in loads:
        load.start()
    sub = lax.broadcasted_iota(jnp.int32, (HEAD, BLK), 0)
    lane = lax.broadcasted_iota(jnp.int32, (HEAD, BLK), 1)
    lane_row = (lane * 43) >> 8
    lane_col = lane - lane_row * cols
    lane8 = lane[:8]

    def find(i, carry):
        count, place = carry
        for j in range(cols):
            here = mask_ref[j, i]
            place = place + jnp.where(lane8 == count, here * (j * rows + i), 0)
            count = count + here
        return count, place

    zero = jnp.int32(0)
    _, place = lax.fori_loop(0, rows, find, (zero, jnp.zeros((8, BLK), jnp.int32)), unroll=3)
    place_v[...] = place
    move = pltpu.make_async_copy(place_v, place_s, sems.at[cols])
    move.start()

    def mark(i, carry):
        count, head = carry
        below = 8 + jnp.where(i < cols, i, i - cols + 8)
        for j in range(cols):
            here = mask_ref[j, i]
            cell = ((sub == j) & (lane_row == i)) | ((sub == below) & (lane_col == j))
            head = head + jnp.where(cell, here * (count + 1), 0)
            count = count + here
        return count, head

    _, head = lax.fori_loop(0, rows, mark, (zero, jnp.zeros((HEAD, BLK), jnp.int32)))
    head = jnp.where(lane < rows * cols, head, 0)
    share[pl.ds(TOP, HEAD), :] = head.astype(jnp.float32).astype(share.dtype)
    move.wait()
    for load in loads:
        load.wait()
    for s in range(MAXNZ):
        share[pl.ds((s + 1) * BLK, BLK), :] = x_v[place_s[0, s]]


def pair_lists(rows_ref, cols_ref):
    hr, hc = [], []
    for q in range(16):
        hr.append(rows_ref[q, pl.ds(TOP, HEAD), :].astype(jnp.float32)[0:8])
    for q in range(8):
        top = cols_ref[q, pl.ds(TOP, HEAD), :].astype(jnp.float32)
        hc += [top[8:16], top[16:24]]
    hr, hc = jnp.concatenate(hr, 0), jnp.concatenate(hc, 0)
    both = jnp.where((hr > 0) & (hc > 0), 1.0, 0.0)
    line = lax.broadcasted_iota(jnp.int32, (BLK, BLK), 0)
    before = line > lax.broadcasted_iota(jnp.int32, (BLK, BLK), 1)
    rank = jnp.dot(
        jnp.where(before, 1.0, 0.0).astype(jnp.bfloat16),
        both.astype(jnp.bfloat16),
        preferred_element_type=jnp.float32,
    )
    rank = jnp.where(both > 0, rank, -1.0).astype(jnp.int32)
    place_r = (line >> 3) * SLOTS + hr.astype(jnp.int32)
    place_c = (line >> 4) * SLOTS + hc.astype(jnp.int32)
    count = jnp.sum(both, axis=0, keepdims=True).astype(jnp.int32)
    return rank, place_r, place_c, count


def write_lists(table_v, lists, done):
    rank, place_r, place_c, count = lists
    for p in range(DEPTH):
        at = rank == done + p
        some = count > done + p
        first = jnp.sum(jnp.where(at, place_r, 0), axis=0, keepdims=True)
        second = jnp.sum(jnp.where(at, place_c, 0), axis=0, keepdims=True)
        table_v[pl.ds(p, 1), :] = jnp.where(some, first, 16 * SLOTS)
        table_v[pl.ds(DEPTH + p, 1), :] = jnp.where(some, second, 1)
    most = jnp.max(count, axis=1, keepdims=True)
    table_v[pl.ds(2 * DEPTH, 1), :] = count - done
    table_v[pl.ds(2 * DEPTH + 1, 1), :] = jnp.broadcast_to(most, count.shape)


LAST = 5
SPLIT = 7


def span(first, last):
    low = (first + 1) * BLK if first else TOP
    return pl.ds(low, (last + 1) * BLK - low)


def gather_kernel(
    mask_ref,
    x_ref,
    rows_ref,
    cols_ref,
    table_ref,
    x_v,
    share_ref,
    relay,
    place_v,
    place_s,
    send_sems,
    recv_sems,
    own_sems,
    pack_sems,
    table_v,
):
    row, col, layer = (lax.axis_index(a) for a in ("row", "col", "layer"))
    high, x = row // 4, row % 4
    z, low = col // 2, col % 2

    def along_z(step):
        return 2 * ((z + step) % 4) + low

    def along_x(step):
        return 4 * high + (x + step) % 4

    mate = 2 * z + 1 - low
    far = 4 * (1 - high) + x

    zp, zm = (row, along_z(1), layer), (row, along_z(3), layer)
    xp, xm = (along_x(1), col, layer), (along_x(3), col, layer)
    lo, hi = (row, mate, layer), (far, mate, layer)
    sib = (row, col, 1 - layer)

    barrier = pltpu.get_barrier_semaphore()
    for peer in (zp, zm, xp, xm, lo, hi, sib):
        pl.semaphore_signal(barrier, inc=1, device_id=peer, device_id_type=MESH)
    pack_share(mask_ref, x_ref, x_v, share_ref, place_v, place_s, pack_sems)
    pl.semaphore_wait(barrier, 7)

    ALL = span(0, MAXNZ)
    mine = 2 * col + layer
    keep = [
        pltpu.make_async_copy(share_ref.at[ALL], rows_ref.at[mine].at[ALL], own_sems.at[0]),
        pltpu.make_async_copy(share_ref.at[ALL], cols_ref.at[row].at[ALL], own_sems.at[1]),
    ]

    EARLY = MAXNZ - LAST
    H1, H2 = span(0, HALF), span(HALF, MAXNZ)
    U1, U2, L = span(0, SPLIT), span(SPLIT, EARLY), span(EARLY, MAXNZ)
    V1, V2, V3, V4 = span(0, 4), span(4, SPLIT), span(SPLIT, 10), span(10, EARLY)
    T = pl.ds(0, LAST * BLK)
    started = []
    waited = set()

    def send(src, dst, part, peer, into=None):
        k = len(started)
        copy = pltpu.make_async_remote_copy(
            src_ref=src.at[part],
            dst_ref=dst.at[part if into is None else into],
            send_sem=send_sems.at[k],
            recv_sem=recv_sems.at[k],
            device_id=peer,
            device_id_type=MESH,
        )
        copy.start()
        started.append(copy)
        return k

    def arrived(k, dst, part, peer):
        waited.add(k)
        pltpu.make_async_remote_copy(
            src_ref=dst.at[part],
            dst_ref=dst.at[part],
            send_sem=send_sems.at[k],
            recv_sem=recv_sems.at[k],
            device_id=peer,
            device_id_type=MESH,
        ).wait_recv()

    def other(q):
        return q + 1 - 2 * (q % 2)

    def r(q):
        return rows_ref.at[2 * q + layer]

    def rsib(q):
        return rows_ref.at[2 * q + 1 - layer]

    def c(q):
        return cols_ref.at[q]

    def across(q):
        return c((q + 4) % 8)

    own_r, own_c = r(col), c(row)
    y_r, y_c = r(mate), c(far)
    zm_r, zp_r, zz_r = (r(along_z(s)) for s in (3, 1, 2))
    ym_r, yp_r, yy_r = (r(other(along_z(s))) for s in (3, 1, 2))
    xm_c, xp_c, xx_c = (c(along_x(s)) for s in (3, 1, 2))
    ym_c, yp_c, yy_c = (across(along_x(s)) for s in (3, 1, 2))

    lo1 = send(share_ref, own_r, U1, lo)
    zp1 = send(share_ref, own_r, H1, zp)
    zm2 = send(share_ref, own_r, H2, zm)
    xp1 = send(share_ref, own_c, H1, xp)
    xm2 = send(share_ref, own_c, H2, xm)
    lo2 = send(share_ref, own_r, U2, lo)
    zp2 = send(share_ref, own_r, H2, zp)
    zm1 = send(share_ref, own_r, H1, zm)
    xp2 = send(share_ref, own_c, H2, xp)
    xm1 = send(share_ref, own_c, H1, xm)
    lo3 = send(share_ref, own_r, L, lo)
    sb0 = send(share_ref, own_r, ALL, sib)
    for copy in keep:
        copy.start()
    rows_ref[16, pl.ds(0, BLK), :] = jnp.zeros((BLK, BLK), rows_ref.dtype)

    arrived(lo1, y_r, U1, lo)
    hi1 = send(y_r, own_c, U1, hi)
    yzp1 = send(y_r, y_r, U1, zp)
    arrived(zp1, zm_r, H1, zm)
    fzp = send(zm_r, zm_r, H1, zp)
    arrived(zm2, zp_r, H2, zp)
    fzm = send(zp_r, zp_r, H2, zm)
    arrived(xp1, xm_c, H1, xm)
    fxp = send(xm_c, xm_c, H1, xp)
    arrived(xm2, xp_c, H2, xp)
    fxm = send(xp_c, xp_c, H2, xm)
    txp = send(xp_c, relay.at[0], L, lo, T)
    lzp = send(zp_r, zp_r, L, lo)
    arrived(lo2, y_r, U2, lo)
    hi2 = send(y_r, own_c, U2, hi)
    yzm2 = send(y_r, y_r, U2, zm)
    yzp2 = send(y_r, y_r, U2, zp)
    yzm1 = send(y_r, y_r, U1, zm)
    arrived(hi1, y_c, U1, hi)
    yxp1 = send(y_c, y_c, U1, xp)
    arrived(lo3, y_r, L, lo)
    hi3 = send(y_r, own_c, L, hi)
    sb1 = send(y_r, y_r, ALL, sib)

    arrived(zp2, zm_r, H2, zm)
    arrived(xp2, xm_c, H2, xm)
    txm = send(xm_c, relay.at[1], L, lo, T)
    lzm = send(zm_r, zm_r, L, lo)
    sb2 = send(zm_r, zm_r, ALL, sib)
    arrived(zm1, zp_r, H1, zp)
    sb3 = send(zp_r, zp_r, ALL, sib)
    arrived(hi2, y_c, U2, hi)
    yxm2 = send(y_c, y_c, U2, xm)
    yxp2 = send(y_c, y_c, U2, xp)
    yxm1 = send(y_c, y_c, U1, xm)
    arrived(txp, relay.at[0], T, lo)
    uxp = send(relay.at[0], xp_c, T, hi, L)
    arrived(fxm, xx_c, H2, xp)
    txx = send(xx_c, relay.at[2], L, lo, T)
    arrived(fzm, zz_r, H2, zp)
    lzz = send(zz_r, zz_r, L, lo)
    arrived(fzp, zz_r, H1, zm)
    sb4 = send(zz_r, zz_r, ALL, sib)
    arrived(txm, relay.at[1], T, lo)
    uxm = send(relay.at[1], xm_c, T, hi, L)

    arrived(yzp1, ym_r, U1, zm)
    gzp = send(ym_r, ym_r, V1, zp)
    gzq = send(ym_r, ym_r, V2, zp)
    arrived(yzm2, yp_r, U2, zp)
    gzm = send(yp_r, yp_r, V3, zm)
    gzn = send(yp_r, yp_r, V4, zm)
    arrived(yxp1, ym_c, U1, xm)
    gxp = send(ym_c, ym_c, U1, xp)
    arrived(yxm2, yp_c, U2, xp)
    gxm = send(yp_c, yp_c, U2, xm)
    sb5 = send(ym_r, ym_r, U1, sib)
    sb6 = send(yp_r, yp_r, U2, sib)
    arrived(lzp, yp_r, L, lo)
    sb12 = send(yp_r, yp_r, L, sib)
    arrived(lzm, ym_r, L, lo)
    sb13 = send(ym_r, ym_r, L, sib)
    arrived(txx, relay.at[2], T, lo)
    uxx = send(relay.at[2], xx_c, T, hi, L)
    arrived(yzm1, yp_r, U1, zp)
    sb14 = send(yp_r, yp_r, U1, sib)
    arrived(yzp2, ym_r, U2, zm)
    sb15 = send(ym_r, ym_r, U2, sib)
    arrived(lzz, yy_r, L, lo)
    sb7 = send(yy_r, yy_r, L, sib)
    arrived(gzp, yy_r, V1, zm)
    sb8 = send(yy_r, yy_r, V1, sib)
    arrived(gzm, yy_r, V3, zp)
    sb9 = send(yy_r, yy_r, V3, sib)
    arrived(gzn, yy_r, V4, zp)
    sb10 = send(yy_r, yy_r, V4, sib)
    arrived(gzq, yy_r, V2, zm)
    sb11 = send(yy_r, yy_r, V2, sib)

    for copy in keep:
        copy.wait()
    arrived(xm1, xp_c, H1, xp)
    arrived(fxp, xx_c, H1, xm)
    arrived(yxm1, yp_c, U1, xp)
    arrived(gxp, yy_c, U1, xm)
    arrived(sb0, rsib(col), ALL, sib)
    arrived(sb1, rsib(mate), ALL, sib)
    arrived(sb2, rsib(along_z(3)), ALL, sib)
    arrived(sb3, rsib(along_z(1)), ALL, sib)
    arrived(sb4, rsib(along_z(2)), ALL, sib)
    arrived(sb5, rsib(other(along_z(3))), U1, sib)
    arrived(sb14, rsib(other(along_z(1))), U1, sib)
    arrived(sb8, rsib(other(along_z(2))), V1, sib)
    write_lists(table_v, pair_lists(rows_ref, cols_ref), 0)
    hand = pltpu.make_async_copy(table_v, table_ref, own_sems.at[2])
    hand.start()

    arrived(hi3, y_c, L, hi)
    arrived(yxp2, ym_c, U2, xm)
    arrived(uxp, yp_c, L, hi)
    arrived(uxm, ym_c, L, hi)
    arrived(uxx, yy_c, L, hi)
    arrived(gxm, yy_c, U2, xp)
    arrived(sb6, rsib(other(along_z(1))), U2, sib)
    arrived(sb12, rsib(other(along_z(1))), L, sib)
    arrived(sb13, rsib(other(along_z(3))), L, sib)
    arrived(sb15, rsib(other(along_z(3))), U2, sib)
    arrived(sb7, rsib(other(along_z(2))), L, sib)
    arrived(sb9, rsib(other(along_z(2))), V3, sib)
    arrived(sb10, rsib(other(along_z(2))), V4, sib)
    arrived(sb11, rsib(other(along_z(2))), V2, sib)
    assert waited == set(range(len(started))) and len(started) == COPIES
    for copy in started:
        copy.wait_send()
    hand.wait()


COPIES = 57


def gather(block_mask, similarity):
    dtype = similarity.dtype
    cells = block_mask.size
    return pl.pallas_call(
        gather_kernel,
        out_shape=[
            pltpu.VMEM((17, SHARE, BLK), dtype),
            pltpu.VMEM((8, SHARE, BLK), dtype),
            pltpu.SMEM((2 * DEPTH + 8, BLK), jnp.int32),
        ],
        in_specs=[
            pl.BlockSpec(memory_space=pltpu.SMEM),
            pl.BlockSpec(memory_space=pl.ANY),
        ],
        out_specs=[
            pl.BlockSpec(memory_space=pltpu.VMEM),
            pl.BlockSpec(memory_space=pltpu.VMEM),
            pl.BlockSpec(memory_space=pltpu.SMEM),
        ],
        scratch_shapes=[
            pltpu.VMEM((cells, BLK, BLK), dtype),
            pltpu.VMEM((SHARE, BLK), dtype),
            pltpu.VMEM((3, LAST * BLK, BLK), dtype),
            pltpu.VMEM((8, BLK), jnp.int32),
            pltpu.SMEM((8, BLK), jnp.int32),
            pltpu.SemaphoreType.DMA((COPIES,)),
            pltpu.SemaphoreType.DMA((COPIES,)),
            pltpu.SemaphoreType.DMA((3,)),
            pltpu.SemaphoreType.DMA((7,)),
            pltpu.VMEM((2 * DEPTH + 8, BLK), jnp.int32),
        ],
        compiler_params=pltpu.CompilerParams(
            collective_id=0, has_side_effects=True, vmem_limit_bytes=44 * MIB
        ),
        name="gather",
    )(block_mask.T, similarity)


def group_product(r_ref, c_ref, table, cell, g):
    return sum(
        jnp.dot(
            r_ref[table[p, cell]],
            c_ref[table[DEPTH + p, cell]],
            preferred_element_type=jnp.float32,
        )
        for p in [g * GROUP + t for t in range(GROUP)]
    )


def as_blocks(ref):
    return ref.reshape(ref.shape[0] * SLOTS, BLK, BLK)


AT_ONCE = 4


def later_kernel(rows_ref, cols_ref, table_ref, extra_ref, table_v, table_s, list_s, sem):
    r_ref, c_ref = as_blocks(rows_ref), as_blocks(cols_ref)
    cells = extra_ref.shape[0] - 1

    def look(cell, found):
        list_s[found] = cell
        return found + jnp.where(table_ref[2 * DEPTH, cell] > GROUP, 1, 0)

    found = lax.fori_loop(0, cells, look, jnp.int32(0), unroll=8)
    for t in range(AT_ONCE):
        list_s[found + t] = cells

    @pl.loop(0, (found + AT_ONCE - 1) // AT_ONCE)
    def _(n):
        for t in range(AT_ONCE):
            cell = list_s[n * AT_ONCE + t]
            extra_ref[cell] = group_product(r_ref, c_ref, table_ref, cell, 1)

    def add(table, cell, first):
        @pl.loop(first, (jnp.minimum(table[2 * DEPTH, cell], DEPTH) + GROUP - 1) // GROUP)
        def _(g):
            extra_ref[cell] += group_product(r_ref, c_ref, table, cell, g)

    most = table_ref[2 * DEPTH + 1, 0]

    @pl.when(most > 2 * GROUP)
    def _():
        @pl.loop(0, found)
        def _(n):
            add(table_ref, list_s[n], 2)

    @pl.loop(1, (most + DEPTH - 1) // DEPTH)
    def _(d):
        write_lists(table_v, pair_lists(rows_ref, cols_ref), d * DEPTH)
        copy = pltpu.make_async_copy(table_v, table_s, sem)
        copy.start()
        copy.wait()

        @pl.loop(0, found)
        def _(n):
            add(table_s, list_s[n], 0)


VMEM, SMEM = pl.BlockSpec(memory_space=pltpu.VMEM), pl.BlockSpec(memory_space=pltpu.SMEM)


def later(rows, cols, table, cells):
    return pl.pallas_call(
        later_kernel,
        out_shape=pltpu.VMEM((cells + 1, BLK, BLK), jnp.float32),
        in_specs=[VMEM, VMEM, SMEM],
        out_specs=VMEM,
        scratch_shapes=[
            pltpu.VMEM(table.shape, jnp.int32),
            pltpu.SMEM(table.shape, jnp.int32),
            pltpu.SMEM((BLK,), jnp.int32),
            pltpu.SemaphoreType.DMA(()),
        ],
        compiler_params=pltpu.CompilerParams(vmem_limit_bytes=8 * MIB),
        name="later",
    )(rows, cols, table)


def product_kernel(
    rows_ref, cols_ref, table_ref, extra_ref, out_ref, total_ref, slots, send_sems, recv_sems
):
    row, col, layer = (lax.axis_index(a) for a in ("row", "col", "layer"))
    peers = [((row + s) % 8, col, layer) for s in range(1, 8)]
    barrier = pltpu.get_barrier_semaphore()
    for peer in peers:
        pl.semaphore_signal(barrier, inc=1, device_id=peer, device_id_type=MESH)

    r_ref, c_ref = as_blocks(rows_ref), as_blocks(cols_ref)
    tiles, wide = out_ref.shape[0] // BLK, out_ref.shape[1] // BLK

    def one_row(i, sums):
        lines = pl.ds(pl.multiple_of(i * BLK, BLK), BLK)
        out = []
        for j in range(wide):
            cell = i * wide + j
            value = group_product(r_ref, c_ref, table_ref, cell, 0)
            has_more = jnp.full((BLK, BLK), table_ref[2 * DEPTH, cell], jnp.int32) > GROUP
            value = value + jnp.where(has_more, extra_ref[cell], 0.0)
            value = value * value
            out_ref[lines, pl.ds(j * BLK, BLK)] = value
            out.append(sums[j] + jnp.sum(value.reshape(BLK // 8, 8, BLK), axis=0))
        return tuple(out)

    sums = tuple(jnp.zeros((8, BLK), jnp.float32) for _ in range(wide))
    sums = lax.fori_loop(0, tiles, one_row, sums, unroll=3)
    slots[row] = jnp.concatenate([jnp.sum(v, axis=0, keepdims=True) for v in sums], 1)
    pl.semaphore_wait(barrier, 7)
    copies = [
        pltpu.make_async_remote_copy(
            src_ref=slots.at[row],
            dst_ref=slots.at[row],
            send_sem=send_sems.at[k],
            recv_sem=recv_sems.at[k],
            device_id=peer,
            device_id_type=MESH,
        )
        for k, peer in enumerate(peers)
    ]
    for copy in copies:
        copy.start()
    for copy in copies:
        copy.wait()
    total = slots[0]
    for q in range(1, 8):
        total = total + slots[q]
    total_ref[...] = total


def product(rows, cols, table, extra, shape):
    lanes = shape[1]
    return pl.pallas_call(
        product_kernel,
        out_shape=[pltpu.VMEM(shape, jnp.float32), pltpu.VMEM((1, lanes), jnp.float32)],
        in_specs=[VMEM, VMEM, SMEM, VMEM],
        out_specs=[VMEM, VMEM],
        scratch_shapes=[
            pltpu.VMEM((8, 1, lanes), jnp.float32),
            pltpu.SemaphoreType.DMA((7,)),
            pltpu.SemaphoreType.DMA((7,)),
        ],
        compiler_params=pltpu.CompilerParams(
            collective_id=1, has_side_effects=True, vmem_limit_bytes=8 * MIB
        ),
        name="product",
    )(rows, cols, table, extra)


STEPS = 6


def scale_kernel(scaling, value_ref, total_ref, out_ref, staged, sems):
    step = staged.shape[1]
    total = total_ref[...]
    copies = []
    for t in range(STEPS):
        here = pl.ds(t * step, step)
        staged[t] = scaling * value_ref[here, :] / total
        copy = pltpu.make_async_copy(staged.at[t], out_ref.at[here], sems.at[t])
        copy.start()
        copies.append(copy)
    for copy in copies:
        copy.wait()


def scale(value, total, scaling):
    rows, lanes = value.shape
    return pl.pallas_call(
        functools.partial(scale_kernel, scaling),
        out_shape=jax.ShapeDtypeStruct(value.shape, jnp.float32),
        in_specs=[pl.BlockSpec(memory_space=pltpu.VMEM)] * 2,
        out_specs=pl.BlockSpec(memory_space=pltpu.HBM),
        scratch_shapes=[
            pltpu.VMEM((STEPS, rows // STEPS, lanes), jnp.float32),
            pltpu.SemaphoreType.DMA((STEPS,)),
        ],
        compiler_params=pltpu.CompilerParams(vmem_limit_bytes=16 * MIB),
        name="scale",
    )(value, total)


def body(similarity, block_mask):
    rows, cols, table = gather(block_mask, similarity)
    extra = later(rows, cols, table, block_mask.size)
    value, total = product(rows, cols, table, extra, similarity.shape)
    scaling = similarity.shape[0] * lax.axis_size("row")
    return scale(value, total, float(scaling))


def solution(mesh):
    return jax.shard_map(
        body,
        mesh=mesh,
        in_specs=(P("row", ("col", "layer")), P("row", ("col", "layer"))),
        out_specs=P("row", ("col", "layer")),
        check_vma=False,
    )
```

```python
import functools

import jax
import jax.numpy as jnp
from jax import lax
from jax.experimental import pallas as pl
from jax.experimental.pallas import tpu as pltpu
from jax.sharding import PartitionSpec as P

BLK = 128
MAXNZ = 18
HEAD = 32
HALF = MAXNZ // 2
SLOTS = MAXNZ + 1
SHARE = SLOTS * BLK
TOP = BLK - HEAD
GROUP = 4
DEPTH = 16
MIB = 1 << 20
MESH = pl.DeviceIdType.MESH


def pack_share(mask_ref, x_ref, mask_s, x_v, share, place_v, place_s, signal, sems):
    cols, rows = mask_ref.shape
    fetch = pltpu.make_async_copy(mask_ref, mask_s, sems.at[cols + 1])
    fetch.start()
    strips = x_v.reshape(cols * rows * BLK, BLK)
    loads = [
        pltpu.make_async_copy(
            x_ref.at[:, pl.ds(j * BLK, BLK)],
            strips.at[pl.ds(j * rows * BLK, rows * BLK)],
            sems.at[j],
        )
        for j in range(cols)
    ]
    for load in loads:
        load.start()
    signal()
    sub = lax.broadcasted_iota(jnp.int32, (HEAD, BLK), 0)
    lane = lax.broadcasted_iota(jnp.int32, (HEAD, BLK), 1)
    lane_row = (lane * 43) >> 8
    lane_col = lane - lane_row * cols
    lane8 = lane[:8]

    def find(i, carry):
        count, place = carry
        for j in range(cols):
            here = mask_s[j, i]
            place = place + jnp.where(lane8 == count, here * (j * rows + i), 0)
            count = count + here
        return count, place

    fetch.wait()
    zero = jnp.int32(0)
    _, place = lax.fori_loop(0, rows, find, (zero, jnp.zeros((8, BLK), jnp.int32)), unroll=3)
    place_v[...] = place
    move = pltpu.make_async_copy(place_v, place_s, sems.at[cols])
    move.start()

    def mark(i, carry):
        count, head = carry
        below = 8 + jnp.where(i < cols, i, i - cols + 8)
        for j in range(cols):
            here = mask_s[j, i]
            cell = ((sub == j) & (lane_row == i)) | ((sub == below) & (lane_col == j))
            head = head + jnp.where(cell, here * (count + 1), 0)
            count = count + here
        return count, head

    _, head = lax.fori_loop(0, rows, mark, (zero, jnp.zeros((HEAD, BLK), jnp.int32)))
    head = jnp.where(lane < rows * cols, head, 0)
    share[pl.ds(TOP, HEAD), :] = head.astype(jnp.float32).astype(share.dtype)
    move.wait()
    for load in loads:
        load.wait()
    for s in range(MAXNZ):
        share[pl.ds((s + 1) * BLK, BLK), :] = x_v[place_s[0, s]]


def pair_lists(rows_ref, cols_ref):
    hr, hc = [], []
    for q in range(16):
        hr.append(rows_ref[q, pl.ds(TOP, HEAD), :].astype(jnp.float32)[0:8])
    for q in range(8):
        top = cols_ref[q, pl.ds(TOP, HEAD), :].astype(jnp.float32)
        hc += [top[8:16], top[16:24]]
    hr, hc = jnp.concatenate(hr, 0), jnp.concatenate(hc, 0)
    both = jnp.where((hr > 0) & (hc > 0), 1.0, 0.0)
    line = lax.broadcasted_iota(jnp.int32, (BLK, BLK), 0)
    before = line > lax.broadcasted_iota(jnp.int32, (BLK, BLK), 1)
    rank = jnp.dot(
        jnp.where(before, 1.0, 0.0).astype(jnp.bfloat16),
        both.astype(jnp.bfloat16),
        preferred_element_type=jnp.float32,
    )
    rank = jnp.where(both > 0, rank, -1.0).astype(jnp.int32)
    place_r = (line >> 3) * SLOTS + hr.astype(jnp.int32)
    place_c = (line >> 4) * SLOTS + hc.astype(jnp.int32)
    count = jnp.sum(both, axis=0, keepdims=True).astype(jnp.int32)
    return rank, place_r, place_c, count


def write_lists(table_v, lists, done):
    rank, place_r, place_c, count = lists
    for p in range(DEPTH):
        at = rank == done + p
        some = count > done + p
        first = jnp.sum(jnp.where(at, place_r, 0), axis=0, keepdims=True)
        second = jnp.sum(jnp.where(at, place_c, 0), axis=0, keepdims=True)
        table_v[pl.ds(p, 1), :] = jnp.where(some, first, 16 * SLOTS)
        table_v[pl.ds(DEPTH + p, 1), :] = jnp.where(some, second, 1)
    most = jnp.max(count, axis=1, keepdims=True)
    table_v[pl.ds(2 * DEPTH, 1), :] = count - done
    table_v[pl.ds(2 * DEPTH + 1, 1), :] = jnp.broadcast_to(most, count.shape)


LAST = 5
SPLIT = 7


def span(first, last):
    low = (first + 1) * BLK if first else TOP
    return pl.ds(low, (last + 1) * BLK - low)


def gather_kernel(
    mask_ref,
    x_ref,
    rows_ref,
    cols_ref,
    table_ref,
    mask_s,
    x_v,
    share_ref,
    relay,
    place_v,
    place_s,
    send_sems,
    recv_sems,
    own_sems,
    pack_sems,
    table_v,
):
    row, col, layer = (lax.axis_index(a) for a in ("row", "col", "layer"))
    high, x = row // 4, row % 4
    z, low = col // 2, col % 2

    def along_z(step):
        return 2 * ((z + step) % 4) + low

    def along_x(step):
        return 4 * high + (x + step) % 4

    mate = 2 * z + 1 - low
    far = 4 * (1 - high) + x

    zp, zm = (row, along_z(1), layer), (row, along_z(3), layer)
    xp, xm = (along_x(1), col, layer), (along_x(3), col, layer)
    lo, hi = (row, mate, layer), (far, mate, layer)
    sib = (row, col, 1 - layer)

    barrier = pltpu.get_barrier_semaphore()

    def signal():
        for peer in (zp, zm, xp, xm, lo, hi, sib):
            pl.semaphore_signal(barrier, inc=1, device_id=peer, device_id_type=MESH)

    pack_share(mask_ref, x_ref, mask_s, x_v, share_ref, place_v, place_s, signal, pack_sems)
    pl.semaphore_wait(barrier, 7)

    ALL = span(0, MAXNZ)
    mine = 2 * col + layer
    keep = [
        pltpu.make_async_copy(share_ref.at[ALL], rows_ref.at[mine].at[ALL], own_sems.at[0]),
        pltpu.make_async_copy(share_ref.at[ALL], cols_ref.at[row].at[ALL], own_sems.at[1]),
    ]

    EARLY = MAXNZ - LAST
    H1, H2 = span(0, HALF), span(HALF, MAXNZ)
    U1, U2, L = span(0, SPLIT), span(SPLIT, EARLY), span(EARLY, MAXNZ)
    V1, V2, V3, V4 = span(0, 4), span(4, SPLIT), span(SPLIT, 10), span(10, EARLY)
    T = pl.ds(0, LAST * BLK)
    started = []
    waited = set()

    def send(src, dst, part, peer, into=None):
        k = len(started)
        copy = pltpu.make_async_remote_copy(
            src_ref=src.at[part],
            dst_ref=dst.at[part if into is None else into],
            send_sem=send_sems.at[k],
            recv_sem=recv_sems.at[k],
            device_id=peer,
            device_id_type=MESH,
        )
        copy.start()
        started.append(copy)
        return k

    def arrived(k, dst, part, peer):
        waited.add(k)
        pltpu.make_async_remote_copy(
            src_ref=dst.at[part],
            dst_ref=dst.at[part],
            send_sem=send_sems.at[k],
            recv_sem=recv_sems.at[k],
            device_id=peer,
            device_id_type=MESH,
        ).wait_recv()

    def other(q):
        return q + 1 - 2 * (q % 2)

    def r(q):
        return rows_ref.at[2 * q + layer]

    def rsib(q):
        return rows_ref.at[2 * q + 1 - layer]

    def c(q):
        return cols_ref.at[q]

    def across(q):
        return c((q + 4) % 8)

    own_r, own_c = r(col), c(row)
    y_r, y_c = r(mate), c(far)
    zm_r, zp_r, zz_r = (r(along_z(s)) for s in (3, 1, 2))
    ym_r, yp_r, yy_r = (r(other(along_z(s))) for s in (3, 1, 2))
    xm_c, xp_c, xx_c = (c(along_x(s)) for s in (3, 1, 2))
    ym_c, yp_c, yy_c = (across(along_x(s)) for s in (3, 1, 2))

    lo1 = send(share_ref, own_r, U1, lo)
    zp1 = send(share_ref, own_r, H1, zp)
    zm2 = send(share_ref, own_r, H2, zm)
    xp1 = send(share_ref, own_c, H1, xp)
    xm2 = send(share_ref, own_c, H2, xm)
    lo2 = send(share_ref, own_r, U2, lo)
    zp2 = send(share_ref, own_r, H2, zp)
    zm1 = send(share_ref, own_r, H1, zm)
    xp2 = send(share_ref, own_c, H2, xp)
    xm1 = send(share_ref, own_c, H1, xm)
    lo3 = send(share_ref, own_r, L, lo)
    sb0 = send(share_ref, own_r, ALL, sib)
    for copy in keep:
        copy.start()
    rows_ref[16, pl.ds(0, BLK), :] = jnp.zeros((BLK, BLK), rows_ref.dtype)

    arrived(lo1, y_r, U1, lo)
    hi1 = send(y_r, own_c, U1, hi)
    yzp1 = send(y_r, y_r, U1, zp)
    arrived(zp1, zm_r, H1, zm)
    fzp = send(zm_r, zm_r, H1, zp)
    arrived(zm2, zp_r, H2, zp)
    fzm = send(zp_r, zp_r, H2, zm)
    arrived(xp1, xm_c, H1, xm)
    fxp = send(xm_c, xm_c, H1, xp)
    arrived(xm2, xp_c, H2, xp)
    fxm = send(xp_c, xp_c, H2, xm)
    txp = send(xp_c, relay.at[0], L, lo, T)
    lzp = send(zp_r, zp_r, L, lo)
    arrived(lo2, y_r, U2, lo)
    hi2 = send(y_r, own_c, U2, hi)
    yzm2 = send(y_r, y_r, U2, zm)
    yzp2 = send(y_r, y_r, U2, zp)
    yzm1 = send(y_r, y_r, U1, zm)
    arrived(hi1, y_c, U1, hi)
    yxp1 = send(y_c, y_c, U1, xp)
    arrived(lo3, y_r, L, lo)
    hi3 = send(y_r, own_c, L, hi)
    sb1 = send(y_r, y_r, ALL, sib)

    arrived(zp2, zm_r, H2, zm)
    arrived(xp2, xm_c, H2, xm)
    txm = send(xm_c, relay.at[1], L, lo, T)
    lzm = send(zm_r, zm_r, L, lo)
    sb2 = send(zm_r, zm_r, ALL, sib)
    arrived(zm1, zp_r, H1, zp)
    sb3 = send(zp_r, zp_r, ALL, sib)
    arrived(hi2, y_c, U2, hi)
    yxm2 = send(y_c, y_c, U2, xm)
    yxp2 = send(y_c, y_c, U2, xp)
    yxm1 = send(y_c, y_c, U1, xm)
    arrived(txp, relay.at[0], T, lo)
    uxp = send(relay.at[0], xp_c, T, hi, L)
    arrived(fxm, xx_c, H2, xp)
    txx = send(xx_c, relay.at[2], L, lo, T)
    arrived(fzm, zz_r, H2, zp)
    lzz = send(zz_r, zz_r, L, lo)
    arrived(fzp, zz_r, H1, zm)
    sb4 = send(zz_r, zz_r, ALL, sib)
    arrived(txm, relay.at[1], T, lo)
    uxm = send(relay.at[1], xm_c, T, hi, L)

    arrived(yzp1, ym_r, U1, zm)
    gzp = send(ym_r, ym_r, V1, zp)
    gzq = send(ym_r, ym_r, V2, zp)
    arrived(yzm2, yp_r, U2, zp)
    gzm = send(yp_r, yp_r, V3, zm)
    gzn = send(yp_r, yp_r, V4, zm)
    arrived(yxp1, ym_c, U1, xm)
    gxp = send(ym_c, ym_c, U1, xp)
    arrived(yxm2, yp_c, U2, xp)
    gxm = send(yp_c, yp_c, U2, xm)
    sb5 = send(ym_r, ym_r, U1, sib)
    sb6 = send(yp_r, yp_r, U2, sib)
    arrived(lzp, yp_r, L, lo)
    sb12 = send(yp_r, yp_r, L, sib)
    arrived(lzm, ym_r, L, lo)
    sb13 = send(ym_r, ym_r, L, sib)
    arrived(txx, relay.at[2], T, lo)
    uxx = send(relay.at[2], xx_c, T, hi, L)
    arrived(yzm1, yp_r, U1, zp)
    sb14 = send(yp_r, yp_r, U1, sib)
    arrived(yzp2, ym_r, U2, zm)
    sb15 = send(ym_r, ym_r, U2, sib)
    arrived(lzz, yy_r, L, lo)
    sb7 = send(yy_r, yy_r, L, sib)
    arrived(gzp, yy_r, V1, zm)
    sb8 = send(yy_r, yy_r, V1, sib)
    arrived(gzm, yy_r, V3, zp)
    sb9 = send(yy_r, yy_r, V3, sib)
    arrived(gzn, yy_r, V4, zp)
    sb10 = send(yy_r, yy_r, V4, sib)
    arrived(gzq, yy_r, V2, zm)
    sb11 = send(yy_r, yy_r, V2, sib)

    for copy in keep:
        copy.wait()
    arrived(xm1, xp_c, H1, xp)
    arrived(fxp, xx_c, H1, xm)
    arrived(yxm1, yp_c, U1, xp)
    arrived(gxp, yy_c, U1, xm)
    arrived(sb0, rsib(col), ALL, sib)
    arrived(sb1, rsib(mate), ALL, sib)
    arrived(sb2, rsib(along_z(3)), ALL, sib)
    arrived(sb3, rsib(along_z(1)), ALL, sib)
    arrived(sb4, rsib(along_z(2)), ALL, sib)
    arrived(sb5, rsib(other(along_z(3))), U1, sib)
    arrived(sb14, rsib(other(along_z(1))), U1, sib)
    arrived(sb8, rsib(other(along_z(2))), V1, sib)
    write_lists(table_v, pair_lists(rows_ref, cols_ref), 0)
    hand = pltpu.make_async_copy(table_v, table_ref, own_sems.at[2])
    hand.start()

    arrived(hi3, y_c, L, hi)
    arrived(yxp2, ym_c, U2, xm)
    arrived(uxp, yp_c, L, hi)
    arrived(uxm, ym_c, L, hi)
    arrived(uxx, yy_c, L, hi)
    arrived(gxm, yy_c, U2, xp)
    arrived(sb6, rsib(other(along_z(1))), U2, sib)
    arrived(sb12, rsib(other(along_z(1))), L, sib)
    arrived(sb13, rsib(other(along_z(3))), L, sib)
    arrived(sb15, rsib(other(along_z(3))), U2, sib)
    arrived(sb7, rsib(other(along_z(2))), L, sib)
    arrived(sb9, rsib(other(along_z(2))), V3, sib)
    arrived(sb10, rsib(other(along_z(2))), V4, sib)
    arrived(sb11, rsib(other(along_z(2))), V2, sib)
    assert waited == set(range(len(started))) and len(started) == COPIES
    for copy in started:
        copy.wait_send()
    hand.wait()


COPIES = 57


def gather(block_mask, similarity):
    dtype = similarity.dtype
    cells = block_mask.size
    return pl.pallas_call(
        gather_kernel,
        out_shape=[
            pltpu.VMEM((17, SHARE, BLK), dtype),
            pltpu.VMEM((8, SHARE, BLK), dtype),
            pltpu.SMEM((2 * DEPTH + 8, BLK), jnp.int32),
        ],
        in_specs=[pl.BlockSpec(memory_space=pltpu.HBM)] * 2,
        out_specs=[
            pl.BlockSpec(memory_space=pltpu.VMEM),
            pl.BlockSpec(memory_space=pltpu.VMEM),
            pl.BlockSpec(memory_space=pltpu.SMEM),
        ],
        scratch_shapes=[
            pltpu.SMEM(block_mask.shape[::-1], jnp.int32),
            pltpu.VMEM((cells, BLK, BLK), dtype),
            pltpu.VMEM((SHARE, BLK), dtype),
            pltpu.VMEM((3, LAST * BLK, BLK), dtype),
            pltpu.VMEM((8, BLK), jnp.int32),
            pltpu.SMEM((8, BLK), jnp.int32),
            pltpu.SemaphoreType.DMA((COPIES,)),
            pltpu.SemaphoreType.DMA((COPIES,)),
            pltpu.SemaphoreType.DMA((3,)),
            pltpu.SemaphoreType.DMA((8,)),
            pltpu.VMEM((2 * DEPTH + 8, BLK), jnp.int32),
        ],
        compiler_params=pltpu.CompilerParams(
            collective_id=0, has_side_effects=True, vmem_limit_bytes=44 * MIB
        ),
        name="gather",
    )(block_mask.T, similarity)


def group_product(r_ref, c_ref, table, cell, g):
    return sum(
        jnp.dot(
            r_ref[table[p, cell]],
            c_ref[table[DEPTH + p, cell]],
            preferred_element_type=jnp.float32,
        )
        for p in [g * GROUP + t for t in range(GROUP)]
    )


def as_blocks(ref):
    return ref.reshape(ref.shape[0] * SLOTS, BLK, BLK)


AT_ONCE = 4


def later_kernel(rows_ref, cols_ref, table_ref, extra_ref, table_v, table_s, list_s, sem):
    r_ref, c_ref = as_blocks(rows_ref), as_blocks(cols_ref)
    cells = extra_ref.shape[0] - 1

    def look(cell, found):
        list_s[found] = cell
        return found + jnp.where(table_ref[2 * DEPTH, cell] > GROUP, 1, 0)

    found = lax.fori_loop(0, cells, look, jnp.int32(0), unroll=8)
    for t in range(AT_ONCE):
        list_s[found + t] = cells

    @pl.loop(0, (found + AT_ONCE - 1) // AT_ONCE)
    def _(n):
        for t in range(AT_ONCE):
            cell = list_s[n * AT_ONCE + t]
            extra_ref[cell] = group_product(r_ref, c_ref, table_ref, cell, 1)

    def add(table, cell, first):
        @pl.loop(first, (jnp.minimum(table[2 * DEPTH, cell], DEPTH) + GROUP - 1) // GROUP)
        def _(g):
            extra_ref[cell] += group_product(r_ref, c_ref, table, cell, g)

    most = table_ref[2 * DEPTH + 1, 0]

    @pl.when(most > 2 * GROUP)
    def _():
        @pl.loop(0, found)
        def _(n):
            add(table_ref, list_s[n], 2)

    @pl.loop(1, (most + DEPTH - 1) // DEPTH)
    def _(d):
        write_lists(table_v, pair_lists(rows_ref, cols_ref), d * DEPTH)
        copy = pltpu.make_async_copy(table_v, table_s, sem)
        copy.start()
        copy.wait()

        @pl.loop(0, found)
        def _(n):
            add(table_s, list_s[n], 0)


VMEM, SMEM = pl.BlockSpec(memory_space=pltpu.VMEM), pl.BlockSpec(memory_space=pltpu.SMEM)


def later(rows, cols, table, cells):
    return pl.pallas_call(
        later_kernel,
        out_shape=pltpu.VMEM((cells + 1, BLK, BLK), jnp.float32),
        in_specs=[VMEM, VMEM, SMEM],
        out_specs=VMEM,
        scratch_shapes=[
            pltpu.VMEM(table.shape, jnp.int32),
            pltpu.SMEM(table.shape, jnp.int32),
            pltpu.SMEM((BLK,), jnp.int32),
            pltpu.SemaphoreType.DMA(()),
        ],
        compiler_params=pltpu.CompilerParams(vmem_limit_bytes=8 * MIB),
        name="later",
    )(rows, cols, table)


def product_kernel(
    rows_ref, cols_ref, table_ref, extra_ref, out_ref, total_ref, slots, send_sems, recv_sems
):
    row, col, layer = (lax.axis_index(a) for a in ("row", "col", "layer"))
    peers = [((row + s) % 8, col, layer) for s in range(1, 8)]
    barrier = pltpu.get_barrier_semaphore()
    for peer in peers:
        pl.semaphore_signal(barrier, inc=1, device_id=peer, device_id_type=MESH)

    r_ref, c_ref = as_blocks(rows_ref), as_blocks(cols_ref)
    tiles, wide = out_ref.shape[0] // BLK, out_ref.shape[1] // BLK

    def one_row(i, sums):
        lines = pl.ds(pl.multiple_of(i * BLK, BLK), BLK)
        out = []
        for j in range(wide):
            cell = i * wide + j
            value = group_product(r_ref, c_ref, table_ref, cell, 0)
            has_more = jnp.full((BLK, BLK), table_ref[2 * DEPTH, cell], jnp.int32) > GROUP
            value = value + jnp.where(has_more, extra_ref[cell], 0.0)
            value = value * value
            out_ref[lines, pl.ds(j * BLK, BLK)] = value
            out.append(sums[j] + jnp.sum(value.reshape(BLK // 8, 8, BLK), axis=0))
        return tuple(out)

    sums = tuple(jnp.zeros((8, BLK), jnp.float32) for _ in range(wide))
    sums = lax.fori_loop(0, tiles, one_row, sums, unroll=3)
    slots[row] = jnp.concatenate([jnp.sum(v, axis=0, keepdims=True) for v in sums], 1)
    pl.semaphore_wait(barrier, 7)
    copies = [
        pltpu.make_async_remote_copy(
            src_ref=slots.at[row],
            dst_ref=slots.at[row],
            send_sem=send_sems.at[k],
            recv_sem=recv_sems.at[k],
            device_id=peer,
            device_id_type=MESH,
        )
        for k, peer in enumerate(peers)
    ]
    for copy in copies:
        copy.start()
    for copy in copies:
        copy.wait()
    total = slots[0]
    for q in range(1, 8):
        total = total + slots[q]
    total_ref[...] = total


def product(rows, cols, table, extra, shape):
    lanes = shape[1]
    return pl.pallas_call(
        product_kernel,
        out_shape=[pltpu.VMEM(shape, jnp.float32), pltpu.VMEM((1, lanes), jnp.float32)],
        in_specs=[VMEM, VMEM, SMEM, VMEM],
        out_specs=[VMEM, VMEM],
        scratch_shapes=[
            pltpu.VMEM((8, 1, lanes), jnp.float32),
            pltpu.SemaphoreType.DMA((7,)),
            pltpu.SemaphoreType.DMA((7,)),
        ],
        compiler_params=pltpu.CompilerParams(
            collective_id=1, has_side_effects=True, vmem_limit_bytes=8 * MIB
        ),
        name="product",
    )(rows, cols, table, extra)


STEPS = 6


def scale_kernel(scaling, value_ref, total_ref, out_ref, staged, sems):
    step = staged.shape[1]
    factor = scaling / total_ref[...]
    copies = []
    for t in range(STEPS):
        here = pl.ds(t * step, step)
        staged[t] = value_ref[here, :] * factor
        copy = pltpu.make_async_copy(staged.at[t], out_ref.at[here], sems.at[t])
        copy.start()
        copies.append(copy)
    for copy in copies:
        copy.wait()


def scale(value, total, scaling):
    rows, lanes = value.shape
    return pl.pallas_call(
        functools.partial(scale_kernel, scaling),
        out_shape=jax.ShapeDtypeStruct(value.shape, jnp.float32),
        in_specs=[pl.BlockSpec(memory_space=pltpu.VMEM)] * 2,
        out_specs=pl.BlockSpec(memory_space=pltpu.HBM),
        scratch_shapes=[
            pltpu.VMEM((STEPS, rows // STEPS, lanes), jnp.float32),
            pltpu.SemaphoreType.DMA((STEPS,)),
        ],
        compiler_params=pltpu.CompilerParams(vmem_limit_bytes=16 * MIB),
        name="scale",
    )(value, total)


def body(similarity, block_mask):
    rows, cols, table = gather(block_mask, similarity)
    extra = later(rows, cols, table, block_mask.size)
    value, total = product(rows, cols, table, extra, similarity.shape)
    scaling = similarity.shape[0] * lax.axis_size("row")
    return scale(value, total, float(scaling))


def solution(mesh):
    return jax.shard_map(
        body,
        mesh=mesh,
        in_specs=(P("row", ("col", "layer")), P("row", ("col", "layer"))),
        out_specs=P("row", ("col", "layer")),
        check_vma=False,
    )
```

```python
import functools

import jax
import jax.numpy as jnp
from jax import lax
from jax.experimental import pallas as pl
from jax.experimental.pallas import tpu as pltpu
from jax.sharding import PartitionSpec as P

BLK = 128
MAXNZ = 18
HEAD = 32
HALF = MAXNZ // 2
SLOTS = MAXNZ + 1
SHARE = SLOTS * BLK
TOP = BLK - HEAD
GROUP = 4
DEPTH = 16
FIELD = 256
COUNT = 512 * FIELD
MIB = 1 << 20
MESH = pl.DeviceIdType.MESH


def pack_share(mask_ref, x_ref, mask_s, x_v, share, place_v, place_s, signal, sems):
    cols, rows = mask_ref.shape
    fetch = pltpu.make_async_copy(mask_ref, mask_s, sems.at[cols + 1])
    fetch.start()
    strips = x_v.reshape(cols * rows * BLK, BLK)
    loads = [
        pltpu.make_async_copy(
            x_ref.at[:, pl.ds(j * BLK, BLK)],
            strips.at[pl.ds(j * rows * BLK, rows * BLK)],
            sems.at[j],
        )
        for j in range(cols)
    ]
    for load in loads:
        load.start()
    signal()
    sub = lax.broadcasted_iota(jnp.int32, (HEAD, BLK), 0)
    lane = lax.broadcasted_iota(jnp.int32, (HEAD, BLK), 1)
    lane_row = (lane * 43) >> 8
    lane_col = lane - lane_row * cols
    lane8 = lane[:8]

    def find(i, carry):
        count, place = carry
        for j in range(cols):
            here = mask_s[j, i]
            place = place + jnp.where(lane8 == count, here * (j * rows + i), 0)
            count = count + here
        return count, place

    fetch.wait()
    zero = jnp.int32(0)
    _, place = lax.fori_loop(0, rows, find, (zero, jnp.zeros((8, BLK), jnp.int32)), unroll=3)
    place_v[...] = place
    move = pltpu.make_async_copy(place_v, place_s, sems.at[cols])
    move.start()

    def mark(i, carry):
        count, head = carry
        below = 8 + jnp.where(i < cols, i, i - cols + 8)
        for j in range(cols):
            here = mask_s[j, i]
            cell = ((sub == j) & (lane_row == i)) | ((sub == below) & (lane_col == j))
            head = head + jnp.where(cell, here * (count + 1), 0)
            count = count + here
        return count, head

    _, head = lax.fori_loop(0, rows, mark, (zero, jnp.zeros((HEAD, BLK), jnp.int32)))
    head = jnp.where(lane < rows * cols, head, 0)
    share[pl.ds(TOP, HEAD), :] = head.astype(jnp.float32).astype(share.dtype)
    move.wait()
    for load in loads:
        load.wait()
    for s in range(MAXNZ):
        share[pl.ds((s + 1) * BLK, BLK), :] = x_v[place_s[0, s]]


def pair_lists(rows_ref, cols_ref):
    hr, hc = [], []
    for q in range(16):
        hr.append(rows_ref[q, pl.ds(TOP, HEAD), :].astype(jnp.float32)[0:8])
    for q in range(8):
        top = cols_ref[q, pl.ds(TOP, HEAD), :].astype(jnp.float32)
        hc += [top[8:16], top[16:24]]
    hr, hc = jnp.concatenate(hr, 0), jnp.concatenate(hc, 0)
    both = jnp.where((hr > 0) & (hc > 0), 1.0, 0.0)
    line = lax.broadcasted_iota(jnp.int32, (BLK, BLK), 0)
    before = line > lax.broadcasted_iota(jnp.int32, (BLK, BLK), 1)
    rank = jnp.dot(
        jnp.where(before, 1.0, 0.0).astype(jnp.bfloat16),
        both.astype(jnp.bfloat16),
        preferred_element_type=jnp.float32,
    )
    rank = jnp.where(both > 0, rank, -1.0).astype(jnp.int32)
    place_r = (line >> 3) * SLOTS + hr.astype(jnp.int32)
    place_c = (line >> 4) * SLOTS + hc.astype(jnp.int32)
    count = jnp.sum(both, axis=0, keepdims=True).astype(jnp.int32)
    return rank, place_r * FIELD + place_c, count


def write_lists(table_v, lists, done):
    rank, place, count = lists
    most = jnp.max(count, axis=1, keepdims=True)
    lane = lax.broadcasted_iota(jnp.int32, count.shape, 1)
    for p in range(DEPTH):
        one = jnp.sum(jnp.where(rank == done + p, place, 0), axis=0, keepdims=True)
        one = jnp.where(count > done + p, one, IDLE)
        if p == 0:
            length = jnp.where(lane == BLK - 1, most, jnp.maximum(count - done, 0))
            one = one + COUNT * length
        table_v[pl.ds(p, 1), :] = one


IDLE = 16 * SLOTS * FIELD + 1


def length_of(table, cell):
    return table[0, cell] >> 17


LAST = 5
SPLIT = 7


def span(first, last):
    low = (first + 1) * BLK if first else TOP
    return pl.ds(low, (last + 1) * BLK - low)


def gather_kernel(
    mask_ref,
    x_ref,
    rows_ref,
    cols_ref,
    table_ref,
    mask_s,
    x_v,
    share_ref,
    relay,
    place_v,
    place_s,
    send_sems,
    recv_sems,
    own_sems,
    pack_sems,
    table_v,
):
    row, col, layer = (lax.axis_index(a) for a in ("row", "col", "layer"))
    high, x = row // 4, row % 4
    z, low = col // 2, col % 2

    def along_z(step):
        return 2 * ((z + step) % 4) + low

    def along_x(step):
        return 4 * high + (x + step) % 4

    mate = 2 * z + 1 - low
    far = 4 * (1 - high) + x

    zp, zm = (row, along_z(1), layer), (row, along_z(3), layer)
    xp, xm = (along_x(1), col, layer), (along_x(3), col, layer)
    lo, hi = (row, mate, layer), (far, mate, layer)
    sib = (row, col, 1 - layer)

    barrier = pltpu.get_barrier_semaphore()

    def signal():
        for peer in (zp, zm, xp, xm, lo, hi, sib):
            pl.semaphore_signal(barrier, inc=1, device_id=peer, device_id_type=MESH)

    pack_share(mask_ref, x_ref, mask_s, x_v, share_ref, place_v, place_s, signal, pack_sems)
    pl.semaphore_wait(barrier, 7)

    ALL = span(0, MAXNZ)
    mine = 2 * col + layer
    keep = [
        pltpu.make_async_copy(share_ref.at[ALL], rows_ref.at[mine].at[ALL], own_sems.at[0]),
        pltpu.make_async_copy(share_ref.at[ALL], cols_ref.at[row].at[ALL], own_sems.at[1]),
    ]

    EARLY = MAXNZ - LAST
    H1, H2 = span(0, HALF), span(HALF, MAXNZ)
    U1, U2, L = span(0, SPLIT), span(SPLIT, EARLY), span(EARLY, MAXNZ)
    V1, V2, V3, V4 = span(0, 4), span(4, SPLIT), span(SPLIT, 10), span(10, EARLY)
    T = pl.ds(0, LAST * BLK)
    started = []
    waited = set()

    def send(src, dst, part, peer, into=None):
        k = len(started)
        copy = pltpu.make_async_remote_copy(
            src_ref=src.at[part],
            dst_ref=dst.at[part if into is None else into],
            send_sem=send_sems.at[k],
            recv_sem=recv_sems.at[k],
            device_id=peer,
            device_id_type=MESH,
        )
        copy.start()
        started.append(copy)
        return k

    def arrived(k, dst, part, peer):
        waited.add(k)
        pltpu.make_async_remote_copy(
            src_ref=dst.at[part],
            dst_ref=dst.at[part],
            send_sem=send_sems.at[k],
            recv_sem=recv_sems.at[k],
            device_id=peer,
            device_id_type=MESH,
        ).wait_recv()

    def other(q):
        return q + 1 - 2 * (q % 2)

    def r(q):
        return rows_ref.at[2 * q + layer]

    def rsib(q):
        return rows_ref.at[2 * q + 1 - layer]

    def c(q):
        return cols_ref.at[q]

    def across(q):
        return c((q + 4) % 8)

    own_r, own_c = r(col), c(row)
    y_r, y_c = r(mate), c(far)
    zm_r, zp_r, zz_r = (r(along_z(s)) for s in (3, 1, 2))
    ym_r, yp_r, yy_r = (r(other(along_z(s))) for s in (3, 1, 2))
    xm_c, xp_c, xx_c = (c(along_x(s)) for s in (3, 1, 2))
    ym_c, yp_c, yy_c = (across(along_x(s)) for s in (3, 1, 2))

    lo1 = send(share_ref, own_r, U1, lo)
    zp1 = send(share_ref, own_r, H1, zp)
    zm2 = send(share_ref, own_r, H2, zm)
    xp1 = send(share_ref, own_c, H1, xp)
    xm2 = send(share_ref, own_c, H2, xm)
    lo2 = send(share_ref, own_r, U2, lo)
    zp2 = send(share_ref, own_r, H2, zp)
    zm1 = send(share_ref, own_r, H1, zm)
    xp2 = send(share_ref, own_c, H2, xp)
    xm1 = send(share_ref, own_c, H1, xm)
    lo3 = send(share_ref, own_r, L, lo)
    sb0 = send(share_ref, own_r, ALL, sib)
    for copy in keep:
        copy.start()
    rows_ref[16, pl.ds(0, BLK), :] = jnp.zeros((BLK, BLK), rows_ref.dtype)

    arrived(lo1, y_r, U1, lo)
    hi1 = send(y_r, own_c, U1, hi)
    yzp1 = send(y_r, y_r, U1, zp)
    arrived(zp1, zm_r, H1, zm)
    fzp = send(zm_r, zm_r, H1, zp)
    arrived(zm2, zp_r, H2, zp)
    fzm = send(zp_r, zp_r, H2, zm)
    arrived(xp1, xm_c, H1, xm)
    fxp = send(xm_c, xm_c, H1, xp)
    arrived(xm2, xp_c, H2, xp)
    fxm = send(xp_c, xp_c, H2, xm)
    txp = send(xp_c, relay.at[0], L, lo, T)
    lzp = send(zp_r, zp_r, L, lo)
    arrived(lo2, y_r, U2, lo)
    hi2 = send(y_r, own_c, U2, hi)
    yzm2 = send(y_r, y_r, U2, zm)
    yzp2 = send(y_r, y_r, U2, zp)
    yzm1 = send(y_r, y_r, U1, zm)
    arrived(hi1, y_c, U1, hi)
    yxp1 = send(y_c, y_c, U1, xp)
    arrived(lo3, y_r, L, lo)
    hi3 = send(y_r, own_c, L, hi)
    sb1 = send(y_r, y_r, ALL, sib)

    arrived(zp2, zm_r, H2, zm)
    arrived(xp2, xm_c, H2, xm)
    txm = send(xm_c, relay.at[1], L, lo, T)
    lzm = send(zm_r, zm_r, L, lo)
    sb2 = send(zm_r, zm_r, ALL, sib)
    arrived(zm1, zp_r, H1, zp)
    sb3 = send(zp_r, zp_r, ALL, sib)
    arrived(hi2, y_c, U2, hi)
    yxm2 = send(y_c, y_c, U2, xm)
    yxp2 = send(y_c, y_c, U2, xp)
    yxm1 = send(y_c, y_c, U1, xm)
    arrived(txp, relay.at[0], T, lo)
    uxp = send(relay.at[0], xp_c, T, hi, L)
    arrived(fxm, xx_c, H2, xp)
    txx = send(xx_c, relay.at[2], L, lo, T)
    arrived(fzm, zz_r, H2, zp)
    lzz = send(zz_r, zz_r, L, lo)
    arrived(fzp, zz_r, H1, zm)
    sb4 = send(zz_r, zz_r, ALL, sib)
    arrived(txm, relay.at[1], T, lo)
    uxm = send(relay.at[1], xm_c, T, hi, L)

    arrived(yzp1, ym_r, U1, zm)
    gzp = send(ym_r, ym_r, V1, zp)
    gzq = send(ym_r, ym_r, V2, zp)
    arrived(yzm2, yp_r, U2, zp)
    gzm = send(yp_r, yp_r, V3, zm)
    gzn = send(yp_r, yp_r, V4, zm)
    arrived(yxp1, ym_c, U1, xm)
    gxp = send(ym_c, ym_c, V1, xp)
    gxq = send(ym_c, ym_c, V2, xp)
    arrived(yxm2, yp_c, U2, xp)
    gxm = send(yp_c, yp_c, U2, xm)
    sb5 = send(ym_r, ym_r, U1, sib)
    sb6 = send(yp_r, yp_r, U2, sib)
    arrived(lzp, yp_r, L, lo)
    sb12 = send(yp_r, yp_r, L, sib)
    arrived(lzm, ym_r, L, lo)
    sb13 = send(ym_r, ym_r, L, sib)
    arrived(txx, relay.at[2], T, lo)
    uxx = send(relay.at[2], xx_c, T, hi, L)
    arrived(yzm1, yp_r, U1, zp)
    sb14 = send(yp_r, yp_r, U1, sib)
    arrived(yzp2, ym_r, U2, zm)
    sb15 = send(ym_r, ym_r, U2, sib)
    arrived(lzz, yy_r, L, lo)
    sb7 = send(yy_r, yy_r, L, sib)
    for copy in keep:
        copy.wait()
    arrived(xm1, xp_c, H1, xp)
    arrived(fxp, xx_c, H1, xm)
    arrived(yxm1, yp_c, U1, xp)
    arrived(sb0, rsib(col), ALL, sib)
    arrived(sb1, rsib(mate), ALL, sib)
    arrived(sb2, rsib(along_z(3)), ALL, sib)
    arrived(sb3, rsib(along_z(1)), ALL, sib)
    arrived(gzp, yy_r, V1, zm)
    sb8 = send(yy_r, yy_r, V1, sib)
    arrived(gzm, yy_r, V3, zp)
    sb9 = send(yy_r, yy_r, V3, sib)
    arrived(gxp, yy_c, V1, xm)
    arrived(sb4, rsib(along_z(2)), ALL, sib)
    arrived(sb5, rsib(other(along_z(3))), U1, sib)
    arrived(sb14, rsib(other(along_z(1))), U1, sib)
    arrived(sb8, rsib(other(along_z(2))), V1, sib)
    write_lists(table_v, pair_lists(rows_ref, cols_ref), 0)
    hand = pltpu.make_async_copy(table_v, table_ref, own_sems.at[2])
    hand.start()
    arrived(gzn, yy_r, V4, zp)
    sb10 = send(yy_r, yy_r, V4, sib)
    arrived(gzq, yy_r, V2, zm)
    sb11 = send(yy_r, yy_r, V2, sib)

    arrived(hi3, y_c, L, hi)
    arrived(yxp2, ym_c, U2, xm)
    arrived(uxp, yp_c, L, hi)
    arrived(uxm, ym_c, L, hi)
    arrived(uxx, yy_c, L, hi)
    arrived(gxm, yy_c, U2, xp)
    arrived(gxq, yy_c, V2, xm)
    arrived(sb6, rsib(other(along_z(1))), U2, sib)
    arrived(sb12, rsib(other(along_z(1))), L, sib)
    arrived(sb13, rsib(other(along_z(3))), L, sib)
    arrived(sb15, rsib(other(along_z(3))), U2, sib)
    arrived(sb7, rsib(other(along_z(2))), L, sib)
    arrived(sb9, rsib(other(along_z(2))), V3, sib)
    arrived(sb10, rsib(other(along_z(2))), V4, sib)
    arrived(sb11, rsib(other(along_z(2))), V2, sib)
    assert waited == set(range(len(started))) and len(started) == COPIES
    for copy in started:
        copy.wait_send()
    hand.wait()


COPIES = 58


def gather(block_mask, similarity):
    dtype = similarity.dtype
    cells = block_mask.size
    return pl.pallas_call(
        gather_kernel,
        out_shape=[
            pltpu.VMEM((17, SHARE, BLK), dtype),
            pltpu.VMEM((8, SHARE, BLK), dtype),
            pltpu.SMEM((DEPTH, BLK), jnp.int32),
        ],
        in_specs=[pl.BlockSpec(memory_space=pltpu.HBM)] * 2,
        out_specs=[
            pl.BlockSpec(memory_space=pltpu.VMEM),
            pl.BlockSpec(memory_space=pltpu.VMEM),
            pl.BlockSpec(memory_space=pltpu.SMEM),
        ],
        scratch_shapes=[
            pltpu.SMEM(block_mask.shape[::-1], jnp.int32),
            pltpu.VMEM((cells, BLK, BLK), dtype),
            pltpu.VMEM((SHARE, BLK), dtype),
            pltpu.VMEM((3, LAST * BLK, BLK), dtype),
            pltpu.VMEM((8, BLK), jnp.int32),
            pltpu.SMEM((8, BLK), jnp.int32),
            pltpu.SemaphoreType.DMA((COPIES,)),
            pltpu.SemaphoreType.DMA((COPIES,)),
            pltpu.SemaphoreType.DMA((3,)),
            pltpu.SemaphoreType.DMA((8,)),
            pltpu.VMEM((DEPTH, BLK), jnp.int32),
        ],
        compiler_params=pltpu.CompilerParams(
            collective_id=0, has_side_effects=True, vmem_limit_bytes=44 * MIB
        ),
        name="gather",
    )(block_mask.T, similarity)


def group_product(r_ref, c_ref, table, cell, g):
    words = [table[g * GROUP + t, cell] for t in range(GROUP)]
    return sum(
        jnp.dot(
            r_ref[(word >> 8) & 511],
            c_ref[word & 255],
            preferred_element_type=jnp.float32,
        )
        for word in words
    )


def as_blocks(ref):
    return ref.reshape(ref.shape[0] * SLOTS, BLK, BLK)


AT_ONCE = 4


def later_kernel(rows_ref, cols_ref, table_ref, extra_ref, table_v, table_s, list_s, sem):
    r_ref, c_ref = as_blocks(rows_ref), as_blocks(cols_ref)
    cells = extra_ref.shape[0] - 1

    def look(cell, found):
        list_s[found] = cell
        return found + jnp.where(length_of(table_ref, cell) > GROUP, 1, 0)

    found = lax.fori_loop(0, cells, look, jnp.int32(0), unroll=8)
    for t in range(AT_ONCE):
        list_s[found + t] = cells

    @pl.loop(0, (found + AT_ONCE - 1) // AT_ONCE)
    def _(n):
        for t in range(AT_ONCE):
            cell = list_s[n * AT_ONCE + t]
            extra_ref[cell] = group_product(r_ref, c_ref, table_ref, cell, 1)

    def add(table, cell, first):
        @pl.loop(first, (jnp.minimum(length_of(table, cell), DEPTH) + GROUP - 1) // GROUP)
        def _(g):
            extra_ref[cell] += group_product(r_ref, c_ref, table, cell, g)

    most = length_of(table_ref, BLK - 1)

    @pl.when(most > 2 * GROUP)
    def _():
        @pl.loop(0, found)
        def _(n):
            add(table_ref, list_s[n], 2)

    @pl.loop(1, (most + DEPTH - 1) // DEPTH)
    def _(d):
        write_lists(table_v, pair_lists(rows_ref, cols_ref), d * DEPTH)
        copy = pltpu.make_async_copy(table_v, table_s, sem)
        copy.start()
        copy.wait()

        @pl.loop(0, found)
        def _(n):
            add(table_s, list_s[n], 0)


VMEM, SMEM = pl.BlockSpec(memory_space=pltpu.VMEM), pl.BlockSpec(memory_space=pltpu.SMEM)


def later(rows, cols, table, cells):
    return pl.pallas_call(
        later_kernel,
        out_shape=pltpu.VMEM((cells + 1, BLK, BLK), jnp.float32),
        in_specs=[VMEM, VMEM, SMEM],
        out_specs=VMEM,
        scratch_shapes=[
            pltpu.VMEM(table.shape, jnp.int32),
            pltpu.SMEM(table.shape, jnp.int32),
            pltpu.SMEM((BLK,), jnp.int32),
            pltpu.SemaphoreType.DMA(()),
        ],
        compiler_params=pltpu.CompilerParams(vmem_limit_bytes=8 * MIB),
        name="later",
    )(rows, cols, table)


def product_kernel(
    rows_ref, cols_ref, table_ref, extra_ref, out_ref, total_ref, slots, send_sems, recv_sems
):
    row, col, layer = (lax.axis_index(a) for a in ("row", "col", "layer"))
    peers = [((row + s) % 8, col, layer) for s in range(1, 8)]
    barrier = pltpu.get_barrier_semaphore()
    for peer in peers:
        pl.semaphore_signal(barrier, inc=1, device_id=peer, device_id_type=MESH)

    r_ref, c_ref = as_blocks(rows_ref), as_blocks(cols_ref)
    tiles, wide = out_ref.shape[0] // BLK, out_ref.shape[1] // BLK

    def one_row(i, sums):
        lines = pl.ds(pl.multiple_of(i * BLK, BLK), BLK)
        out = []
        for j in range(wide):
            cell = i * wide + j
            value = group_product(r_ref, c_ref, table_ref, cell, 0)
            has_more = jnp.full((BLK, BLK), length_of(table_ref, cell), jnp.int32) > GROUP
            value = value + jnp.where(has_more, extra_ref[cell], 0.0)
            value = value * value
            out_ref[lines, pl.ds(j * BLK, BLK)] = value
            out.append(sums[j] + jnp.sum(value.reshape(BLK // 8, 8, BLK), axis=0))
        return tuple(out)

    sums = tuple(jnp.zeros((8, BLK), jnp.float32) for _ in range(wide))
    sums = lax.fori_loop(0, tiles, one_row, sums, unroll=6)
    slots[row] = jnp.concatenate([jnp.sum(v, axis=0, keepdims=True) for v in sums], 1)
    pl.semaphore_wait(barrier, 7)
    copies = [
        pltpu.make_async_remote_copy(
            src_ref=slots.at[row],
            dst_ref=slots.at[row],
            send_sem=send_sems.at[k],
            recv_sem=recv_sems.at[k],
            device_id=peer,
            device_id_type=MESH,
        )
        for k, peer in enumerate(peers)
    ]
    for copy in copies:
        copy.start()
    for copy in copies:
        copy.wait()
    total = slots[0]
    for q in range(1, 8):
        total = total + slots[q]
    total_ref[...] = total


def product(rows, cols, table, extra, shape):
    lanes = shape[1]
    return pl.pallas_call(
        product_kernel,
        out_shape=[pltpu.VMEM(shape, jnp.float32), pltpu.VMEM((1, lanes), jnp.float32)],
        in_specs=[VMEM, VMEM, SMEM, VMEM],
        out_specs=[VMEM, VMEM],
        scratch_shapes=[
            pltpu.VMEM((8, 1, lanes), jnp.float32),
            pltpu.SemaphoreType.DMA((7,)),
            pltpu.SemaphoreType.DMA((7,)),
        ],
        compiler_params=pltpu.CompilerParams(
            collective_id=1, has_side_effects=True, vmem_limit_bytes=8 * MIB
        ),
        name="product",
    )(rows, cols, table, extra)


STEPS = 6


def scale_kernel(scaling, value_ref, total_ref, out_ref, staged, sems):
    step = staged.shape[1]
    factor = scaling / total_ref[...]
    copies = []
    for t in range(STEPS):
        here = pl.ds(t * step, step)
        staged[t] = value_ref[here, :] * factor
        copy = pltpu.make_async_copy(staged.at[t], out_ref.at[here], sems.at[t])
        copy.start()
        copies.append(copy)
    for copy in copies:
        copy.wait()


def scale(value, total, scaling):
    rows, lanes = value.shape
    return pl.pallas_call(
        functools.partial(scale_kernel, scaling),
        out_shape=jax.ShapeDtypeStruct(value.shape, jnp.float32),
        in_specs=[pl.BlockSpec(memory_space=pltpu.VMEM)] * 2,
        out_specs=pl.BlockSpec(memory_space=pltpu.HBM),
        scratch_shapes=[
            pltpu.VMEM((STEPS, rows // STEPS, lanes), jnp.float32),
            pltpu.SemaphoreType.DMA((STEPS,)),
        ],
        compiler_params=pltpu.CompilerParams(vmem_limit_bytes=16 * MIB),
        name="scale",
    )(value, total)


def body(similarity, block_mask):
    rows, cols, table = gather(block_mask, similarity)
    extra = later(rows, cols, table, block_mask.size)
    value, total = product(rows, cols, table, extra, similarity.shape)
    scaling = similarity.shape[0] * lax.axis_size("row")
    return scale(value, total, float(scaling))


def solution(mesh):
    return jax.shard_map(
        body,
        mesh=mesh,
        in_specs=(P("row", ("col", "layer")), P("row", ("col", "layer"))),
        out_specs=P("row", ("col", "layer")),
        check_vma=False,
    )
```

```python
import functools

import jax
import jax.numpy as jnp
from jax import lax
from jax.experimental import pallas as pl
from jax.experimental.pallas import tpu as pltpu
from jax.sharding import PartitionSpec as P

BLK = 128
MAXNZ = 18
HEAD = 32
HALF = MAXNZ // 2
SLOTS = MAXNZ + 1
SHARE = SLOTS * BLK
TOP = BLK - HEAD
GROUP = 4
DEPTH = 16
FIELD = 256
COUNT = 512 * FIELD
MIB = 1 << 20
MESH = pl.DeviceIdType.MESH


def pack_share(mask_ref, x_ref, mask_s, x_v, share, place_v, place_s, signal, sems):
    cols, rows = mask_ref.shape
    fetch = pltpu.make_async_copy(mask_ref, mask_s, sems.at[cols + 1])
    fetch.start()
    strips = x_v.reshape(cols * rows * BLK, BLK)
    loads = [
        pltpu.make_async_copy(
            x_ref.at[:, pl.ds(j * BLK, BLK)],
            strips.at[pl.ds(j * rows * BLK, rows * BLK)],
            sems.at[j],
        )
        for j in range(cols)
    ]
    for load in loads:
        load.start()
    signal()
    sub = lax.broadcasted_iota(jnp.int32, (HEAD, BLK), 0)
    lane = lax.broadcasted_iota(jnp.int32, (HEAD, BLK), 1)
    lane_row = (lane * 43) >> 8
    lane_col = lane - lane_row * cols
    lane8 = lane[:8]

    def find(i, carry):
        count, place = carry
        for j in range(cols):
            here = mask_s[j, i]
            place = place + jnp.where(lane8 == count, here * (j * rows + i), 0)
            count = count + here
        return count, place

    fetch.wait()
    zero = jnp.int32(0)
    _, place = lax.fori_loop(0, rows, find, (zero, jnp.zeros((8, BLK), jnp.int32)), unroll=3)
    place_v[...] = place
    move = pltpu.make_async_copy(place_v, place_s, sems.at[cols])
    move.start()

    def mark(i, carry):
        count, head = carry
        below = 8 + jnp.where(i < cols, i, i - cols + 8)
        for j in range(cols):
            here = mask_s[j, i]
            cell = ((sub == j) & (lane_row == i)) | ((sub == below) & (lane_col == j))
            head = head + jnp.where(cell, here * (count + 1), 0)
            count = count + here
        return count, head

    _, head = lax.fori_loop(0, rows, mark, (zero, jnp.zeros((HEAD, BLK), jnp.int32)))
    head = jnp.where(lane < rows * cols, head, 0)
    share[pl.ds(TOP, HEAD), :] = head.astype(jnp.float32).astype(share.dtype)
    move.wait()
    for load in loads:
        load.wait()
    for s in range(MAXNZ):
        share[pl.ds((s + 1) * BLK, BLK), :] = x_v[place_s[0, s]]


def pair_lists(rows_ref, cols_ref):
    hr, hc = [], []
    for q in range(16):
        hr.append(rows_ref[q, pl.ds(TOP, HEAD), :].astype(jnp.float32)[0:8])
    for q in range(8):
        top = cols_ref[q, pl.ds(TOP, HEAD), :].astype(jnp.float32)
        hc += [top[8:16], top[16:24]]
    hr, hc = jnp.concatenate(hr, 0), jnp.concatenate(hc, 0)
    both = jnp.where((hr > 0) & (hc > 0), 1.0, 0.0)
    line = lax.broadcasted_iota(jnp.int32, (BLK, BLK), 0)
    before = line > lax.broadcasted_iota(jnp.int32, (BLK, BLK), 1)
    rank = jnp.dot(
        jnp.where(before, 1.0, 0.0).astype(jnp.bfloat16),
        both.astype(jnp.bfloat16),
        preferred_element_type=jnp.float32,
    )
    rank = jnp.where(both > 0, rank, -1.0).astype(jnp.int32)
    place_r = (line >> 3) * SLOTS + hr.astype(jnp.int32)
    place_c = (line >> 4) * SLOTS + hc.astype(jnp.int32)
    count = jnp.sum(both, axis=0, keepdims=True).astype(jnp.int32)
    return rank, place_r * FIELD + place_c, count


def write_lists(table_v, lists, done):
    rank, place, count = lists
    most = jnp.max(count, axis=1, keepdims=True)
    lane = lax.broadcasted_iota(jnp.int32, count.shape, 1)
    for p in range(DEPTH):
        one = jnp.sum(jnp.where(rank == done + p, place, 0), axis=0, keepdims=True)
        one = jnp.where(count > done + p, one, IDLE)
        if p == 0:
            length = jnp.where(lane == BLK - 1, most, jnp.maximum(count - done, 0))
            one = one + COUNT * length
        table_v[pl.ds(p, 1), :] = one


IDLE = 16 * SLOTS * FIELD + 1


def length_of(table, cell):
    return table[0, cell] >> 17


LAST_R = 5
LAST_C = 4
SPLIT = 7


def span(first, last):
    low = (first + 1) * BLK if first else TOP
    return pl.ds(low, (last + 1) * BLK - low)


def gather_kernel(
    mask_ref,
    x_ref,
    rows_ref,
    cols_ref,
    table_ref,
    mask_s,
    x_v,
    share_ref,
    relay,
    place_v,
    place_s,
    send_sems,
    recv_sems,
    own_sems,
    pack_sems,
    table_v,
):
    row, col, layer = (lax.axis_index(a) for a in ("row", "col", "layer"))
    high, x = row // 4, row % 4
    z, low = col // 2, col % 2

    def along_z(step):
        return 2 * ((z + step) % 4) + low

    def along_x(step):
        return 4 * high + (x + step) % 4

    mate = 2 * z + 1 - low
    far = 4 * (1 - high) + x

    zp, zm = (row, along_z(1), layer), (row, along_z(3), layer)
    xp, xm = (along_x(1), col, layer), (along_x(3), col, layer)
    lo, hi = (row, mate, layer), (far, mate, layer)
    sib = (row, col, 1 - layer)

    barrier = pltpu.get_barrier_semaphore()

    def signal():
        for peer in (zp, zm, xp, xm, lo, hi, sib):
            pl.semaphore_signal(barrier, inc=1, device_id=peer, device_id_type=MESH)

    pack_share(mask_ref, x_ref, mask_s, x_v, share_ref, place_v, place_s, signal, pack_sems)
    pl.semaphore_wait(barrier, 7)

    ALL = span(0, MAXNZ)
    mine = 2 * col + layer
    keep = [
        pltpu.make_async_copy(share_ref.at[ALL], rows_ref.at[mine].at[ALL], own_sems.at[0]),
        pltpu.make_async_copy(share_ref.at[ALL], cols_ref.at[row].at[ALL], own_sems.at[1]),
    ]

    EARLY, EARLY_C = MAXNZ - LAST_R, MAXNZ - LAST_C
    H1, H2 = span(0, HALF), span(HALF, MAXNZ)
    U1, U2, L = span(0, SPLIT), span(SPLIT, EARLY), span(EARLY, MAXNZ)
    V1, V2, V3, V4 = span(0, 4), span(4, SPLIT), span(SPLIT, 10), span(10, EARLY)
    W2, K = span(SPLIT, EARLY_C), span(EARLY_C, MAXNZ)
    T = pl.ds(0, LAST_C * BLK)
    started = []
    waited = set()

    def send(src, dst, part, peer, into=None):
        k = len(started)
        copy = pltpu.make_async_remote_copy(
            src_ref=src.at[part],
            dst_ref=dst.at[part if into is None else into],
            send_sem=send_sems.at[k],
            recv_sem=recv_sems.at[k],
            device_id=peer,
            device_id_type=MESH,
        )
        copy.start()
        started.append(copy)
        return k

    def arrived(k, dst, part, peer):
        waited.add(k)
        pltpu.make_async_remote_copy(
            src_ref=dst.at[part],
            dst_ref=dst.at[part],
            send_sem=send_sems.at[k],
            recv_sem=recv_sems.at[k],
            device_id=peer,
            device_id_type=MESH,
        ).wait_recv()

    def other(q):
        return q + 1 - 2 * (q % 2)

    def r(q):
        return rows_ref.at[2 * q + layer]

    def rsib(q):
        return rows_ref.at[2 * q + 1 - layer]

    def c(q):
        return cols_ref.at[q]

    def across(q):
        return c((q + 4) % 8)

    own_r, own_c = r(col), c(row)
    y_r, y_c = r(mate), c(far)
    zm_r, zp_r, zz_r = (r(along_z(s)) for s in (3, 1, 2))
    ym_r, yp_r, yy_r = (r(other(along_z(s))) for s in (3, 1, 2))
    xm_c, xp_c, xx_c = (c(along_x(s)) for s in (3, 1, 2))
    ym_c, yp_c, yy_c = (across(along_x(s)) for s in (3, 1, 2))

    lo1 = send(share_ref, own_r, U1, lo)
    zp1 = send(share_ref, own_r, H1, zp)
    zm2 = send(share_ref, own_r, H2, zm)
    xp1 = send(share_ref, own_c, H1, xp)
    xm2 = send(share_ref, own_c, H2, xm)
    lo2 = send(share_ref, own_r, U2, lo)
    zp2 = send(share_ref, own_r, H2, zp)
    zm1 = send(share_ref, own_r, H1, zm)
    xp2 = send(share_ref, own_c, H2, xp)
    xm1 = send(share_ref, own_c, H1, xm)
    lo3 = send(share_ref, own_r, L, lo)
    sb0 = send(share_ref, own_r, ALL, sib)
    for copy in keep:
        copy.start()
    rows_ref[16, pl.ds(0, BLK), :] = jnp.zeros((BLK, BLK), rows_ref.dtype)

    arrived(lo1, y_r, U1, lo)
    hi1 = send(y_r, own_c, U1, hi)
    yzp1 = send(y_r, y_r, U1, zp)
    arrived(zp1, zm_r, H1, zm)
    fzp = send(zm_r, zm_r, H1, zp)
    arrived(zm2, zp_r, H2, zp)
    fzm = send(zp_r, zp_r, H2, zm)
    arrived(xp1, xm_c, H1, xm)
    fxp = send(xm_c, xm_c, H1, xp)
    arrived(xm2, xp_c, H2, xp)
    fxm = send(xp_c, xp_c, H2, xm)
    txp = send(xp_c, relay.at[0], K, lo, T)
    lzp = send(zp_r, zp_r, L, lo)
    arrived(lo2, y_r, U2, lo)
    hi2 = send(y_r, own_c, U2, hi)
    yzm2 = send(y_r, y_r, U2, zm)
    yzp2 = send(y_r, y_r, U2, zp)
    yzm1 = send(y_r, y_r, U1, zm)
    arrived(hi1, y_c, U1, hi)
    yxp1 = send(y_c, y_c, U1, xp)
    arrived(lo3, y_r, L, lo)
    hi3 = send(y_r, own_c, L, hi)
    sb1 = send(y_r, y_r, ALL, sib)

    arrived(zp2, zm_r, H2, zm)
    arrived(xp2, xm_c, H2, xm)
    txm = send(xm_c, relay.at[1], K, lo, T)
    lzm = send(zm_r, zm_r, L, lo)
    sb2 = send(zm_r, zm_r, ALL, sib)
    arrived(zm1, zp_r, H1, zp)
    sb3 = send(zp_r, zp_r, ALL, sib)
    arrived(hi2, y_c, U2, hi)
    arrived(hi3, y_c, L, hi)
    yxm2 = send(y_c, y_c, W2, xm)
    yxp2 = send(y_c, y_c, W2, xp)
    yxm1 = send(y_c, y_c, U1, xm)
    arrived(txp, relay.at[0], T, lo)
    uxp = send(relay.at[0], xp_c, T, hi, K)
    arrived(fxm, xx_c, H2, xp)
    txx = send(xx_c, relay.at[2], K, lo, T)
    arrived(fzm, zz_r, H2, zp)
    lzz = send(zz_r, zz_r, L, lo)
    arrived(fzp, zz_r, H1, zm)
    sb4 = send(zz_r, zz_r, ALL, sib)
    arrived(txm, relay.at[1], T, lo)
    uxm = send(relay.at[1], xm_c, T, hi, K)

    arrived(yzp1, ym_r, U1, zm)
    gzp = send(ym_r, ym_r, V1, zp)
    gzq = send(ym_r, ym_r, V2, zp)
    arrived(yzm2, yp_r, U2, zp)
    gzm = send(yp_r, yp_r, V3, zm)
    gzn = send(yp_r, yp_r, V4, zm)
    arrived(yxp1, ym_c, U1, xm)
    gxp = send(ym_c, ym_c, V1, xp)
    gxq = send(ym_c, ym_c, V2, xp)
    arrived(yxm2, yp_c, W2, xp)
    gxm = send(yp_c, yp_c, W2, xm)
    sb5 = send(ym_r, ym_r, U1, sib)
    sb6 = send(yp_r, yp_r, U2, sib)
    arrived(lzp, yp_r, L, lo)
    sb12 = send(yp_r, yp_r, L, sib)
    arrived(lzm, ym_r, L, lo)
    sb13 = send(ym_r, ym_r, L, sib)
    arrived(txx, relay.at[2], T, lo)
    uxx = send(relay.at[2], xx_c, T, hi, K)
    arrived(yzm1, yp_r, U1, zp)
    sb14 = send(yp_r, yp_r, U1, sib)
    arrived(yzp2, ym_r, U2, zm)
    sb15 = send(ym_r, ym_r, U2, sib)
    arrived(lzz, yy_r, L, lo)
    sb7 = send(yy_r, yy_r, L, sib)
    for copy in keep:
        copy.wait()
    arrived(xm1, xp_c, H1, xp)
    arrived(fxp, xx_c, H1, xm)
    arrived(yxm1, yp_c, U1, xp)
    arrived(sb0, rsib(col), ALL, sib)
    arrived(sb1, rsib(mate), ALL, sib)
    arrived(sb2, rsib(along_z(3)), ALL, sib)
    arrived(sb3, rsib(along_z(1)), ALL, sib)
    arrived(gzp, yy_r, V1, zm)
    sb8 = send(yy_r, yy_r, V1, sib)
    arrived(gzm, yy_r, V3, zp)
    sb9 = send(yy_r, yy_r, V3, sib)
    arrived(gxp, yy_c, V1, xm)
    arrived(sb4, rsib(along_z(2)), ALL, sib)
    arrived(sb5, rsib(other(along_z(3))), U1, sib)
    arrived(sb14, rsib(other(along_z(1))), U1, sib)
    arrived(sb8, rsib(other(along_z(2))), V1, sib)
    write_lists(table_v, pair_lists(rows_ref, cols_ref), 0)
    hand = pltpu.make_async_copy(table_v, table_ref, own_sems.at[2])
    hand.start()
    arrived(gzn, yy_r, V4, zp)
    sb10 = send(yy_r, yy_r, V4, sib)
    arrived(gzq, yy_r, V2, zm)
    sb11 = send(yy_r, yy_r, V2, sib)

    arrived(yxp2, ym_c, W2, xm)
    arrived(uxp, yp_c, K, hi)
    arrived(uxm, ym_c, K, hi)
    arrived(uxx, yy_c, K, hi)
    arrived(gxm, yy_c, W2, xp)
    arrived(gxq, yy_c, V2, xm)
    arrived(sb6, rsib(other(along_z(1))), U2, sib)
    arrived(sb12, rsib(other(along_z(1))), L, sib)
    arrived(sb13, rsib(other(along_z(3))), L, sib)
    arrived(sb15, rsib(other(along_z(3))), U2, sib)
    arrived(sb7, rsib(other(along_z(2))), L, sib)
    arrived(sb9, rsib(other(along_z(2))), V3, sib)
    arrived(sb10, rsib(other(along_z(2))), V4, sib)
    arrived(sb11, rsib(other(along_z(2))), V2, sib)
    assert waited == set(range(len(started))) and len(started) == COPIES
    for copy in started:
        copy.wait_send()
    hand.wait()


COPIES = 58


def gather(block_mask, similarity):
    dtype = similarity.dtype
    cells = block_mask.size
    return pl.pallas_call(
        gather_kernel,
        out_shape=[
            pltpu.VMEM((17, SHARE, BLK), dtype),
            pltpu.VMEM((8, SHARE, BLK), dtype),
            pltpu.SMEM((DEPTH, BLK), jnp.int32),
        ],
        in_specs=[pl.BlockSpec(memory_space=pltpu.HBM)] * 2,
        out_specs=[
            pl.BlockSpec(memory_space=pltpu.VMEM),
            pl.BlockSpec(memory_space=pltpu.VMEM),
            pl.BlockSpec(memory_space=pltpu.SMEM),
        ],
        scratch_shapes=[
            pltpu.SMEM(block_mask.shape[::-1], jnp.int32),
            pltpu.VMEM((cells, BLK, BLK), dtype),
            pltpu.VMEM((SHARE, BLK), dtype),
            pltpu.VMEM((3, LAST_C * BLK, BLK), dtype),
            pltpu.VMEM((8, BLK), jnp.int32),
            pltpu.SMEM((8, BLK), jnp.int32),
            pltpu.SemaphoreType.DMA((COPIES,)),
            pltpu.SemaphoreType.DMA((COPIES,)),
            pltpu.SemaphoreType.DMA((3,)),
            pltpu.SemaphoreType.DMA((8,)),
            pltpu.VMEM((DEPTH, BLK), jnp.int32),
        ],
        compiler_params=pltpu.CompilerParams(
            collective_id=0, has_side_effects=True, vmem_limit_bytes=44 * MIB
        ),
        name="gather",
    )(block_mask.T, similarity)


def group_product(r_ref, c_ref, table, cell, g):
    words = [table[g * GROUP + t, cell] for t in range(GROUP)]
    return sum(
        jnp.dot(
            r_ref[(word >> 8) & 511],
            c_ref[word & 255],
            preferred_element_type=jnp.float32,
        )
        for word in words
    )


def as_blocks(ref):
    return ref.reshape(ref.shape[0] * SLOTS, BLK, BLK)


AT_ONCE = 4


def later_kernel(rows_ref, cols_ref, table_ref, extra_ref, table_v, table_s, list_s, sem):
    r_ref, c_ref = as_blocks(rows_ref), as_blocks(cols_ref)
    cells = extra_ref.shape[0] - 1

    def look(cell, found):
        list_s[found] = cell
        return found + jnp.where(length_of(table_ref, cell) > GROUP, 1, 0)

    found = lax.fori_loop(0, cells, look, jnp.int32(0), unroll=8)
    for t in range(AT_ONCE):
        list_s[found + t] = cells

    @pl.loop(0, (found + AT_ONCE - 1) // AT_ONCE)
    def _(n):
        for t in range(AT_ONCE):
            cell = list_s[n * AT_ONCE + t]
            extra_ref[cell] = group_product(r_ref, c_ref, table_ref, cell, 1)

    def add(table, cell, first):
        @pl.loop(first, (jnp.minimum(length_of(table, cell), DEPTH) + GROUP - 1) // GROUP)
        def _(g):
            extra_ref[cell] += group_product(r_ref, c_ref, table, cell, g)

    most = length_of(table_ref, BLK - 1)

    @pl.when(most > 2 * GROUP)
    def _():
        @pl.loop(0, found)
        def _(n):
            add(table_ref, list_s[n], 2)

    @pl.loop(1, (most + DEPTH - 1) // DEPTH)
    def _(d):
        write_lists(table_v, pair_lists(rows_ref, cols_ref), d * DEPTH)
        copy = pltpu.make_async_copy(table_v, table_s, sem)
        copy.start()
        copy.wait()

        @pl.loop(0, found)
        def _(n):
            add(table_s, list_s[n], 0)


VMEM, SMEM = pl.BlockSpec(memory_space=pltpu.VMEM), pl.BlockSpec(memory_space=pltpu.SMEM)


def later(rows, cols, table, cells):
    return pl.pallas_call(
        later_kernel,
        out_shape=pltpu.VMEM((cells + 1, BLK, BLK), jnp.float32),
        in_specs=[VMEM, VMEM, SMEM],
        out_specs=VMEM,
        scratch_shapes=[
            pltpu.VMEM(table.shape, jnp.int32),
            pltpu.SMEM(table.shape, jnp.int32),
            pltpu.SMEM((BLK,), jnp.int32),
            pltpu.SemaphoreType.DMA(()),
        ],
        compiler_params=pltpu.CompilerParams(vmem_limit_bytes=8 * MIB),
        name="later",
    )(rows, cols, table)


def product_kernel(
    rows_ref, cols_ref, table_ref, extra_ref, out_ref, total_ref, slots, send_sems, recv_sems
):
    row, col, layer = (lax.axis_index(a) for a in ("row", "col", "layer"))
    peers = [((row + s) % 8, col, layer) for s in range(1, 8)]
    barrier = pltpu.get_barrier_semaphore()
    for peer in peers:
        pl.semaphore_signal(barrier, inc=1, device_id=peer, device_id_type=MESH)

    r_ref, c_ref = as_blocks(rows_ref), as_blocks(cols_ref)
    tiles, wide = out_ref.shape[0] // BLK, out_ref.shape[1] // BLK

    def one_row(i, sums):
        lines = pl.ds(pl.multiple_of(i * BLK, BLK), BLK)
        out = []
        for j in range(wide):
            cell = i * wide + j
            value = group_product(r_ref, c_ref, table_ref, cell, 0)
            has_more = jnp.full((BLK, BLK), length_of(table_ref, cell), jnp.int32) > GROUP
            value = value + jnp.where(has_more, extra_ref[cell], 0.0)
            value = value * value
            out_ref[lines, pl.ds(j * BLK, BLK)] = value
            out.append(sums[j] + jnp.sum(value.reshape(BLK // 8, 8, BLK), axis=0))
        return tuple(out)

    sums = tuple(jnp.zeros((8, BLK), jnp.float32) for _ in range(wide))
    sums = lax.fori_loop(0, tiles, one_row, sums, unroll=6)
    slots[row] = jnp.concatenate([jnp.sum(v, axis=0, keepdims=True) for v in sums], 1)
    pl.semaphore_wait(barrier, 7)
    copies = [
        pltpu.make_async_remote_copy(
            src_ref=slots.at[row],
            dst_ref=slots.at[row],
            send_sem=send_sems.at[k],
            recv_sem=recv_sems.at[k],
            device_id=peer,
            device_id_type=MESH,
        )
        for k, peer in enumerate(peers)
    ]
    for copy in copies:
        copy.start()
    for copy in copies:
        copy.wait()
    total = slots[0]
    for q in range(1, 8):
        total = total + slots[q]
    total_ref[...] = total


def product(rows, cols, table, extra, shape):
    lanes = shape[1]
    return pl.pallas_call(
        product_kernel,
        out_shape=[pltpu.VMEM(shape, jnp.float32), pltpu.VMEM((1, lanes), jnp.float32)],
        in_specs=[VMEM, VMEM, SMEM, VMEM],
        out_specs=[VMEM, VMEM],
        scratch_shapes=[
            pltpu.VMEM((8, 1, lanes), jnp.float32),
            pltpu.SemaphoreType.DMA((7,)),
            pltpu.SemaphoreType.DMA((7,)),
        ],
        compiler_params=pltpu.CompilerParams(
            collective_id=1, has_side_effects=True, vmem_limit_bytes=8 * MIB
        ),
        name="product",
    )(rows, cols, table, extra)


STEPS = 6


def scale_kernel(scaling, value_ref, total_ref, out_ref, staged, sems):
    step = staged.shape[1]
    factor = scaling / total_ref[...]
    copies = []
    for t in range(STEPS):
        here = pl.ds(t * step, step)
        staged[t] = value_ref[here, :] * factor
        copy = pltpu.make_async_copy(staged.at[t], out_ref.at[here], sems.at[t])
        copy.start()
        copies.append(copy)
    for copy in copies:
        copy.wait()


def scale(value, total, scaling):
    rows, lanes = value.shape
    return pl.pallas_call(
        functools.partial(scale_kernel, scaling),
        out_shape=jax.ShapeDtypeStruct(value.shape, jnp.float32),
        in_specs=[pl.BlockSpec(memory_space=pltpu.VMEM)] * 2,
        out_specs=pl.BlockSpec(memory_space=pltpu.HBM),
        scratch_shapes=[
            pltpu.VMEM((STEPS, rows // STEPS, lanes), jnp.float32),
            pltpu.SemaphoreType.DMA((STEPS,)),
        ],
        compiler_params=pltpu.CompilerParams(vmem_limit_bytes=16 * MIB),
        name="scale",
    )(value, total)


def body(similarity, block_mask):
    rows, cols, table = gather(block_mask, similarity)
    extra = later(rows, cols, table, block_mask.size)
    value, total = product(rows, cols, table, extra, similarity.shape)
    scaling = similarity.shape[0] * lax.axis_size("row")
    return scale(value, total, float(scaling))


def solution(mesh):
    return jax.shard_map(
        body,
        mesh=mesh,
        in_specs=(P("row", ("col", "layer")), P("row", ("col", "layer"))),
        out_specs=P("row", ("col", "layer")),
        check_vma=False,
    )
```

```python
import functools

import jax
import jax.numpy as jnp
from jax import lax
from jax.experimental import pallas as pl
from jax.experimental.pallas import tpu as pltpu
from jax.sharding import PartitionSpec as P

BLK = 128
MAXNZ = 18
HEAD = 32
HALF = MAXNZ // 2
SLOTS = MAXNZ + 1
SHARE = SLOTS * BLK
TOP = BLK - HEAD
GROUP = 4
DEPTH = 16
FIELD = 256
COUNT = 512 * FIELD
MIB = 1 << 20
MESH = pl.DeviceIdType.MESH


def pack_share(mask_ref, x_ref, mask_s, x_v, share, place_v, place_s, signal, sems):
    cols, rows = mask_ref.shape
    fetch = pltpu.make_async_copy(mask_ref, mask_s, sems.at[cols + 1])
    fetch.start()
    strips = x_v.reshape(cols * rows * BLK, BLK)
    loads = [
        pltpu.make_async_copy(
            x_ref.at[:, pl.ds(j * BLK, BLK)],
            strips.at[pl.ds(j * rows * BLK, rows * BLK)],
            sems.at[j],
        )
        for j in range(cols)
    ]
    for load in loads:
        load.start()
    signal()
    sub = lax.broadcasted_iota(jnp.int32, (HEAD, BLK), 0)
    lane = lax.broadcasted_iota(jnp.int32, (HEAD, BLK), 1)
    lane_row = (lane * 43) >> 8
    lane_col = lane - lane_row * cols
    lane8 = lane[:8]

    def find(i, carry):
        count, place = carry
        for j in range(cols):
            here = mask_s[j, i]
            place = place + jnp.where(lane8 == count, here * (j * rows + i), 0)
            count = count + here
        return count, place

    fetch.wait()
    zero = jnp.int32(0)
    _, place = lax.fori_loop(0, rows, find, (zero, jnp.zeros((8, BLK), jnp.int32)), unroll=3)
    place_v[...] = place
    move = pltpu.make_async_copy(place_v, place_s, sems.at[cols])
    move.start()

    def mark(i, carry):
        count, head = carry
        below = 8 + jnp.where(i < cols, i, i - cols + 8)
        for j in range(cols):
            here = mask_s[j, i]
            cell = ((sub == j) & (lane_row == i)) | ((sub == below) & (lane_col == j))
            head = head + jnp.where(cell, here * (count + 1), 0)
            count = count + here
        return count, head

    _, head = lax.fori_loop(0, rows, mark, (zero, jnp.zeros((HEAD, BLK), jnp.int32)))
    head = jnp.where(lane < rows * cols, head, 0)
    share[pl.ds(TOP, HEAD), :] = head.astype(jnp.float32).astype(share.dtype)
    move.wait()
    for load in loads:
        load.wait()
    for s in range(MAXNZ):
        share[pl.ds((s + 1) * BLK, BLK), :] = x_v[place_s[0, s]]


def pair_lists(rows_ref, cols_ref):
    hr, hc = [], []
    for q in range(16):
        hr.append(rows_ref[q, pl.ds(TOP, HEAD), :].astype(jnp.float32)[0:8])
    for q in range(8):
        top = cols_ref[q, pl.ds(TOP, HEAD), :].astype(jnp.float32)
        hc += [top[8:16], top[16:24]]
    hr, hc = jnp.concatenate(hr, 0), jnp.concatenate(hc, 0)
    both = jnp.where((hr > 0) & (hc > 0), 1.0, 0.0)
    line = lax.broadcasted_iota(jnp.int32, (BLK, BLK), 0)
    before = line > lax.broadcasted_iota(jnp.int32, (BLK, BLK), 1)
    rank = jnp.dot(
        jnp.where(before, 1.0, 0.0).astype(jnp.bfloat16),
        both.astype(jnp.bfloat16),
        preferred_element_type=jnp.float32,
    )
    rank = jnp.where(both > 0, rank, -1.0).astype(jnp.int32)
    place_r = (line >> 3) * SLOTS + hr.astype(jnp.int32)
    place_c = (line >> 4) * SLOTS + hc.astype(jnp.int32)
    count = jnp.sum(both, axis=0, keepdims=True).astype(jnp.int32)
    return rank, place_r * FIELD + place_c, count


def write_lists(table_v, lists, done):
    rank, place, count = lists
    most = jnp.max(count, axis=1, keepdims=True)
    lane = lax.broadcasted_iota(jnp.int32, count.shape, 1)
    for p in range(DEPTH):
        one = jnp.sum(jnp.where(rank == done + p, place, 0), axis=0, keepdims=True)
        one = jnp.where(count > done + p, one, IDLE)
        if p == 0:
            length = jnp.where(lane == BLK - 1, most, jnp.maximum(count - done, 0))
            one = one + COUNT * length
        table_v[pl.ds(p, 1), :] = one


IDLE = 16 * SLOTS * FIELD + 1


def length_of(table, cell):
    return table[0, cell] >> 17


LAST_R = 5
LAST_C = 4
SPLIT = 7
SHIFT_Z = 2
SHIFT_X = 1


def span(first, last):
    low = (first + 1) * BLK if first else TOP
    return pl.ds(low, (last + 1) * BLK - low)


def gather_kernel(
    mask_ref,
    x_ref,
    rows_ref,
    cols_ref,
    table_ref,
    mask_s,
    x_v,
    share_ref,
    relay,
    place_v,
    place_s,
    send_sems,
    recv_sems,
    own_sems,
    pack_sems,
    table_v,
):
    row, col, layer = (lax.axis_index(a) for a in ("row", "col", "layer"))
    high, x = row // 4, row % 4
    z, low = col // 2, col % 2

    def along_z(step):
        return 2 * ((z + step) % 4) + low

    def along_x(step):
        return 4 * high + (x + step) % 4

    mate = 2 * z + 1 - low
    far = 4 * (1 - high) + x

    zp, zm = (row, along_z(1), layer), (row, along_z(3), layer)
    xp, xm = (along_x(1), col, layer), (along_x(3), col, layer)
    lo, hi = (row, mate, layer), (far, mate, layer)
    sib = (row, col, 1 - layer)

    barrier = pltpu.get_barrier_semaphore()

    def signal():
        for peer in (zp, zm, xp, xm, lo, hi, sib):
            pl.semaphore_signal(barrier, inc=1, device_id=peer, device_id_type=MESH)

    pack_share(mask_ref, x_ref, mask_s, x_v, share_ref, place_v, place_s, signal, pack_sems)
    pl.semaphore_wait(barrier, 7)

    ALL = span(0, MAXNZ)
    mine = 2 * col + layer
    keep = [
        pltpu.make_async_copy(share_ref.at[ALL], rows_ref.at[mine].at[ALL], own_sems.at[0]),
        pltpu.make_async_copy(share_ref.at[ALL], cols_ref.at[row].at[ALL], own_sems.at[1]),
    ]

    EARLY, EARLY_C = MAXNZ - LAST_R, MAXNZ - LAST_C
    H1, H2 = span(0, HALF), span(HALF, MAXNZ)
    U1, U2, L = span(0, SPLIT), span(SPLIT, EARLY), span(EARLY, MAXNZ)
    V1, V2, V3, V4 = span(0, 4), span(4, SPLIT), span(SPLIT, 10), span(10, EARLY)
    W2, K = span(SPLIT, EARLY_C), span(EARLY_C, MAXNZ)
    T = pl.ds(0, LAST_C * BLK)
    started = []
    waited = set()

    def either(part, act):
        if isinstance(part, tuple):
            flag, held, plain = part
            pl.when(flag)(lambda: act(held))
            pl.when(jnp.logical_not(flag))(lambda: act(plain))
        else:
            act(part)

    def copy_of(k, src, dst, part, into, peer):
        return pltpu.make_async_remote_copy(
            src_ref=src.at[part],
            dst_ref=dst.at[part if into is None else into],
            send_sem=send_sems.at[k],
            recv_sem=recv_sems.at[k],
            device_id=peer,
            device_id_type=MESH,
        )

    def send(src, dst, part, peer, into=None):
        k = len(started)
        either(part, lambda p: copy_of(k, src, dst, p, into, peer).start())
        started.append((part, lambda p: copy_of(k, src, dst, p, into, peer).wait_send()))
        return k

    def arrived(k, dst, part, peer):
        waited.add(k)
        either(part, lambda p: copy_of(k, dst, dst, p, None, peer).wait_recv())

    def halves(place, shift):
        cut = HALF - shift
        pairs = []
        for step in (0, 3, 1, 2):
            flag = (place + step) % 4 == 2
            pairs.append(((flag, span(0, cut), H1), (flag, span(cut, MAXNZ), H2)))
        return pairs

    (A1, A2), (M1, M2), (P1, P2), (F1, F2) = halves(z, SHIFT_Z)
    (B1, B2), (N1, N2), (Q1, Q2), (G1, G2) = halves(x, SHIFT_X)

    def other(q):
        return q + 1 - 2 * (q % 2)

    def r(q):
        return rows_ref.at[2 * q + layer]

    def rsib(q):
        return rows_ref.at[2 * q + 1 - layer]

    def c(q):
        return cols_ref.at[q]

    def across(q):
        return c((q + 4) % 8)

    own_r, own_c = r(col), c(row)
    y_r, y_c = r(mate), c(far)
    zm_r, zp_r, zz_r = (r(along_z(s)) for s in (3, 1, 2))
    ym_r, yp_r, yy_r = (r(other(along_z(s))) for s in (3, 1, 2))
    xm_c, xp_c, xx_c = (c(along_x(s)) for s in (3, 1, 2))
    ym_c, yp_c, yy_c = (across(along_x(s)) for s in (3, 1, 2))

    lo1 = send(share_ref, own_r, U1, lo)
    zp1 = send(share_ref, own_r, A1, zp)
    zm2 = send(share_ref, own_r, A2, zm)
    xp1 = send(share_ref, own_c, B1, xp)
    xm2 = send(share_ref, own_c, B2, xm)
    lo2 = send(share_ref, own_r, U2, lo)
    zp2 = send(share_ref, own_r, A2, zp)
    zm1 = send(share_ref, own_r, A1, zm)
    xp2 = send(share_ref, own_c, B2, xp)
    xm1 = send(share_ref, own_c, B1, xm)
    lo3 = send(share_ref, own_r, L, lo)
    sb0 = send(share_ref, own_r, ALL, sib)
    for copy in keep:
        copy.start()
    rows_ref[16, pl.ds(0, BLK), :] = jnp.zeros((BLK, BLK), rows_ref.dtype)

    arrived(lo1, y_r, U1, lo)
    hi1 = send(y_r, own_c, U1, hi)
    yzp1 = send(y_r, y_r, U1, zp)
    arrived(zp1, zm_r, M1, zm)
    fzp = send(zm_r, zm_r, M1, zp)
    arrived(zm2, zp_r, P2, zp)
    fzm = send(zp_r, zp_r, P2, zm)
    arrived(xp1, xm_c, N1, xm)
    fxp = send(xm_c, xm_c, N1, xp)
    arrived(xm2, xp_c, Q2, xp)
    fxm = send(xp_c, xp_c, Q2, xm)
    txp = send(xp_c, relay.at[0], K, lo, T)
    lzp = send(zp_r, zp_r, L, lo)
    arrived(lo2, y_r, U2, lo)
    hi2 = send(y_r, own_c, U2, hi)
    yzm2 = send(y_r, y_r, U2, zm)
    yzp2 = send(y_r, y_r, U2, zp)
    yzm1 = send(y_r, y_r, U1, zm)
    arrived(hi1, y_c, U1, hi)
    yxp1 = send(y_c, y_c, U1, xp)
    arrived(lo3, y_r, L, lo)
    hi3 = send(y_r, own_c, L, hi)
    sb1 = send(y_r, y_r, ALL, sib)

    arrived(zp2, zm_r, M2, zm)
    arrived(xp2, xm_c, N2, xm)
    txm = send(xm_c, relay.at[1], K, lo, T)
    lzm = send(zm_r, zm_r, L, lo)
    sb2 = send(zm_r, zm_r, ALL, sib)
    arrived(zm1, zp_r, P1, zp)
    sb3 = send(zp_r, zp_r, ALL, sib)
    arrived(hi2, y_c, U2, hi)
    arrived(hi3, y_c, L, hi)
    yxm2 = send(y_c, y_c, W2, xm)
    yxp2 = send(y_c, y_c, W2, xp)
    yxm1 = send(y_c, y_c, U1, xm)
    arrived(txp, relay.at[0], T, lo)
    uxp = send(relay.at[0], xp_c, T, hi, K)
    arrived(fxm, xx_c, G2, xp)
    txx = send(xx_c, relay.at[2], K, lo, T)
    arrived(fzm, zz_r, F2, zp)
    lzz = send(zz_r, zz_r, L, lo)
    arrived(fzp, zz_r, F1, zm)
    sb4 = send(zz_r, zz_r, ALL, sib)
    arrived(txm, relay.at[1], T, lo)
    uxm = send(relay.at[1], xm_c, T, hi, K)

    arrived(yzp1, ym_r, U1, zm)
    gzp = send(ym_r, ym_r, V1, zp)
    gzq = send(ym_r, ym_r, V2, zp)
    arrived(yzm2, yp_r, U2, zp)
    gzm = send(yp_r, yp_r, V3, zm)
    gzn = send(yp_r, yp_r, V4, zm)
    arrived(yxp1, ym_c, U1, xm)
    gxp = send(ym_c, ym_c, V1, xp)
    gxq = send(ym_c, ym_c, V2, xp)
    arrived(yxm2, yp_c, W2, xp)
    gxm = send(yp_c, yp_c, W2, xm)
    sb5 = send(ym_r, ym_r, U1, sib)
    sb6 = send(yp_r, yp_r, U2, sib)
    arrived(lzp, yp_r, L, lo)
    sb12 = send(yp_r, yp_r, L, sib)
    arrived(lzm, ym_r, L, lo)
    sb13 = send(ym_r, ym_r, L, sib)
    arrived(txx, relay.at[2], T, lo)
    uxx = send(relay.at[2], xx_c, T, hi, K)
    arrived(yzm1, yp_r, U1, zp)
    sb14 = send(yp_r, yp_r, U1, sib)
    arrived(yzp2, ym_r, U2, zm)
    sb15 = send(ym_r, ym_r, U2, sib)
    arrived(lzz, yy_r, L, lo)
    sb7 = send(yy_r, yy_r, L, sib)
    for copy in keep:
        copy.wait()
    arrived(xm1, xp_c, Q1, xp)
    arrived(fxp, xx_c, G1, xm)
    arrived(yxm1, yp_c, U1, xp)
    arrived(sb0, rsib(col), ALL, sib)
    arrived(sb1, rsib(mate), ALL, sib)
    arrived(sb2, rsib(along_z(3)), ALL, sib)
    arrived(sb3, rsib(along_z(1)), ALL, sib)
    arrived(gzp, yy_r, V1, zm)
    sb8 = send(yy_r, yy_r, V1, sib)
    arrived(gzm, yy_r, V3, zp)
    sb9 = send(yy_r, yy_r, V3, sib)
    arrived(gxp, yy_c, V1, xm)
    arrived(sb4, rsib(along_z(2)), ALL, sib)
    arrived(sb5, rsib(other(along_z(3))), U1, sib)
    arrived(sb14, rsib(other(along_z(1))), U1, sib)
    arrived(sb8, rsib(other(along_z(2))), V1, sib)
    write_lists(table_v, pair_lists(rows_ref, cols_ref), 0)
    hand = pltpu.make_async_copy(table_v, table_ref, own_sems.at[2])
    hand.start()
    arrived(gzn, yy_r, V4, zp)
    sb10 = send(yy_r, yy_r, V4, sib)
    arrived(gzq, yy_r, V2, zm)
    sb11 = send(yy_r, yy_r, V2, sib)

    arrived(yxp2, ym_c, W2, xm)
    arrived(uxp, yp_c, K, hi)
    arrived(uxm, ym_c, K, hi)
    arrived(uxx, yy_c, K, hi)
    arrived(gxm, yy_c, W2, xp)
    arrived(gxq, yy_c, V2, xm)
    arrived(sb6, rsib(other(along_z(1))), U2, sib)
    arrived(sb12, rsib(other(along_z(1))), L, sib)
    arrived(sb13, rsib(other(along_z(3))), L, sib)
    arrived(sb15, rsib(other(along_z(3))), U2, sib)
    arrived(sb7, rsib(other(along_z(2))), L, sib)
    arrived(sb9, rsib(other(along_z(2))), V3, sib)
    arrived(sb10, rsib(other(along_z(2))), V4, sib)
    arrived(sb11, rsib(other(along_z(2))), V2, sib)
    assert waited == set(range(len(started))) and len(started) == COPIES
    for part, wait in started:
        either(part, wait)
    hand.wait()


COPIES = 58


def gather(block_mask, similarity):
    dtype = similarity.dtype
    cells = block_mask.size
    return pl.pallas_call(
        gather_kernel,
        out_shape=[
            pltpu.VMEM((17, SHARE, BLK), dtype),
            pltpu.VMEM((8, SHARE, BLK), dtype),
            pltpu.SMEM((DEPTH, BLK), jnp.int32),
        ],
        in_specs=[pl.BlockSpec(memory_space=pltpu.HBM)] * 2,
        out_specs=[
            pl.BlockSpec(memory_space=pltpu.VMEM),
            pl.BlockSpec(memory_space=pltpu.VMEM),
            pl.BlockSpec(memory_space=pltpu.SMEM),
        ],
        scratch_shapes=[
            pltpu.SMEM(block_mask.shape[::-1], jnp.int32),
            pltpu.VMEM((cells, BLK, BLK), dtype),
            pltpu.VMEM((SHARE, BLK), dtype),
            pltpu.VMEM((3, LAST_C * BLK, BLK), dtype),
            pltpu.VMEM((8, BLK), jnp.int32),
            pltpu.SMEM((8, BLK), jnp.int32),
            pltpu.SemaphoreType.DMA((COPIES,)),
            pltpu.SemaphoreType.DMA((COPIES,)),
            pltpu.SemaphoreType.DMA((3,)),
            pltpu.SemaphoreType.DMA((8,)),
            pltpu.VMEM((DEPTH, BLK), jnp.int32),
        ],
        compiler_params=pltpu.CompilerParams(
            collective_id=0, has_side_effects=True, vmem_limit_bytes=44 * MIB
        ),
        name="gather",
    )(block_mask.T, similarity)


def group_product(r_ref, c_ref, table, cell, g):
    words = [table[g * GROUP + t, cell] for t in range(GROUP)]
    return sum(
        jnp.dot(
            r_ref[(word >> 8) & 511],
            c_ref[word & 255],
            preferred_element_type=jnp.float32,
        )
        for word in words
    )


def as_blocks(ref):
    return ref.reshape(ref.shape[0] * SLOTS, BLK, BLK)


AT_ONCE = 4


def later_kernel(rows_ref, cols_ref, table_ref, extra_ref, table_v, table_s, list_s, sem):
    r_ref, c_ref = as_blocks(rows_ref), as_blocks(cols_ref)
    cells = extra_ref.shape[0] - 1

    def look(cell, found):
        list_s[found] = cell
        return found + jnp.where(length_of(table_ref, cell) > GROUP, 1, 0)

    found = lax.fori_loop(0, cells, look, jnp.int32(0), unroll=8)
    for t in range(AT_ONCE):
        list_s[found + t] = cells

    @pl.loop(0, (found + AT_ONCE - 1) // AT_ONCE)
    def _(n):
        for t in range(AT_ONCE):
            cell = list_s[n * AT_ONCE + t]
            extra_ref[cell] = group_product(r_ref, c_ref, table_ref, cell, 1)

    def add(table, cell, first):
        @pl.loop(first, (jnp.minimum(length_of(table, cell), DEPTH) + GROUP - 1) // GROUP)
        def _(g):
            extra_ref[cell] += group_product(r_ref, c_ref, table, cell, g)

    most = length_of(table_ref, BLK - 1)

    @pl.when(most > 2 * GROUP)
    def _():
        @pl.loop(0, found)
        def _(n):
            add(table_ref, list_s[n], 2)

    @pl.loop(1, (most + DEPTH - 1) // DEPTH)
    def _(d):
        write_lists(table_v, pair_lists(rows_ref, cols_ref), d * DEPTH)
        copy = pltpu.make_async_copy(table_v, table_s, sem)
        copy.start()
        copy.wait()

        @pl.loop(0, found)
        def _(n):
            add(table_s, list_s[n], 0)


VMEM, SMEM = pl.BlockSpec(memory_space=pltpu.VMEM), pl.BlockSpec(memory_space=pltpu.SMEM)


def later(rows, cols, table, cells):
    return pl.pallas_call(
        later_kernel,
        out_shape=pltpu.VMEM((cells + 1, BLK, BLK), jnp.float32),
        in_specs=[VMEM, VMEM, SMEM],
        out_specs=VMEM,
        scratch_shapes=[
            pltpu.VMEM(table.shape, jnp.int32),
            pltpu.SMEM(table.shape, jnp.int32),
            pltpu.SMEM((BLK,), jnp.int32),
            pltpu.SemaphoreType.DMA(()),
        ],
        compiler_params=pltpu.CompilerParams(vmem_limit_bytes=8 * MIB),
        name="later",
    )(rows, cols, table)


def product_kernel(
    rows_ref, cols_ref, table_ref, extra_ref, out_ref, total_ref, slots, send_sems, recv_sems
):
    row, col, layer = (lax.axis_index(a) for a in ("row", "col", "layer"))
    peers = [((row + s) % 8, col, layer) for s in range(1, 8)]
    barrier = pltpu.get_barrier_semaphore()
    for peer in peers:
        pl.semaphore_signal(barrier, inc=1, device_id=peer, device_id_type=MESH)

    r_ref, c_ref = as_blocks(rows_ref), as_blocks(cols_ref)
    tiles, wide = out_ref.shape[0] // BLK, out_ref.shape[1] // BLK

    def one_row(i, sums):
        lines = pl.ds(pl.multiple_of(i * BLK, BLK), BLK)
        out = []
        for j in range(wide):
            cell = i * wide + j
            value = group_product(r_ref, c_ref, table_ref, cell, 0)
            has_more = jnp.full((BLK, BLK), length_of(table_ref, cell), jnp.int32) > GROUP
            value = value + jnp.where(has_more, extra_ref[cell], 0.0)
            value = value * value
            out_ref[lines, pl.ds(j * BLK, BLK)] = value
            out.append(sums[j] + jnp.sum(value.reshape(BLK // 8, 8, BLK), axis=0))
        return tuple(out)

    sums = tuple(jnp.zeros((8, BLK), jnp.float32) for _ in range(wide))
    sums = lax.fori_loop(0, tiles, one_row, sums, unroll=6)
    slots[row] = jnp.concatenate([jnp.sum(v, axis=0, keepdims=True) for v in sums], 1)
    pl.semaphore_wait(barrier, 7)
    copies = [
        pltpu.make_async_remote_copy(
            src_ref=slots.at[row],
            dst_ref=slots.at[row],
            send_sem=send_sems.at[k],
            recv_sem=recv_sems.at[k],
            device_id=peer,
            device_id_type=MESH,
        )
        for k, peer in enumerate(peers)
    ]
    for copy in copies:
        copy.start()
    for copy in copies:
        copy.wait()
    total = slots[0]
    for q in range(1, 8):
        total = total + slots[q]
    total_ref[...] = total


def product(rows, cols, table, extra, shape):
    lanes = shape[1]
    return pl.pallas_call(
        product_kernel,
        out_shape=[pltpu.VMEM(shape, jnp.float32), pltpu.VMEM((1, lanes), jnp.float32)],
        in_specs=[VMEM, VMEM, SMEM, VMEM],
        out_specs=[VMEM, VMEM],
        scratch_shapes=[
            pltpu.VMEM((8, 1, lanes), jnp.float32),
            pltpu.SemaphoreType.DMA((7,)),
            pltpu.SemaphoreType.DMA((7,)),
        ],
        compiler_params=pltpu.CompilerParams(
            collective_id=1, has_side_effects=True, vmem_limit_bytes=8 * MIB
        ),
        name="product",
    )(rows, cols, table, extra)


STEPS = 6


def scale_kernel(scaling, value_ref, total_ref, out_ref, staged, sems):
    step = staged.shape[1]
    factor = scaling / total_ref[...]
    copies = []
    for t in range(STEPS):
        here = pl.ds(t * step, step)
        staged[t] = value_ref[here, :] * factor
        copy = pltpu.make_async_copy(staged.at[t], out_ref.at[here], sems.at[t])
        copy.start()
        copies.append(copy)
    for copy in copies:
        copy.wait()


def scale(value, total, scaling):
    rows, lanes = value.shape
    return pl.pallas_call(
        functools.partial(scale_kernel, scaling),
        out_shape=jax.ShapeDtypeStruct(value.shape, jnp.float32),
        in_specs=[pl.BlockSpec(memory_space=pltpu.VMEM)] * 2,
        out_specs=pl.BlockSpec(memory_space=pltpu.HBM),
        scratch_shapes=[
            pltpu.VMEM((STEPS, rows // STEPS, lanes), jnp.float32),
            pltpu.SemaphoreType.DMA((STEPS,)),
        ],
        compiler_params=pltpu.CompilerParams(vmem_limit_bytes=16 * MIB),
        name="scale",
    )(value, total)


def body(similarity, block_mask):
    rows, cols, table = gather(block_mask, similarity)
    extra = later(rows, cols, table, block_mask.size)
    value, total = product(rows, cols, table, extra, similarity.shape)
    scaling = similarity.shape[0] * lax.axis_size("row")
    return scale(value, total, float(scaling))


def solution(mesh):
    return jax.shard_map(
        body,
        mesh=mesh,
        in_specs=(P("row", ("col", "layer")), P("row", ("col", "layer"))),
        out_specs=P("row", ("col", "layer")),
        check_vma=False,
    )
```

```python
import functools

import jax
import jax.numpy as jnp
from jax import lax
from jax.experimental import pallas as pl
from jax.experimental.pallas import tpu as pltpu
from jax.sharding import PartitionSpec as P

BLK = 128
MAXNZ = 18
HEAD = 32
HALF = MAXNZ // 2
SLOTS = MAXNZ + 1
SHARE = SLOTS * BLK
TOP = BLK - HEAD
GROUP = 4
DEPTH = 16
FIELD = 256
COUNT = 512 * FIELD
MIB = 1 << 20
MESH = pl.DeviceIdType.MESH


def pack_share(mask_ref, x_ref, mask_s, x_v, share, place_v, place_s, signal, sems):
    cols, rows = mask_ref.shape
    fetch = pltpu.make_async_copy(mask_ref, mask_s, sems.at[cols + 1])
    fetch.start()
    strips = x_v.reshape(cols * rows * BLK, BLK)
    loads = [
        pltpu.make_async_copy(
            x_ref.at[:, pl.ds(j * BLK, BLK)],
            strips.at[pl.ds(j * rows * BLK, rows * BLK)],
            sems.at[j],
        )
        for j in range(cols)
    ]
    for load in loads:
        load.start()
    signal()
    sub = lax.broadcasted_iota(jnp.int32, (HEAD, BLK), 0)
    lane = lax.broadcasted_iota(jnp.int32, (HEAD, BLK), 1)
    lane_row = (lane * 43) >> 8
    lane_col = lane - lane_row * cols
    lane8 = lane[:8]

    def find(i, carry):
        count, place = carry
        for j in range(cols):
            here = mask_s[j, i]
            place = place + jnp.where(lane8 == count, here * (j * rows + i), 0)
            count = count + here
        return count, place

    fetch.wait()
    zero = jnp.int32(0)
    _, place = lax.fori_loop(0, rows, find, (zero, jnp.zeros((8, BLK), jnp.int32)), unroll=3)
    place_v[...] = place
    move = pltpu.make_async_copy(place_v, place_s, sems.at[cols])
    move.start()

    def mark(i, carry):
        count, head = carry
        below = 8 + jnp.where(i < cols, i, i - cols + 8)
        for j in range(cols):
            here = mask_s[j, i]
            cell = ((sub == j) & (lane_row == i)) | ((sub == below) & (lane_col == j))
            head = head + jnp.where(cell, here * (count + 1), 0)
            count = count + here
        return count, head

    _, head = lax.fori_loop(0, rows, mark, (zero, jnp.zeros((HEAD, BLK), jnp.int32)))
    head = jnp.where(lane < rows * cols, head, 0)
    share[pl.ds(TOP, HEAD), :] = head.astype(jnp.float32).astype(share.dtype)
    move.wait()
    for load in loads:
        load.wait()
    for s in range(MAXNZ):
        share[pl.ds((s + 1) * BLK, BLK), :] = x_v[place_s[0, s]]


def pair_lists(rows_ref, cols_ref):
    hr, hc = [], []
    for q in range(16):
        hr.append(rows_ref[q, pl.ds(TOP, HEAD), :].astype(jnp.float32)[0:8])
    for q in range(8):
        top = cols_ref[q, pl.ds(TOP, HEAD), :].astype(jnp.float32)
        hc += [top[8:16], top[16:24]]
    hr, hc = jnp.concatenate(hr, 0), jnp.concatenate(hc, 0)
    both = jnp.where((hr > 0) & (hc > 0), 1.0, 0.0)
    line = lax.broadcasted_iota(jnp.int32, (BLK, BLK), 0)
    before = line > lax.broadcasted_iota(jnp.int32, (BLK, BLK), 1)
    rank = jnp.dot(
        jnp.where(before, 1.0, 0.0).astype(jnp.bfloat16),
        both.astype(jnp.bfloat16),
        preferred_element_type=jnp.float32,
    )
    rank = jnp.where(both > 0, rank, -1.0).astype(jnp.int32)
    place_r = (line >> 3) * SLOTS + hr.astype(jnp.int32)
    place_c = (line >> 4) * SLOTS + hc.astype(jnp.int32)
    count = jnp.sum(both, axis=0, keepdims=True).astype(jnp.int32)
    return rank, place_r * FIELD + place_c, count


def write_lists(table_v, lists, done):
    rank, place, count = lists
    most = jnp.max(count, axis=1, keepdims=True)
    lane = lax.broadcasted_iota(jnp.int32, count.shape, 1)
    for p in range(DEPTH):
        one = jnp.sum(jnp.where(rank == done + p, place, 0), axis=0, keepdims=True)
        one = jnp.where(count > done + p, one, IDLE)
        if p == 0:
            length = jnp.where(lane == BLK - 1, most, jnp.maximum(count - done, 0))
            one = one + COUNT * length
        table_v[pl.ds(p, 1), :] = one


IDLE = 16 * SLOTS * FIELD + 1


def length_of(table, cell):
    return table[0, cell] >> 17


LAST_R = 5
LAST_C = 4
SPLIT = 7
SHIFT_Z = 2
SHIFT_X = 1


def span(first, last):
    low = (first + 1) * BLK if first else TOP
    return pl.ds(low, (last + 1) * BLK - low)


def gather_kernel(
    mask_ref,
    x_ref,
    rows_ref,
    cols_ref,
    table_ref,
    mask_s,
    x_v,
    share_ref,
    relay,
    place_v,
    place_s,
    send_sems,
    recv_sems,
    own_sems,
    pack_sems,
    table_v,
):
    row, col, layer = (lax.axis_index(a) for a in ("row", "col", "layer"))
    high, x = row // 4, row % 4
    z, low = col // 2, col % 2

    def along_z(step):
        return 2 * ((z + step) % 4) + low

    def along_x(step):
        return 4 * high + (x + step) % 4

    mate = 2 * z + 1 - low
    far = 4 * (1 - high) + x

    zp, zm = (row, along_z(1), layer), (row, along_z(3), layer)
    xp, xm = (along_x(1), col, layer), (along_x(3), col, layer)
    lo, hi = (row, mate, layer), (far, mate, layer)
    sib = (row, col, 1 - layer)

    barrier = pltpu.get_barrier_semaphore()

    def signal():
        for peer in (zp, zm, xp, xm, lo, hi, sib):
            pl.semaphore_signal(barrier, inc=1, device_id=peer, device_id_type=MESH)

    pack_share(mask_ref, x_ref, mask_s, x_v, share_ref, place_v, place_s, signal, pack_sems)
    pl.semaphore_wait(barrier, 7)

    ALL = span(0, MAXNZ)
    mine = 2 * col + layer
    keep = [
        pltpu.make_async_copy(share_ref.at[ALL], rows_ref.at[mine].at[ALL], own_sems.at[0]),
        pltpu.make_async_copy(share_ref.at[ALL], cols_ref.at[row].at[ALL], own_sems.at[1]),
    ]

    EARLY, EARLY_C = MAXNZ - LAST_R, MAXNZ - LAST_C
    H1, H2 = span(0, HALF), span(HALF, MAXNZ)
    U1, U2, L = span(0, SPLIT), span(SPLIT, EARLY), span(EARLY, MAXNZ)
    V1, V2, V3, V4 = span(0, 4), span(4, SPLIT), span(SPLIT, 10), span(10, EARLY)
    W2, K = span(SPLIT, EARLY_C), span(EARLY_C, MAXNZ)
    T = pl.ds(0, LAST_C * BLK)
    started = []
    waited = set()

    def either(part, act):
        if isinstance(part, tuple):
            flag, held, plain = part
            pl.when(flag)(lambda: act(held))
            pl.when(jnp.logical_not(flag))(lambda: act(plain))
        else:
            act(part)

    def copy_of(k, src, dst, part, into, peer):
        return pltpu.make_async_remote_copy(
            src_ref=src.at[part],
            dst_ref=dst.at[part if into is None else into],
            send_sem=send_sems.at[k],
            recv_sem=recv_sems.at[k],
            device_id=peer,
            device_id_type=MESH,
        )

    def send(src, dst, part, peer, into=None):
        k = len(started)
        either(part, lambda p: copy_of(k, src, dst, p, into, peer).start())
        started.append((part, lambda p: copy_of(k, src, dst, p, into, peer).wait_send()))
        return k

    def arrived(k, dst, part, peer):
        waited.add(k)
        either(part, lambda p: copy_of(k, dst, dst, p, None, peer).wait_recv())

    def halves(place, shift):
        cut = HALF - shift
        pairs = []
        for step in (0, 3, 1, 2):
            flag = (place + step) % 4 == 2
            pairs.append(((flag, span(0, cut), H1), (flag, span(cut, MAXNZ), H2)))
        return pairs

    (A1, A2), (M1, M2), (P1, P2), (F1, F2) = halves(z, SHIFT_Z)
    (B1, B2), (N1, N2), (Q1, Q2), (G1, G2) = halves(x, SHIFT_X)

    def other(q):
        return q + 1 - 2 * (q % 2)

    def r(q):
        return rows_ref.at[2 * q + layer]

    def rsib(q):
        return rows_ref.at[2 * q + 1 - layer]

    def c(q):
        return cols_ref.at[q]

    def across(q):
        return c((q + 4) % 8)

    own_r, own_c = r(col), c(row)
    y_r, y_c = r(mate), c(far)
    zm_r, zp_r, zz_r = (r(along_z(s)) for s in (3, 1, 2))
    ym_r, yp_r, yy_r = (r(other(along_z(s))) for s in (3, 1, 2))
    xm_c, xp_c, xx_c = (c(along_x(s)) for s in (3, 1, 2))
    ym_c, yp_c, yy_c = (across(along_x(s)) for s in (3, 1, 2))

    lo1 = send(share_ref, own_r, U1, lo)
    zp1 = send(share_ref, own_r, A1, zp)
    zm2 = send(share_ref, own_r, A2, zm)
    xp1 = send(share_ref, own_c, B1, xp)
    xm2 = send(share_ref, own_c, B2, xm)
    lo2 = send(share_ref, own_r, U2, lo)
    zp2 = send(share_ref, own_r, A2, zp)
    zm1 = send(share_ref, own_r, A1, zm)
    xp2 = send(share_ref, own_c, B2, xp)
    xm1 = send(share_ref, own_c, B1, xm)
    lo3 = send(share_ref, own_r, L, lo)
    sb0 = send(share_ref, own_r, ALL, sib)
    for copy in keep:
        copy.start()
    rows_ref[16, pl.ds(0, BLK), :] = jnp.zeros((BLK, BLK), rows_ref.dtype)

    arrived(lo1, y_r, U1, lo)
    hi1 = send(y_r, own_c, U1, hi)
    yzp1 = send(y_r, y_r, U1, zp)
    arrived(zp1, zm_r, M1, zm)
    fzp = send(zm_r, zm_r, M1, zp)
    arrived(zm2, zp_r, P2, zp)
    fzm = send(zp_r, zp_r, P2, zm)
    arrived(xp1, xm_c, N1, xm)
    fxp = send(xm_c, xm_c, N1, xp)
    arrived(xm2, xp_c, Q2, xp)
    fxm = send(xp_c, xp_c, Q2, xm)
    txp = send(xp_c, relay.at[0], K, lo, T)
    lzp = send(zp_r, zp_r, L, lo)
    arrived(lo2, y_r, U2, lo)
    hi2 = send(y_r, own_c, U2, hi)
    yzm2 = send(y_r, y_r, U2, zm)
    yzp2 = send(y_r, y_r, U2, zp)
    yzm1 = send(y_r, y_r, U1, zm)
    arrived(hi1, y_c, U1, hi)
    yxp1 = send(y_c, y_c, U1, xp)
    arrived(lo3, y_r, L, lo)
    hi3 = send(y_r, own_c, L, hi)
    sb1 = send(y_r, y_r, ALL, sib)

    arrived(zp2, zm_r, M2, zm)
    arrived(xp2, xm_c, N2, xm)
    txm = send(xm_c, relay.at[1], K, lo, T)
    lzm = send(zm_r, zm_r, L, lo)
    sb2 = send(zm_r, zm_r, ALL, sib)
    arrived(zm1, zp_r, P1, zp)
    sb3 = send(zp_r, zp_r, ALL, sib)
    arrived(hi2, y_c, U2, hi)
    arrived(hi3, y_c, L, hi)
    yxm2 = send(y_c, y_c, W2, xm)
    yxp2 = send(y_c, y_c, W2, xp)
    yxm1 = send(y_c, y_c, U1, xm)
    arrived(txp, relay.at[0], T, lo)
    uxp = send(relay.at[0], xp_c, T, hi, K)
    arrived(fxm, xx_c, G2, xp)
    txx = send(xx_c, relay.at[2], K, lo, T)
    arrived(fzm, zz_r, F2, zp)
    lzz = send(zz_r, zz_r, L, lo)
    arrived(fzp, zz_r, F1, zm)
    sb4 = send(zz_r, zz_r, ALL, sib)
    arrived(txm, relay.at[1], T, lo)
    uxm = send(relay.at[1], xm_c, T, hi, K)

    arrived(yzp1, ym_r, U1, zm)
    gzp = send(ym_r, ym_r, V1, zp)
    gzq = send(ym_r, ym_r, V2, zp)
    arrived(yzm2, yp_r, U2, zp)
    gzm = send(yp_r, yp_r, V3, zm)
    gzn = send(yp_r, yp_r, V4, zm)
    arrived(yxp1, ym_c, U1, xm)
    gxp = send(ym_c, ym_c, V1, xp)
    gxq = send(ym_c, ym_c, V2, xp)
    arrived(yxm2, yp_c, W2, xp)
    gxm = send(yp_c, yp_c, W2, xm)
    sb5 = send(ym_r, ym_r, U1, sib)
    sb6 = send(yp_r, yp_r, U2, sib)
    arrived(lzp, yp_r, L, lo)
    sb12 = send(yp_r, yp_r, L, sib)
    arrived(lzm, ym_r, L, lo)
    sb13 = send(ym_r, ym_r, L, sib)
    arrived(txx, relay.at[2], T, lo)
    uxx = send(relay.at[2], xx_c, T, hi, K)
    arrived(yzm1, yp_r, U1, zp)
    sb14 = send(yp_r, yp_r, U1, sib)
    arrived(yzp2, ym_r, U2, zm)
    sb15 = send(ym_r, ym_r, U2, sib)
    arrived(lzz, yy_r, L, lo)
    sb7 = send(yy_r, yy_r, L, sib)
    for copy in keep:
        copy.wait()
    arrived(xm1, xp_c, Q1, xp)
    arrived(fxp, xx_c, G1, xm)
    arrived(yxm1, yp_c, U1, xp)
    arrived(sb0, rsib(col), ALL, sib)
    arrived(sb1, rsib(mate), ALL, sib)
    arrived(sb2, rsib(along_z(3)), ALL, sib)
    arrived(sb3, rsib(along_z(1)), ALL, sib)
    arrived(gzp, yy_r, V1, zm)
    sb8 = send(yy_r, yy_r, V1, sib)
    arrived(gzm, yy_r, V3, zp)
    sb9 = send(yy_r, yy_r, V3, sib)
    arrived(gxp, yy_c, V1, xm)
    arrived(sb4, rsib(along_z(2)), ALL, sib)
    arrived(sb5, rsib(other(along_z(3))), U1, sib)
    arrived(sb14, rsib(other(along_z(1))), U1, sib)
    arrived(sb8, rsib(other(along_z(2))), V1, sib)
    write_lists(table_v, pair_lists(rows_ref, cols_ref), 0)
    hand = pltpu.make_async_copy(table_v, table_ref, own_sems.at[2])
    hand.start()
    arrived(gzn, yy_r, V4, zp)
    sb10 = send(yy_r, yy_r, V4, sib)
    arrived(gzq, yy_r, V2, zm)
    sb11 = send(yy_r, yy_r, V2, sib)

    arrived(yxp2, ym_c, W2, xm)
    arrived(uxp, yp_c, K, hi)
    arrived(uxm, ym_c, K, hi)
    arrived(uxx, yy_c, K, hi)
    arrived(gxm, yy_c, W2, xp)
    arrived(gxq, yy_c, V2, xm)
    arrived(sb6, rsib(other(along_z(1))), U2, sib)
    arrived(sb12, rsib(other(along_z(1))), L, sib)
    arrived(sb13, rsib(other(along_z(3))), L, sib)
    arrived(sb15, rsib(other(along_z(3))), U2, sib)
    arrived(sb7, rsib(other(along_z(2))), L, sib)
    arrived(sb9, rsib(other(along_z(2))), V3, sib)
    arrived(sb10, rsib(other(along_z(2))), V4, sib)
    arrived(sb11, rsib(other(along_z(2))), V2, sib)
    assert waited == set(range(len(started))) and len(started) == COPIES
    for part, wait in started:
        either(part, wait)
    hand.wait()


COPIES = 58


def gather(block_mask, similarity):
    dtype = similarity.dtype
    cells = block_mask.size
    return pl.pallas_call(
        gather_kernel,
        out_shape=[
            pltpu.VMEM((17, SHARE, BLK), dtype),
            pltpu.VMEM((8, SHARE, BLK), dtype),
            pltpu.SMEM((DEPTH, BLK), jnp.int32),
        ],
        in_specs=[pl.BlockSpec(memory_space=pltpu.HBM)] * 2,
        out_specs=[
            pl.BlockSpec(memory_space=pltpu.VMEM),
            pl.BlockSpec(memory_space=pltpu.VMEM),
            pl.BlockSpec(memory_space=pltpu.SMEM),
        ],
        scratch_shapes=[
            pltpu.SMEM(block_mask.shape[::-1], jnp.int32),
            pltpu.VMEM((cells, BLK, BLK), dtype),
            pltpu.VMEM((SHARE, BLK), dtype),
            pltpu.VMEM((3, LAST_C * BLK, BLK), dtype),
            pltpu.VMEM((8, BLK), jnp.int32),
            pltpu.SMEM((8, BLK), jnp.int32),
            pltpu.SemaphoreType.DMA((COPIES,)),
            pltpu.SemaphoreType.DMA((COPIES,)),
            pltpu.SemaphoreType.DMA((3,)),
            pltpu.SemaphoreType.DMA((8,)),
            pltpu.VMEM((DEPTH, BLK), jnp.int32),
        ],
        compiler_params=pltpu.CompilerParams(
            collective_id=0, has_side_effects=True, vmem_limit_bytes=44 * MIB
        ),
        name="gather",
    )(block_mask.T, similarity)


def group_product(r_ref, c_ref, table, cell, g):
    words = [table[g * GROUP + t, cell] for t in range(GROUP)]
    return sum(
        jnp.dot(
            r_ref[(word >> 8) & 511],
            c_ref[word & 255],
            preferred_element_type=jnp.float32,
        )
        for word in words
    )


def as_blocks(ref):
    return ref.reshape(ref.shape[0] * SLOTS, BLK, BLK)


AT_ONCE = 4


def later_kernel(rows_ref, cols_ref, table_ref, extra_ref, table_v, table_s, list_s, sem):
    r_ref, c_ref = as_blocks(rows_ref), as_blocks(cols_ref)
    cells = extra_ref.shape[0] - 1

    def look(cell, found):
        list_s[found] = cell
        return found + jnp.where(length_of(table_ref, cell) > GROUP, 1, 0)

    found = lax.fori_loop(0, cells, look, jnp.int32(0), unroll=8)
    for t in range(AT_ONCE):
        list_s[found + t] = cells

    @pl.loop(0, (found + AT_ONCE - 1) // AT_ONCE)
    def _(n):
        for t in range(AT_ONCE):
            cell = list_s[n * AT_ONCE + t]
            extra_ref[cell] = group_product(r_ref, c_ref, table_ref, cell, 1)

    def add(table, cell, first):
        @pl.loop(first, (jnp.minimum(length_of(table, cell), DEPTH) + GROUP - 1) // GROUP)
        def _(g):
            extra_ref[cell] += group_product(r_ref, c_ref, table, cell, g)

    most = length_of(table_ref, BLK - 1)

    @pl.when(most > 2 * GROUP)
    def _():
        @pl.loop(0, found)
        def _(n):
            add(table_ref, list_s[n], 2)

    @pl.loop(1, (most + DEPTH - 1) // DEPTH)
    def _(d):
        write_lists(table_v, pair_lists(rows_ref, cols_ref), d * DEPTH)
        copy = pltpu.make_async_copy(table_v, table_s, sem)
        copy.start()
        copy.wait()

        @pl.loop(0, found)
        def _(n):
            add(table_s, list_s[n], 0)


VMEM, SMEM = pl.BlockSpec(memory_space=pltpu.VMEM), pl.BlockSpec(memory_space=pltpu.SMEM)


def later(rows, cols, table, cells):
    return pl.pallas_call(
        later_kernel,
        out_shape=pltpu.VMEM((cells + 1, BLK, BLK), jnp.float32),
        in_specs=[VMEM, VMEM, SMEM],
        out_specs=VMEM,
        scratch_shapes=[
            pltpu.VMEM(table.shape, jnp.int32),
            pltpu.SMEM(table.shape, jnp.int32),
            pltpu.SMEM((BLK,), jnp.int32),
            pltpu.SemaphoreType.DMA(()),
        ],
        compiler_params=pltpu.CompilerParams(vmem_limit_bytes=8 * MIB),
        name="later",
    )(rows, cols, table)


def product_kernel(
    rows_ref, cols_ref, table_ref, extra_ref, out_ref, total_ref, slots, send_sems, recv_sems
):
    row, col, layer = (lax.axis_index(a) for a in ("row", "col", "layer"))
    high, x = row // 4, row % 4
    steps = [(1, 2), (1, 1), (1, 3), (1, 0), (0, 2), (0, 1), (0, 3)]
    peers = [((high + h) % 2 * 4 + (x + d) % 4, col, layer) for h, d in steps]
    barrier = pltpu.get_barrier_semaphore()
    for peer in peers:
        pl.semaphore_signal(barrier, inc=1, device_id=peer, device_id_type=MESH)

    r_ref, c_ref = as_blocks(rows_ref), as_blocks(cols_ref)
    tiles, wide = out_ref.shape[0] // BLK, out_ref.shape[1] // BLK

    def one_row(i, sums):
        lines = pl.ds(pl.multiple_of(i * BLK, BLK), BLK)
        out = []
        for j in range(wide):
            cell = i * wide + j
            value = group_product(r_ref, c_ref, table_ref, cell, 0)
            has_more = jnp.full((BLK, BLK), length_of(table_ref, cell), jnp.int32) > GROUP
            value = value + jnp.where(has_more, extra_ref[cell], 0.0)
            value = value * value
            out_ref[lines, pl.ds(j * BLK, BLK)] = value
            out.append(sums[j] + jnp.sum(value.reshape(BLK // 8, 8, BLK), axis=0))
        return tuple(out)

    sums = tuple(jnp.zeros((8, BLK), jnp.float32) for _ in range(wide))
    sums = lax.fori_loop(0, tiles, one_row, sums, unroll=6)
    slots[row] = jnp.concatenate([jnp.sum(v, axis=0, keepdims=True) for v in sums], 1)
    pl.semaphore_wait(barrier, 7)
    copies = [
        pltpu.make_async_remote_copy(
            src_ref=slots.at[row],
            dst_ref=slots.at[row],
            send_sem=send_sems.at[k],
            recv_sem=recv_sems.at[k],
            device_id=peer,
            device_id_type=MESH,
        )
        for k, peer in enumerate(peers)
    ]
    for copy in copies:
        copy.start()
    for copy in copies:
        copy.wait()
    total = slots[0]
    for q in range(1, 8):
        total = total + slots[q]
    total_ref[...] = total


def product(rows, cols, table, extra, shape):
    lanes = shape[1]
    return pl.pallas_call(
        product_kernel,
        out_shape=[pltpu.VMEM(shape, jnp.float32), pltpu.VMEM((1, lanes), jnp.float32)],
        in_specs=[VMEM, VMEM, SMEM, VMEM],
        out_specs=[VMEM, VMEM],
        scratch_shapes=[
            pltpu.VMEM((8, 1, lanes), jnp.float32),
            pltpu.SemaphoreType.DMA((7,)),
            pltpu.SemaphoreType.DMA((7,)),
        ],
        compiler_params=pltpu.CompilerParams(
            collective_id=1, has_side_effects=True, vmem_limit_bytes=8 * MIB
        ),
        name="product",
    )(rows, cols, table, extra)


STEPS = 6


def scale_kernel(scaling, value_ref, total_ref, out_ref, staged, sems):
    step = staged.shape[1]
    factor = scaling / total_ref[...]
    copies = []
    for t in range(STEPS):
        here = pl.ds(t * step, step)
        staged[t] = value_ref[here, :] * factor
        copy = pltpu.make_async_copy(staged.at[t], out_ref.at[here], sems.at[t])
        copy.start()
        copies.append(copy)
    for copy in copies:
        copy.wait()


def scale(value, total, scaling):
    rows, lanes = value.shape
    return pl.pallas_call(
        functools.partial(scale_kernel, scaling),
        out_shape=jax.ShapeDtypeStruct(value.shape, jnp.float32),
        in_specs=[pl.BlockSpec(memory_space=pltpu.VMEM)] * 2,
        out_specs=pl.BlockSpec(memory_space=pltpu.HBM),
        scratch_shapes=[
            pltpu.VMEM((STEPS, rows // STEPS, lanes), jnp.float32),
            pltpu.SemaphoreType.DMA((STEPS,)),
        ],
        compiler_params=pltpu.CompilerParams(vmem_limit_bytes=16 * MIB),
        name="scale",
    )(value, total)


def body(similarity, block_mask):
    rows, cols, table = gather(block_mask, similarity)
    extra = later(rows, cols, table, block_mask.size)
    value, total = product(rows, cols, table, extra, similarity.shape)
    scaling = similarity.shape[0] * lax.axis_size("row")
    return scale(value, total, float(scaling))


def solution(mesh):
    return jax.shard_map(
        body,
        mesh=mesh,
        in_specs=(P("row", ("col", "layer")), P("row", ("col", "layer"))),
        out_specs=P("row", ("col", "layer")),
        check_vma=False,
    )
```

```python
import functools

import jax
import jax.numpy as jnp
from jax import lax
from jax.experimental import pallas as pl
from jax.experimental.pallas import tpu as pltpu
from jax.sharding import PartitionSpec as P

BLK = 128
MAXNZ = 18
HEAD = 32
HALF_Z = 8
HALF_X = 9
SLOTS = MAXNZ + 1
SHARE = SLOTS * BLK
TOP = BLK - HEAD
GROUP = 4
DEPTH = 16
FIELD = 256
COUNT = 512 * FIELD
MIB = 1 << 20
MESH = pl.DeviceIdType.MESH


def pack_share(mask_ref, x_ref, mask_s, x_v, share, place_v, place_s, signal, sems):
    cols, rows = mask_ref.shape
    fetch = pltpu.make_async_copy(mask_ref, mask_s, sems.at[cols + 1])
    fetch.start()
    strips = x_v.reshape(cols * rows * BLK, BLK)
    loads = [
        pltpu.make_async_copy(
            x_ref.at[:, pl.ds(j * BLK, BLK)],
            strips.at[pl.ds(j * rows * BLK, rows * BLK)],
            sems.at[j],
        )
        for j in range(cols)
    ]
    for load in loads:
        load.start()
    signal()
    sub = lax.broadcasted_iota(jnp.int32, (HEAD, BLK), 0)
    lane = lax.broadcasted_iota(jnp.int32, (HEAD, BLK), 1)
    lane_row = (lane * 43) >> 8
    lane_col = lane - lane_row * cols
    lane8 = lane[:8]

    def find(i, carry):
        count, place = carry
        for j in range(cols):
            here = mask_s[j, i]
            place = place + jnp.where(lane8 == count, here * (j * rows + i), 0)
            count = count + here
        return count, place

    fetch.wait()
    zero = jnp.int32(0)
    _, place = lax.fori_loop(0, rows, find, (zero, jnp.zeros((8, BLK), jnp.int32)), unroll=3)
    place_v[...] = place
    move = pltpu.make_async_copy(place_v, place_s, sems.at[cols])
    move.start()

    def mark(i, carry):
        count, head = carry
        below = 8 + jnp.where(i < cols, i, i - cols + 8)
        for j in range(cols):
            here = mask_s[j, i]
            cell = ((sub == j) & (lane_row == i)) | ((sub == below) & (lane_col == j))
            head = head + jnp.where(cell, here * (count + 1), 0)
            count = count + here
        return count, head

    _, head = lax.fori_loop(0, rows, mark, (zero, jnp.zeros((HEAD, BLK), jnp.int32)))
    head = jnp.where(lane < rows * cols, head, 0)
    share[pl.ds(TOP, HEAD), :] = head.astype(jnp.float32).astype(share.dtype)
    move.wait()
    for load in loads:
        load.wait()
    for s in range(MAXNZ):
        share[pl.ds((s + 1) * BLK, BLK), :] = x_v[place_s[0, s]]


def pair_lists(rows_ref, cols_ref):
    hr, hc = [], []
    for q in range(16):
        hr.append(rows_ref[q, pl.ds(TOP, HEAD), :].astype(jnp.float32)[0:8])
    for q in range(8):
        top = cols_ref[q, pl.ds(TOP, HEAD), :].astype(jnp.float32)
        hc += [top[8:16], top[16:24]]
    hr, hc = jnp.concatenate(hr, 0), jnp.concatenate(hc, 0)
    both = jnp.where((hr > 0) & (hc > 0), 1.0, 0.0)
    line = lax.broadcasted_iota(jnp.int32, (BLK, BLK), 0)
    before = line > lax.broadcasted_iota(jnp.int32, (BLK, BLK), 1)
    rank = jnp.dot(
        jnp.where(before, 1.0, 0.0).astype(jnp.bfloat16),
        both.astype(jnp.bfloat16),
        preferred_element_type=jnp.float32,
    )
    rank = jnp.where(both > 0, rank, -1.0).astype(jnp.int32)
    place_r = (line >> 3) * SLOTS + hr.astype(jnp.int32)
    place_c = (line >> 4) * SLOTS + hc.astype(jnp.int32)
    count = jnp.sum(both, axis=0, keepdims=True).astype(jnp.int32)
    return rank, place_r * FIELD + place_c, count


def write_lists(table_v, lists, done):
    rank, place, count = lists
    most = jnp.max(count, axis=1, keepdims=True)
    lane = lax.broadcasted_iota(jnp.int32, count.shape, 1)
    for p in range(DEPTH):
        one = jnp.sum(jnp.where(rank == done + p, place, 0), axis=0, keepdims=True)
        one = jnp.where(count > done + p, one, IDLE)
        if p == 0:
            length = jnp.where(lane == BLK - 1, most, jnp.maximum(count - done, 0))
            one = one + COUNT * length
        table_v[pl.ds(p, 1), :] = one


IDLE = 16 * SLOTS * FIELD + 1


def length_of(table, cell):
    return table[0, cell] >> 17


LAST_R = 5
LAST_C = 4.5
SPLIT = 6.5
SHIFT_Z = 2
SHIFT_X = 1


def span(first, last):
    low = int((first + 1) * BLK) if first else TOP
    return pl.ds(low, int((last + 1) * BLK) - low)


def gather_kernel(
    mask_ref,
    x_ref,
    rows_ref,
    cols_ref,
    table_ref,
    mask_s,
    x_v,
    share_ref,
    relay,
    place_v,
    place_s,
    send_sems,
    recv_sems,
    own_sems,
    pack_sems,
    table_v,
):
    row, col, layer = (lax.axis_index(a) for a in ("row", "col", "layer"))
    high, x = row // 4, row % 4
    z, low = col // 2, col % 2

    def along_z(step):
        return 2 * ((z + step) % 4) + low

    def along_x(step):
        return 4 * high + (x + step) % 4

    mate = 2 * z + 1 - low
    far = 4 * (1 - high) + x

    zp, zm = (row, along_z(1), layer), (row, along_z(3), layer)
    xp, xm = (along_x(1), col, layer), (along_x(3), col, layer)
    lo, hi = (row, mate, layer), (far, mate, layer)
    sib = (row, col, 1 - layer)

    barrier = pltpu.get_barrier_semaphore()

    def signal():
        for peer in (zp, zm, xp, xm, lo, hi, sib):
            pl.semaphore_signal(barrier, inc=1, device_id=peer, device_id_type=MESH)

    pack_share(mask_ref, x_ref, mask_s, x_v, share_ref, place_v, place_s, signal, pack_sems)
    pl.semaphore_wait(barrier, 7)

    ALL = span(0, MAXNZ)
    mine = 2 * col + layer
    keep = [
        pltpu.make_async_copy(share_ref.at[ALL], rows_ref.at[mine].at[ALL], own_sems.at[0]),
        pltpu.make_async_copy(share_ref.at[ALL], cols_ref.at[row].at[ALL], own_sems.at[1]),
    ]

    EARLY, EARLY_C = MAXNZ - LAST_R, MAXNZ - LAST_C
    U1, U2, L = span(0, SPLIT), span(SPLIT, EARLY), span(EARLY, MAXNZ)
    V1, V2, V3, V4 = span(0, 4), span(4, SPLIT), span(SPLIT, 10), span(10, EARLY)
    W2, K = span(SPLIT, EARLY_C), span(EARLY_C, MAXNZ)
    T = pl.ds(0, int(LAST_C * BLK))
    started = []
    waited = set()

    def either(part, act):
        if isinstance(part, tuple):
            flag, held, plain = part
            pl.when(flag)(lambda: act(held))
            pl.when(jnp.logical_not(flag))(lambda: act(plain))
        else:
            act(part)

    def copy_of(k, src, dst, part, into, peer):
        return pltpu.make_async_remote_copy(
            src_ref=src.at[part],
            dst_ref=dst.at[part if into is None else into],
            send_sem=send_sems.at[k],
            recv_sem=recv_sems.at[k],
            device_id=peer,
            device_id_type=MESH,
        )

    def send(src, dst, part, peer, into=None):
        k = len(started)
        either(part, lambda p: copy_of(k, src, dst, p, into, peer).start())
        started.append((part, lambda p: copy_of(k, src, dst, p, into, peer).wait_send()))
        return k

    def arrived(k, dst, part, peer):
        waited.add(k)
        either(part, lambda p: copy_of(k, dst, dst, p, None, peer).wait_recv())

    def halves(place, half, shift):
        cut = half - shift
        pairs = []
        for step in (0, 3, 1, 2):
            flag = (place + step) % 4 == 2
            first = (flag, span(0, cut), span(0, half))
            pairs.append((first, (flag, span(cut, MAXNZ), span(half, MAXNZ))))
        return pairs

    (A1, A2), (M1, M2), (P1, P2), (F1, F2) = halves(z, HALF_Z, SHIFT_Z)
    (B1, B2), (N1, N2), (Q1, Q2), (G1, G2) = halves(x, HALF_X, SHIFT_X)

    def other(q):
        return q + 1 - 2 * (q % 2)

    def r(q):
        return rows_ref.at[2 * q + layer]

    def rsib(q):
        return rows_ref.at[2 * q + 1 - layer]

    def c(q):
        return cols_ref.at[q]

    def across(q):
        return c((q + 4) % 8)

    own_r, own_c = r(col), c(row)
    y_r, y_c = r(mate), c(far)
    zm_r, zp_r, zz_r = (r(along_z(s)) for s in (3, 1, 2))
    ym_r, yp_r, yy_r = (r(other(along_z(s))) for s in (3, 1, 2))
    xm_c, xp_c, xx_c = (c(along_x(s)) for s in (3, 1, 2))
    ym_c, yp_c, yy_c = (across(along_x(s)) for s in (3, 1, 2))

    lo1 = send(share_ref, own_r, U1, lo)
    zp1 = send(share_ref, own_r, A1, zp)
    zm2 = send(share_ref, own_r, A2, zm)
    xp1 = send(share_ref, own_c, B1, xp)
    xm2 = send(share_ref, own_c, B2, xm)
    lo2 = send(share_ref, own_r, U2, lo)
    zp2 = send(share_ref, own_r, A2, zp)
    zm1 = send(share_ref, own_r, A1, zm)
    xp2 = send(share_ref, own_c, B2, xp)
    xm1 = send(share_ref, own_c, B1, xm)
    lo3 = send(share_ref, own_r, L, lo)
    sb0 = send(share_ref, own_r, ALL, sib)
    for copy in keep:
        copy.start()
    rows_ref[16, pl.ds(0, BLK), :] = jnp.zeros((BLK, BLK), rows_ref.dtype)

    arrived(lo1, y_r, U1, lo)
    hi1 = send(y_r, own_c, U1, hi)
    yzp1 = send(y_r, y_r, U1, zp)
    arrived(zp1, zm_r, M1, zm)
    fzp = send(zm_r, zm_r, M1, zp)
    arrived(zm2, zp_r, P2, zp)
    fzm = send(zp_r, zp_r, P2, zm)
    arrived(xp1, xm_c, N1, xm)
    fxp = send(xm_c, xm_c, N1, xp)
    arrived(xm2, xp_c, Q2, xp)
    fxm = send(xp_c, xp_c, Q2, xm)
    txp = send(xp_c, relay.at[0], K, lo, T)
    lzp = send(zp_r, zp_r, L, lo)
    arrived(lo2, y_r, U2, lo)
    hi2 = send(y_r, own_c, U2, hi)
    yzm2 = send(y_r, y_r, U2, zm)
    yzp2 = send(y_r, y_r, U2, zp)
    yzm1 = send(y_r, y_r, U1, zm)
    arrived(hi1, y_c, U1, hi)
    yxp1 = send(y_c, y_c, U1, xp)
    arrived(lo3, y_r, L, lo)
    hi3 = send(y_r, own_c, L, hi)
    sb1 = send(y_r, y_r, ALL, sib)

    arrived(zp2, zm_r, M2, zm)
    arrived(xp2, xm_c, N2, xm)
    txm = send(xm_c, relay.at[1], K, lo, T)
    lzm = send(zm_r, zm_r, L, lo)
    sb2 = send(zm_r, zm_r, ALL, sib)
    arrived(zm1, zp_r, P1, zp)
    sb3 = send(zp_r, zp_r, ALL, sib)
    arrived(hi2, y_c, U2, hi)
    arrived(hi3, y_c, L, hi)
    yxm2 = send(y_c, y_c, W2, xm)
    yxp2 = send(y_c, y_c, W2, xp)
    yxm1 = send(y_c, y_c, U1, xm)
    arrived(txp, relay.at[0], T, lo)
    uxp = send(relay.at[0], xp_c, T, hi, K)
    arrived(fxm, xx_c, G2, xp)
    txx = send(xx_c, relay.at[2], K, lo, T)
    arrived(fzm, zz_r, F2, zp)
    lzz = send(zz_r, zz_r, L, lo)
    arrived(fzp, zz_r, F1, zm)
    sb4 = send(zz_r, zz_r, ALL, sib)
    arrived(txm, relay.at[1], T, lo)
    uxm = send(relay.at[1], xm_c, T, hi, K)

    arrived(yzp1, ym_r, U1, zm)
    gzp = send(ym_r, ym_r, V1, zp)
    gzq = send(ym_r, ym_r, V2, zp)
    arrived(yzm2, yp_r, U2, zp)
    gzm = send(yp_r, yp_r, V3, zm)
    gzn = send(yp_r, yp_r, V4, zm)
    arrived(yxp1, ym_c, U1, xm)
    gxp = send(ym_c, ym_c, V1, xp)
    gxq = send(ym_c, ym_c, V2, xp)
    arrived(yxm2, yp_c, W2, xp)
    gxm = send(yp_c, yp_c, W2, xm)
    sb5 = send(ym_r, ym_r, U1, sib)
    sb6 = send(yp_r, yp_r, U2, sib)
    arrived(lzp, yp_r, L, lo)
    sb12 = send(yp_r, yp_r, L, sib)
    arrived(lzm, ym_r, L, lo)
    sb13 = send(ym_r, ym_r, L, sib)
    arrived(txx, relay.at[2], T, lo)
    uxx = send(relay.at[2], xx_c, T, hi, K)
    arrived(yzm1, yp_r, U1, zp)
    sb14 = send(yp_r, yp_r, U1, sib)
    arrived(yzp2, ym_r, U2, zm)
    sb15 = send(ym_r, ym_r, U2, sib)
    arrived(lzz, yy_r, L, lo)
    sb7 = send(yy_r, yy_r, L, sib)
    for copy in keep:
        copy.wait()
    arrived(xm1, xp_c, Q1, xp)
    arrived(fxp, xx_c, G1, xm)
    arrived(yxm1, yp_c, U1, xp)
    arrived(sb0, rsib(col), ALL, sib)
    arrived(sb1, rsib(mate), ALL, sib)
    arrived(sb2, rsib(along_z(3)), ALL, sib)
    arrived(sb3, rsib(along_z(1)), ALL, sib)
    arrived(gzp, yy_r, V1, zm)
    sb8 = send(yy_r, yy_r, V1, sib)
    arrived(gzm, yy_r, V3, zp)
    sb9 = send(yy_r, yy_r, V3, sib)
    arrived(gxp, yy_c, V1, xm)
    arrived(sb4, rsib(along_z(2)), ALL, sib)
    arrived(sb5, rsib(other(along_z(3))), U1, sib)
    arrived(sb14, rsib(other(along_z(1))), U1, sib)
    arrived(sb8, rsib(other(along_z(2))), V1, sib)
    write_lists(table_v, pair_lists(rows_ref, cols_ref), 0)
    hand = pltpu.make_async_copy(table_v, table_ref, own_sems.at[2])
    hand.start()
    arrived(gzn, yy_r, V4, zp)
    sb10 = send(yy_r, yy_r, V4, sib)
    arrived(gzq, yy_r, V2, zm)
    sb11 = send(yy_r, yy_r, V2, sib)

    arrived(yxp2, ym_c, W2, xm)
    arrived(uxp, yp_c, K, hi)
    arrived(uxm, ym_c, K, hi)
    arrived(uxx, yy_c, K, hi)
    arrived(gxm, yy_c, W2, xp)
    arrived(gxq, yy_c, V2, xm)
    arrived(sb6, rsib(other(along_z(1))), U2, sib)
    arrived(sb12, rsib(other(along_z(1))), L, sib)
    arrived(sb13, rsib(other(along_z(3))), L, sib)
    arrived(sb15, rsib(other(along_z(3))), U2, sib)
    arrived(sb7, rsib(other(along_z(2))), L, sib)
    arrived(sb9, rsib(other(along_z(2))), V3, sib)
    arrived(sb10, rsib(other(along_z(2))), V4, sib)
    arrived(sb11, rsib(other(along_z(2))), V2, sib)
    assert waited == set(range(len(started))) and len(started) == COPIES
    for part, wait in started:
        either(part, wait)
    hand.wait()


COPIES = 58


def gather(block_mask, similarity):
    dtype = similarity.dtype
    cells = block_mask.size
    return pl.pallas_call(
        gather_kernel,
        out_shape=[
            pltpu.VMEM((17, SHARE, BLK), dtype),
            pltpu.VMEM((8, SHARE, BLK), dtype),
            pltpu.SMEM((DEPTH, BLK), jnp.int32),
        ],
        in_specs=[pl.BlockSpec(memory_space=pltpu.HBM)] * 2,
        out_specs=[
            pl.BlockSpec(memory_space=pltpu.VMEM),
            pl.BlockSpec(memory_space=pltpu.VMEM),
            pl.BlockSpec(memory_space=pltpu.SMEM),
        ],
        scratch_shapes=[
            pltpu.SMEM(block_mask.shape[::-1], jnp.int32),
            pltpu.VMEM((cells, BLK, BLK), dtype),
            pltpu.VMEM((SHARE, BLK), dtype),
            pltpu.VMEM((3, int(LAST_C * BLK), BLK), dtype),
            pltpu.VMEM((8, BLK), jnp.int32),
            pltpu.SMEM((8, BLK), jnp.int32),
            pltpu.SemaphoreType.DMA((COPIES,)),
            pltpu.SemaphoreType.DMA((COPIES,)),
            pltpu.SemaphoreType.DMA((3,)),
            pltpu.SemaphoreType.DMA((8,)),
            pltpu.VMEM((DEPTH, BLK), jnp.int32),
        ],
        compiler_params=pltpu.CompilerParams(
            collective_id=0, has_side_effects=True, vmem_limit_bytes=44 * MIB
        ),
        name="gather",
    )(block_mask.T, similarity)


def group_product(r_ref, c_ref, table, cell, g):
    words = [table[g * GROUP + t, cell] for t in range(GROUP)]
    return sum(
        jnp.dot(
            r_ref[(word >> 8) & 511],
            c_ref[word & 255],
            preferred_element_type=jnp.float32,
        )
        for word in words
    )


def as_blocks(ref):
    return ref.reshape(ref.shape[0] * SLOTS, BLK, BLK)


AT_ONCE = 4


def later_kernel(rows_ref, cols_ref, table_ref, extra_ref, table_v, table_s, list_s, sem):
    r_ref, c_ref = as_blocks(rows_ref), as_blocks(cols_ref)
    cells = extra_ref.shape[0] - 1

    def look(cell, found):
        list_s[found] = cell
        return found + jnp.where(length_of(table_ref, cell) > GROUP, 1, 0)

    found = lax.fori_loop(0, cells, look, jnp.int32(0), unroll=8)
    for t in range(AT_ONCE):
        list_s[found + t] = cells

    @pl.loop(0, (found + AT_ONCE - 1) // AT_ONCE)
    def _(n):
        for t in range(AT_ONCE):
            cell = list_s[n * AT_ONCE + t]
            extra_ref[cell] = group_product(r_ref, c_ref, table_ref, cell, 1)

    def add(table, cell, first):
        @pl.loop(first, (jnp.minimum(length_of(table, cell), DEPTH) + GROUP - 1) // GROUP)
        def _(g):
            extra_ref[cell] += group_product(r_ref, c_ref, table, cell, g)

    most = length_of(table_ref, BLK - 1)

    @pl.when(most > 2 * GROUP)
    def _():
        @pl.loop(0, found)
        def _(n):
            add(table_ref, list_s[n], 2)

    @pl.loop(1, (most + DEPTH - 1) // DEPTH)
    def _(d):
        write_lists(table_v, pair_lists(rows_ref, cols_ref), d * DEPTH)
        copy = pltpu.make_async_copy(table_v, table_s, sem)
        copy.start()
        copy.wait()

        @pl.loop(0, found)
        def _(n):
            add(table_s, list_s[n], 0)


VMEM, SMEM = pl.BlockSpec(memory_space=pltpu.VMEM), pl.BlockSpec(memory_space=pltpu.SMEM)


def later(rows, cols, table, cells):
    return pl.pallas_call(
        later_kernel,
        out_shape=pltpu.VMEM((cells + 1, BLK, BLK), jnp.float32),
        in_specs=[VMEM, VMEM, SMEM],
        out_specs=VMEM,
        scratch_shapes=[
            pltpu.VMEM(table.shape, jnp.int32),
            pltpu.SMEM(table.shape, jnp.int32),
            pltpu.SMEM((BLK,), jnp.int32),
            pltpu.SemaphoreType.DMA(()),
        ],
        compiler_params=pltpu.CompilerParams(vmem_limit_bytes=8 * MIB),
        name="later",
    )(rows, cols, table)


def product_kernel(
    rows_ref, cols_ref, table_ref, extra_ref, out_ref, total_ref, slots, send_sems, recv_sems
):
    row, col, layer = (lax.axis_index(a) for a in ("row", "col", "layer"))
    high, x = row // 4, row % 4
    steps = [(1, 2), (1, 1), (1, 3), (1, 0), (0, 2), (0, 1), (0, 3)]
    peers = [((high + h) % 2 * 4 + (x + d) % 4, col, layer) for h, d in steps]
    barrier = pltpu.get_barrier_semaphore()
    for peer in peers:
        pl.semaphore_signal(barrier, inc=1, device_id=peer, device_id_type=MESH)

    r_ref, c_ref = as_blocks(rows_ref), as_blocks(cols_ref)
    tiles, wide = out_ref.shape[0] // BLK, out_ref.shape[1] // BLK

    def one_row(i, sums):
        lines = pl.ds(pl.multiple_of(i * BLK, BLK), BLK)
        out = []
        for j in range(wide):
            cell = i * wide + j
            value = group_product(r_ref, c_ref, table_ref, cell, 0)
            has_more = jnp.full((BLK, BLK), length_of(table_ref, cell), jnp.int32) > GROUP
            value = value + jnp.where(has_more, extra_ref[cell], 0.0)
            value = value * value
            out_ref[lines, pl.ds(j * BLK, BLK)] = value
            out.append(sums[j] + jnp.sum(value.reshape(BLK // 8, 8, BLK), axis=0))
        return tuple(out)

    sums = tuple(jnp.zeros((8, BLK), jnp.float32) for _ in range(wide))
    sums = lax.fori_loop(0, tiles, one_row, sums, unroll=6)
    slots[row] = jnp.concatenate([jnp.sum(v, axis=0, keepdims=True) for v in sums], 1)
    pl.semaphore_wait(barrier, 7)
    copies = [
        pltpu.make_async_remote_copy(
            src_ref=slots.at[row],
            dst_ref=slots.at[row],
            send_sem=send_sems.at[k],
            recv_sem=recv_sems.at[k],
            device_id=peer,
            device_id_type=MESH,
        )
        for k, peer in enumerate(peers)
    ]
    for copy in copies:
        copy.start()
    for copy in copies:
        copy.wait()
    total = slots[0]
    for q in range(1, 8):
        total = total + slots[q]
    total_ref[...] = total


def product(rows, cols, table, extra, shape):
    lanes = shape[1]
    return pl.pallas_call(
        product_kernel,
        out_shape=[pltpu.VMEM(shape, jnp.float32), pltpu.VMEM((1, lanes), jnp.float32)],
        in_specs=[VMEM, VMEM, SMEM, VMEM],
        out_specs=[VMEM, VMEM],
        scratch_shapes=[
            pltpu.VMEM((8, 1, lanes), jnp.float32),
            pltpu.SemaphoreType.DMA((7,)),
            pltpu.SemaphoreType.DMA((7,)),
        ],
        compiler_params=pltpu.CompilerParams(
            collective_id=1, has_side_effects=True, vmem_limit_bytes=8 * MIB
        ),
        name="product",
    )(rows, cols, table, extra)


STEPS = 6


def scale_kernel(scaling, value_ref, total_ref, out_ref, staged, sems):
    step = staged.shape[1]
    factor = scaling / total_ref[...]
    copies = []
    for t in range(STEPS):
        here = pl.ds(t * step, step)
        staged[t] = value_ref[here, :] * factor
        copy = pltpu.make_async_copy(staged.at[t], out_ref.at[here], sems.at[t])
        copy.start()
        copies.append(copy)
    for copy in copies:
        copy.wait()


def scale(value, total, scaling):
    rows, lanes = value.shape
    return pl.pallas_call(
        functools.partial(scale_kernel, scaling),
        out_shape=jax.ShapeDtypeStruct(value.shape, jnp.float32),
        in_specs=[pl.BlockSpec(memory_space=pltpu.VMEM)] * 2,
        out_specs=pl.BlockSpec(memory_space=pltpu.HBM),
        scratch_shapes=[
            pltpu.VMEM((STEPS, rows // STEPS, lanes), jnp.float32),
            pltpu.SemaphoreType.DMA((STEPS,)),
        ],
        compiler_params=pltpu.CompilerParams(vmem_limit_bytes=16 * MIB),
        name="scale",
    )(value, total)


def body(similarity, block_mask):
    rows, cols, table = gather(block_mask, similarity)
    extra = later(rows, cols, table, block_mask.size)
    value, total = product(rows, cols, table, extra, similarity.shape)
    scaling = similarity.shape[0] * lax.axis_size("row")
    return scale(value, total, float(scaling))


def solution(mesh):
    return jax.shard_map(
        body,
        mesh=mesh,
        in_specs=(P("row", ("col", "layer")), P("row", ("col", "layer"))),
        out_specs=P("row", ("col", "layer")),
        check_vma=False,
    )
```

```python
import functools

import jax
import jax.numpy as jnp
from jax import lax
from jax.experimental import pallas as pl
from jax.experimental.pallas import tpu as pltpu
from jax.sharding import PartitionSpec as P

BLK = 128
MAXNZ = 18
HEAD = 32
HALF = MAXNZ // 2
SLOTS = MAXNZ + 1
SHARE = SLOTS * BLK
TOP = BLK - HEAD
GROUP = 4
DEPTH = 16
FIELD = 256
COUNT = 512 * FIELD
MIB = 1 << 20
MESH = pl.DeviceIdType.MESH


def pack_share(mask_ref, x_ref, mask_s, x_v, share, place_v, place_s, signal, sems):
    cols, rows = mask_ref.shape
    fetch = pltpu.make_async_copy(mask_ref, mask_s, sems.at[cols + 1])
    fetch.start()
    strips = x_v.reshape(cols * rows * BLK, BLK)
    loads = [
        pltpu.make_async_copy(
            x_ref.at[:, pl.ds(j * BLK, BLK)],
            strips.at[pl.ds(j * rows * BLK, rows * BLK)],
            sems.at[j],
        )
        for j in range(cols)
    ]
    for load in loads:
        load.start()
    signal()
    sub = lax.broadcasted_iota(jnp.int32, (HEAD, BLK), 0)
    lane = lax.broadcasted_iota(jnp.int32, (HEAD, BLK), 1)
    lane_row = (lane * 43) >> 8
    lane_col = lane - lane_row * cols
    lane8 = lane[:8]

    def find(i, carry):
        count, place = carry
        for j in range(cols):
            here = mask_s[j, i]
            place = place + jnp.where(lane8 == count, here * (j * rows + i), 0)
            count = count + here
        return count, place

    fetch.wait()
    zero = jnp.int32(0)
    _, place = lax.fori_loop(0, rows, find, (zero, jnp.zeros((8, BLK), jnp.int32)), unroll=3)
    place_v[...] = place
    move = pltpu.make_async_copy(place_v, place_s, sems.at[cols])
    move.start()

    def mark(i, carry):
        count, head = carry
        below = 8 + jnp.where(i < cols, i, i - cols + 8)
        for j in range(cols):
            here = mask_s[j, i]
            cell = ((sub == j) & (lane_row == i)) | ((sub == below) & (lane_col == j))
            head = head + jnp.where(cell, here * (count + 1), 0)
            count = count + here
        return count, head

    _, head = lax.fori_loop(0, rows, mark, (zero, jnp.zeros((HEAD, BLK), jnp.int32)))
    head = jnp.where(lane < rows * cols, head, 0)
    share[pl.ds(TOP, HEAD), :] = head.astype(jnp.float32).astype(share.dtype)
    move.wait()
    for load in loads:
        load.wait()
    for s in range(MAXNZ):
        share[pl.ds((s + 1) * BLK, BLK), :] = x_v[place_s[0, s]]


def pair_lists(rows_ref, cols_ref):
    hr, hc = [], []
    for q in range(16):
        hr.append(rows_ref[q, pl.ds(TOP, HEAD), :].astype(jnp.float32)[0:8])
    for q in range(8):
        top = cols_ref[q, pl.ds(TOP, HEAD), :].astype(jnp.float32)
        hc += [top[8:16], top[16:24]]
    hr, hc = jnp.concatenate(hr, 0), jnp.concatenate(hc, 0)
    both = jnp.where((hr > 0) & (hc > 0), 1.0, 0.0)
    line = lax.broadcasted_iota(jnp.int32, (BLK, BLK), 0)
    before = line > lax.broadcasted_iota(jnp.int32, (BLK, BLK), 1)
    rank = jnp.dot(
        jnp.where(before, 1.0, 0.0).astype(jnp.bfloat16),
        both.astype(jnp.bfloat16),
        preferred_element_type=jnp.float32,
    )
    rank = jnp.where(both > 0, rank, -1.0).astype(jnp.int32)
    place_r = (line >> 3) * SLOTS + hr.astype(jnp.int32)
    place_c = (line >> 4) * SLOTS + hc.astype(jnp.int32)
    count = jnp.sum(both, axis=0, keepdims=True).astype(jnp.int32)
    return rank, place_r * FIELD + place_c, count


def write_lists(table_v, lists, done):
    rank, place, count = lists
    most = jnp.max(count, axis=1, keepdims=True)
    lane = lax.broadcasted_iota(jnp.int32, count.shape, 1)
    for p in range(DEPTH):
        one = jnp.sum(jnp.where(rank == done + p, place, 0), axis=0, keepdims=True)
        one = jnp.where(count > done + p, one, IDLE)
        if p == 0:
            length = jnp.where(lane == BLK - 1, most, jnp.maximum(count - done, 0))
            one = one + COUNT * length
        table_v[pl.ds(p, 1), :] = one


IDLE = 16 * SLOTS * FIELD + 1


def length_of(table, cell):
    return table[0, cell] >> 17


LAST_R = 5
LAST_C = 4
SPLIT = 7
SHIFT_Z = 2
SHIFT_X = 1


def span(first, last):
    low = (first + 1) * BLK if first else TOP
    return pl.ds(low, (last + 1) * BLK - low)


def gather_kernel(
    mask_ref,
    x_ref,
    rows_ref,
    cols_ref,
    table_ref,
    mask_s,
    x_v,
    share_ref,
    relay,
    place_v,
    place_s,
    send_sems,
    recv_sems,
    own_sems,
    pack_sems,
    table_v,
):
    row, col, layer = (lax.axis_index(a) for a in ("row", "col", "layer"))
    high, x = row // 4, row % 4
    z, low = col // 2, col % 2

    def along_z(step):
        return 2 * ((z + step) % 4) + low

    def along_x(step):
        return 4 * high + (x + step) % 4

    mate = 2 * z + 1 - low
    far = 4 * (1 - high) + x

    zp, zm = (row, along_z(1), layer), (row, along_z(3), layer)
    xp, xm = (along_x(1), col, layer), (along_x(3), col, layer)
    lo, hi = (row, mate, layer), (far, mate, layer)
    sib = (row, col, 1 - layer)

    barrier = pltpu.get_barrier_semaphore()

    def signal():
        for peer in (zp, zm, xp, xm, lo, hi, sib):
            pl.semaphore_signal(barrier, inc=1, device_id=peer, device_id_type=MESH)

    pack_share(mask_ref, x_ref, mask_s, x_v, share_ref, place_v, place_s, signal, pack_sems)
    pl.semaphore_wait(barrier, 7)

    ALL = span(0, MAXNZ)
    mine = 2 * col + layer
    keep = [
        pltpu.make_async_copy(share_ref.at[ALL], rows_ref.at[mine].at[ALL], own_sems.at[0]),
        pltpu.make_async_copy(share_ref.at[ALL], cols_ref.at[row].at[ALL], own_sems.at[1]),
    ]

    EARLY, EARLY_C = MAXNZ - LAST_R, MAXNZ - LAST_C
    H1, H2 = span(0, HALF), span(HALF, MAXNZ)
    U1, U2, L = span(0, SPLIT), span(SPLIT, EARLY), span(EARLY, MAXNZ)
    V1, V2, V3, V4 = span(0, 4), span(4, SPLIT), span(SPLIT, 10), span(10, EARLY)
    W2, K = span(SPLIT, EARLY_C), span(EARLY_C, MAXNZ)
    T = pl.ds(0, LAST_C * BLK)
    started = []
    waited = set()

    def either(part, act):
        if isinstance(part, tuple):
            flag, held, plain = part
            pl.when(flag)(lambda: act(held))
            pl.when(jnp.logical_not(flag))(lambda: act(plain))
        else:
            act(part)

    def copy_of(k, src, dst, part, into, peer):
        return pltpu.make_async_remote_copy(
            src_ref=src.at[part],
            dst_ref=dst.at[part if into is None else into],
            send_sem=send_sems.at[k],
            recv_sem=recv_sems.at[k],
            device_id=peer,
            device_id_type=MESH,
        )

    def send(src, dst, part, peer, into=None):
        k = len(started)
        either(part, lambda p: copy_of(k, src, dst, p, into, peer).start())
        started.append((part, lambda p: copy_of(k, src, dst, p, into, peer).wait_send()))
        return k

    def arrived(k, dst, part, peer):
        waited.add(k)
        either(part, lambda p: copy_of(k, dst, dst, p, None, peer).wait_recv())

    def halves(place, shift):
        cut = HALF - shift
        pairs = []
        for step in (0, 3, 1, 2):
            flag = (place + step) % 4 == 2
            pairs.append(((flag, span(0, cut), H1), (flag, span(cut, MAXNZ), H2)))
        return pairs

    (A1, A2), (M1, M2), (P1, P2), (F1, F2) = halves(z, SHIFT_Z)
    (B1, B2), (N1, N2), (Q1, Q2), (G1, G2) = halves(x, SHIFT_X)

    def other(q):
        return q + 1 - 2 * (q % 2)

    def r(q):
        return rows_ref.at[2 * q + layer]

    def rsib(q):
        return rows_ref.at[2 * q + 1 - layer]

    def c(q):
        return cols_ref.at[q]

    def across(q):
        return c((q + 4) % 8)

    own_r, own_c = r(col), c(row)
    y_r, y_c = r(mate), c(far)
    zm_r, zp_r, zz_r = (r(along_z(s)) for s in (3, 1, 2))
    ym_r, yp_r, yy_r = (r(other(along_z(s))) for s in (3, 1, 2))
    xm_c, xp_c, xx_c = (c(along_x(s)) for s in (3, 1, 2))
    ym_c, yp_c, yy_c = (across(along_x(s)) for s in (3, 1, 2))

    lo1 = send(share_ref, own_r, U1, lo)
    zp1 = send(share_ref, own_r, A1, zp)
    zm2 = send(share_ref, own_r, A2, zm)
    xp1 = send(share_ref, own_c, B1, xp)
    xm2 = send(share_ref, own_c, B2, xm)
    lo2 = send(share_ref, own_r, U2, lo)
    zp2 = send(share_ref, own_r, A2, zp)
    zm1 = send(share_ref, own_r, A1, zm)
    xp2 = send(share_ref, own_c, B2, xp)
    xm1 = send(share_ref, own_c, B1, xm)
    lo3 = send(share_ref, own_r, L, lo)
    sb0 = send(share_ref, own_r, ALL, sib)
    for copy in keep:
        copy.start()
    rows_ref[16, pl.ds(0, BLK), :] = jnp.zeros((BLK, BLK), rows_ref.dtype)

    arrived(lo1, y_r, U1, lo)
    hi1 = send(y_r, own_c, U1, hi)
    yzp1 = send(y_r, y_r, U1, zp)
    arrived(zp1, zm_r, M1, zm)
    fzp = send(zm_r, zm_r, M1, zp)
    arrived(zm2, zp_r, P2, zp)
    fzm = send(zp_r, zp_r, P2, zm)
    arrived(xp1, xm_c, N1, xm)
    fxp = send(xm_c, xm_c, N1, xp)
    arrived(xm2, xp_c, Q2, xp)
    fxm = send(xp_c, xp_c, Q2, xm)
    txp = send(xp_c, relay.at[0], K, lo, T)
    lzp = send(zp_r, zp_r, L, lo)
    arrived(lo2, y_r, U2, lo)
    hi2 = send(y_r, own_c, U2, hi)
    yzm2 = send(y_r, y_r, U2, zm)
    yzp2 = send(y_r, y_r, U2, zp)
    yzm1 = send(y_r, y_r, U1, zm)
    arrived(hi1, y_c, U1, hi)
    yxp1 = send(y_c, y_c, U1, xp)
    arrived(lo3, y_r, L, lo)
    hi3 = send(y_r, own_c, L, hi)
    sb1 = send(y_r, y_r, ALL, sib)

    arrived(zp2, zm_r, M2, zm)
    arrived(xp2, xm_c, N2, xm)
    txm = send(xm_c, relay.at[1], K, lo, T)
    lzm = send(zm_r, zm_r, L, lo)
    sb2 = send(zm_r, zm_r, ALL, sib)
    arrived(zm1, zp_r, P1, zp)
    sb3 = send(zp_r, zp_r, ALL, sib)
    arrived(hi2, y_c, U2, hi)
    arrived(hi3, y_c, L, hi)
    yxm2 = send(y_c, y_c, W2, xm)
    yxp2 = send(y_c, y_c, W2, xp)
    yxm1 = send(y_c, y_c, U1, xm)
    arrived(txp, relay.at[0], T, lo)
    uxp = send(relay.at[0], xp_c, T, hi, K)
    arrived(fxm, xx_c, G2, xp)
    txx = send(xx_c, relay.at[2], K, lo, T)
    arrived(fzm, zz_r, F2, zp)
    lzz = send(zz_r, zz_r, L, lo)
    arrived(fzp, zz_r, F1, zm)
    sb4 = send(zz_r, zz_r, ALL, sib)
    arrived(txm, relay.at[1], T, lo)
    uxm = send(relay.at[1], xm_c, T, hi, K)

    arrived(yzp1, ym_r, U1, zm)
    gzp = send(ym_r, ym_r, V1, zp)
    gzq = send(ym_r, ym_r, V2, zp)
    arrived(yzm2, yp_r, U2, zp)
    gzm = send(yp_r, yp_r, V3, zm)
    gzn = send(yp_r, yp_r, V4, zm)
    arrived(yxp1, ym_c, U1, xm)
    gxp = send(ym_c, ym_c, V1, xp)
    gxq = send(ym_c, ym_c, V2, xp)
    arrived(yxm2, yp_c, W2, xp)
    gxm = send(yp_c, yp_c, W2, xm)
    sb5 = send(ym_r, ym_r, U1, sib)
    sb6 = send(yp_r, yp_r, U2, sib)
    arrived(lzp, yp_r, L, lo)
    sb12 = send(yp_r, yp_r, L, sib)
    arrived(lzm, ym_r, L, lo)
    sb13 = send(ym_r, ym_r, L, sib)
    arrived(txx, relay.at[2], T, lo)
    uxx = send(relay.at[2], xx_c, T, hi, K)
    arrived(yzm1, yp_r, U1, zp)
    sb14 = send(yp_r, yp_r, U1, sib)
    arrived(yzp2, ym_r, U2, zm)
    sb15 = send(ym_r, ym_r, U2, sib)
    arrived(lzz, yy_r, L, lo)
    sb7 = send(yy_r, yy_r, L, sib)
    for copy in keep:
        copy.wait()
    arrived(xm1, xp_c, Q1, xp)
    arrived(fxp, xx_c, G1, xm)
    arrived(yxm1, yp_c, U1, xp)
    arrived(sb0, rsib(col), ALL, sib)
    arrived(sb1, rsib(mate), ALL, sib)
    arrived(sb2, rsib(along_z(3)), ALL, sib)
    arrived(sb3, rsib(along_z(1)), ALL, sib)
    arrived(gzp, yy_r, V1, zm)
    sb8 = send(yy_r, yy_r, V1, sib)
    arrived(gzm, yy_r, V3, zp)
    sb9 = send(yy_r, yy_r, V3, sib)
    arrived(gxp, yy_c, V1, xm)
    arrived(sb4, rsib(along_z(2)), ALL, sib)
    arrived(sb5, rsib(other(along_z(3))), U1, sib)
    arrived(sb14, rsib(other(along_z(1))), U1, sib)
    arrived(sb8, rsib(other(along_z(2))), V1, sib)
    write_lists(table_v, pair_lists(rows_ref, cols_ref), 0)
    hand = pltpu.make_async_copy(table_v, table_ref, own_sems.at[2])
    hand.start()
    arrived(gzn, yy_r, V4, zp)
    sb10 = send(yy_r, yy_r, V4, sib)
    arrived(gzq, yy_r, V2, zm)
    sb11 = send(yy_r, yy_r, V2, sib)

    arrived(yxp2, ym_c, W2, xm)
    arrived(uxp, yp_c, K, hi)
    arrived(uxm, ym_c, K, hi)
    arrived(uxx, yy_c, K, hi)
    arrived(gxm, yy_c, W2, xp)
    arrived(gxq, yy_c, V2, xm)
    arrived(sb6, rsib(other(along_z(1))), U2, sib)
    arrived(sb12, rsib(other(along_z(1))), L, sib)
    arrived(sb13, rsib(other(along_z(3))), L, sib)
    arrived(sb15, rsib(other(along_z(3))), U2, sib)
    arrived(sb7, rsib(other(along_z(2))), L, sib)
    arrived(sb9, rsib(other(along_z(2))), V3, sib)
    arrived(sb10, rsib(other(along_z(2))), V4, sib)
    arrived(sb11, rsib(other(along_z(2))), V2, sib)
    assert waited == set(range(len(started))) and len(started) == COPIES
    for part, wait in started:
        either(part, wait)
    hand.wait()


COPIES = 58


def gather(block_mask, similarity):
    dtype = similarity.dtype
    cells = block_mask.size
    return pl.pallas_call(
        gather_kernel,
        out_shape=[
            pltpu.VMEM((17, SHARE, BLK), dtype),
            pltpu.VMEM((8, SHARE, BLK), dtype),
            pltpu.SMEM((DEPTH, BLK), jnp.int32),
        ],
        in_specs=[pl.BlockSpec(memory_space=pltpu.HBM)] * 2,
        out_specs=[
            pl.BlockSpec(memory_space=pltpu.VMEM),
            pl.BlockSpec(memory_space=pltpu.VMEM),
            pl.BlockSpec(memory_space=pltpu.SMEM),
        ],
        scratch_shapes=[
            pltpu.SMEM(block_mask.shape[::-1], jnp.int32),
            pltpu.VMEM((cells, BLK, BLK), dtype),
            pltpu.VMEM((SHARE, BLK), dtype),
            pltpu.VMEM((3, LAST_C * BLK, BLK), dtype),
            pltpu.VMEM((8, BLK), jnp.int32),
            pltpu.SMEM((8, BLK), jnp.int32),
            pltpu.SemaphoreType.DMA((COPIES,)),
            pltpu.SemaphoreType.DMA((COPIES,)),
            pltpu.SemaphoreType.DMA((3,)),
            pltpu.SemaphoreType.DMA((8,)),
            pltpu.VMEM((DEPTH, BLK), jnp.int32),
        ],
        compiler_params=pltpu.CompilerParams(
            collective_id=0, has_side_effects=True, vmem_limit_bytes=44 * MIB
        ),
        name="gather",
    )(block_mask.T, similarity)


def group_product(r_ref, c_ref, table, cell, g):
    words = [table[g * GROUP + t, cell] for t in range(GROUP)]
    return sum(
        jnp.dot(
            r_ref[(word >> 8) & 511],
            c_ref[word & 255],
            preferred_element_type=jnp.float32,
        )
        for word in words
    )


def as_blocks(ref):
    return ref.reshape(ref.shape[0] * SLOTS, BLK, BLK)


AT_ONCE = 8


def later_kernel(rows_ref, cols_ref, table_ref, extra_ref, table_v, table_s, list_s, sem):
    r_ref, c_ref = as_blocks(rows_ref), as_blocks(cols_ref)
    cells = extra_ref.shape[0] - 1

    def look(cell, found):
        list_s[found] = cell
        return found + jnp.where(length_of(table_ref, cell) > GROUP, 1, 0)

    found = lax.fori_loop(0, cells, look, jnp.int32(0), unroll=8)
    for t in range(AT_ONCE):
        list_s[found + t] = cells

    @pl.loop(0, (found + AT_ONCE - 1) // AT_ONCE)
    def _(n):
        for t in range(AT_ONCE):
            cell = list_s[n * AT_ONCE + t]
            extra_ref[cell] = group_product(r_ref, c_ref, table_ref, cell, 1)

    def add(table, cell, first):
        @pl.loop(first, (jnp.minimum(length_of(table, cell), DEPTH) + GROUP - 1) // GROUP)
        def _(g):
            extra_ref[cell] += group_product(r_ref, c_ref, table, cell, g)

    most = length_of(table_ref, BLK - 1)

    @pl.when(most > 2 * GROUP)
    def _():
        @pl.loop(0, found)
        def _(n):
            add(table_ref, list_s[n], 2)

    @pl.loop(1, (most + DEPTH - 1) // DEPTH)
    def _(d):
        write_lists(table_v, pair_lists(rows_ref, cols_ref), d * DEPTH)
        copy = pltpu.make_async_copy(table_v, table_s, sem)
        copy.start()
        copy.wait()

        @pl.loop(0, found)
        def _(n):
            add(table_s, list_s[n], 0)


VMEM, SMEM = pl.BlockSpec(memory_space=pltpu.VMEM), pl.BlockSpec(memory_space=pltpu.SMEM)


def later(rows, cols, table, cells):
    return pl.pallas_call(
        later_kernel,
        out_shape=pltpu.VMEM((cells + 1, BLK, BLK), jnp.float32),
        in_specs=[VMEM, VMEM, SMEM],
        out_specs=VMEM,
        scratch_shapes=[
            pltpu.VMEM(table.shape, jnp.int32),
            pltpu.SMEM(table.shape, jnp.int32),
            pltpu.SMEM((BLK,), jnp.int32),
            pltpu.SemaphoreType.DMA(()),
        ],
        compiler_params=pltpu.CompilerParams(vmem_limit_bytes=8 * MIB),
        name="later",
    )(rows, cols, table)


def product_kernel(
    rows_ref, cols_ref, table_ref, extra_ref, out_ref, total_ref, slots, send_sems, recv_sems
):
    row, col, layer = (lax.axis_index(a) for a in ("row", "col", "layer"))
    high, x = row // 4, row % 4
    steps = [(1, 2), (1, 1), (1, 3), (1, 0), (0, 2), (0, 1), (0, 3)]
    peers = [((high + h) % 2 * 4 + (x + d) % 4, col, layer) for h, d in steps]
    barrier = pltpu.get_barrier_semaphore()
    for peer in peers:
        pl.semaphore_signal(barrier, inc=1, device_id=peer, device_id_type=MESH)

    r_ref, c_ref = as_blocks(rows_ref), as_blocks(cols_ref)
    tiles, wide = out_ref.shape[0] // BLK, out_ref.shape[1] // BLK

    def one_row(i, sums):
        lines = pl.ds(pl.multiple_of(i * BLK, BLK), BLK)
        out = []
        for j in range(wide):
            cell = i * wide + j
            value = group_product(r_ref, c_ref, table_ref, cell, 0)
            has_more = jnp.full((BLK, BLK), length_of(table_ref, cell), jnp.int32) > GROUP
            value = value + jnp.where(has_more, extra_ref[cell], 0.0)
            value = value * value
            out_ref[lines, pl.ds(j * BLK, BLK)] = value
            out.append(sums[j] + jnp.sum(value.reshape(BLK // 8, 8, BLK), axis=0))
        return tuple(out)

    sums = tuple(jnp.zeros((8, BLK), jnp.float32) for _ in range(wide))
    sums = lax.fori_loop(0, tiles, one_row, sums, unroll=6)
    slots[row] = jnp.concatenate([jnp.sum(v, axis=0, keepdims=True) for v in sums], 1)
    pl.semaphore_wait(barrier, 7)
    copies = [
        pltpu.make_async_remote_copy(
            src_ref=slots.at[row],
            dst_ref=slots.at[row],
            send_sem=send_sems.at[k],
            recv_sem=recv_sems.at[k],
            device_id=peer,
            device_id_type=MESH,
        )
        for k, peer in enumerate(peers)
    ]
    for copy in copies:
        copy.start()
    for copy in copies:
        copy.wait()
    total = slots[0]
    for q in range(1, 8):
        total = total + slots[q]
    total_ref[...] = total


def product(rows, cols, table, extra, shape):
    lanes = shape[1]
    return pl.pallas_call(
        product_kernel,
        out_shape=[pltpu.VMEM(shape, jnp.float32), pltpu.VMEM((1, lanes), jnp.float32)],
        in_specs=[VMEM, VMEM, SMEM, VMEM],
        out_specs=[VMEM, VMEM],
        scratch_shapes=[
            pltpu.VMEM((8, 1, lanes), jnp.float32),
            pltpu.SemaphoreType.DMA((7,)),
            pltpu.SemaphoreType.DMA((7,)),
        ],
        compiler_params=pltpu.CompilerParams(
            collective_id=1, has_side_effects=True, vmem_limit_bytes=8 * MIB
        ),
        name="product",
    )(rows, cols, table, extra)


STEPS = 6


def scale_kernel(scaling, value_ref, total_ref, out_ref, staged, sems):
    step = staged.shape[1]
    factor = scaling / total_ref[...]
    copies = []
    for t in range(STEPS):
        here = pl.ds(t * step, step)
        staged[t] = value_ref[here, :] * factor
        copy = pltpu.make_async_copy(staged.at[t], out_ref.at[here], sems.at[t])
        copy.start()
        copies.append(copy)
    for copy in copies:
        copy.wait()


def scale(value, total, scaling):
    rows, lanes = value.shape
    return pl.pallas_call(
        functools.partial(scale_kernel, scaling),
        out_shape=jax.ShapeDtypeStruct(value.shape, jnp.float32),
        in_specs=[pl.BlockSpec(memory_space=pltpu.VMEM)] * 2,
        out_specs=pl.BlockSpec(memory_space=pltpu.HBM),
        scratch_shapes=[
            pltpu.VMEM((STEPS, rows // STEPS, lanes), jnp.float32),
            pltpu.SemaphoreType.DMA((STEPS,)),
        ],
        compiler_params=pltpu.CompilerParams(vmem_limit_bytes=16 * MIB),
        name="scale",
    )(value, total)


def body(similarity, block_mask):
    rows, cols, table = gather(block_mask, similarity)
    extra = later(rows, cols, table, block_mask.size)
    value, total = product(rows, cols, table, extra, similarity.shape)
    scaling = similarity.shape[0] * lax.axis_size("row")
    return scale(value, total, float(scaling))


def solution(mesh):
    return jax.shard_map(
        body,
        mesh=mesh,
        in_specs=(P("row", ("col", "layer")), P("row", ("col", "layer"))),
        out_specs=P("row", ("col", "layer")),
        check_vma=False,
    )
```

```python
import functools

import jax
import jax.numpy as jnp
from jax import lax
from jax.experimental import pallas as pl
from jax.experimental.pallas import tpu as pltpu
from jax.sharding import PartitionSpec as P

BLK = 128
MAXNZ = 18
HEAD = 32
HALF = MAXNZ // 2
SLOTS = MAXNZ + 1
SHARE = SLOTS * BLK
TOP = BLK - HEAD
GROUP = 4
DEPTH = 16
FIELD = 256
COUNT = 512 * FIELD
MIB = 1 << 20
MESH = pl.DeviceIdType.MESH


def pack_share(mask_ref, x_ref, mask_s, x_v, share, place_v, place_s, signal, sems):
    cols, rows = mask_ref.shape
    fetch = pltpu.make_async_copy(mask_ref, mask_s, sems.at[cols + 1])
    fetch.start()
    strips = x_v.reshape(cols * rows * BLK, BLK)
    loads = [
        pltpu.make_async_copy(
            x_ref.at[:, pl.ds(j * BLK, BLK)],
            strips.at[pl.ds(j * rows * BLK, rows * BLK)],
            sems.at[j],
        )
        for j in range(cols)
    ]
    for load in loads:
        load.start()
    signal()
    sub = lax.broadcasted_iota(jnp.int32, (HEAD, BLK), 0)
    lane = lax.broadcasted_iota(jnp.int32, (HEAD, BLK), 1)
    lane_row = (lane * 43) >> 8
    lane_col = lane - lane_row * cols
    lane8 = lane[:8]

    def find(i, carry):
        count, place = carry
        for j in range(cols):
            here = mask_s[j, i]
            place = place + jnp.where(lane8 == count, here * (j * rows + i), 0)
            count = count + here
        return count, place

    fetch.wait()
    zero = jnp.int32(0)
    _, place = lax.fori_loop(0, rows, find, (zero, jnp.zeros((8, BLK), jnp.int32)), unroll=3)
    place_v[...] = place
    move = pltpu.make_async_copy(place_v, place_s, sems.at[cols])
    move.start()

    def mark(i, carry):
        count, head = carry
        below = 8 + jnp.where(i < cols, i, i - cols + 8)
        for j in range(cols):
            here = mask_s[j, i]
            cell = ((sub == j) & (lane_row == i)) | ((sub == below) & (lane_col == j))
            head = head + jnp.where(cell, here * (count + 1), 0)
            count = count + here
        return count, head

    _, head = lax.fori_loop(0, rows, mark, (zero, jnp.zeros((HEAD, BLK), jnp.int32)))
    head = jnp.where(lane < rows * cols, head, 0)
    share[pl.ds(TOP, HEAD), :] = head.astype(jnp.float32).astype(share.dtype)
    move.wait()
    for load in loads:
        load.wait()
    for s in range(MAXNZ):
        share[pl.ds((s + 1) * BLK, BLK), :] = x_v[place_s[0, s]]


def pair_lists(rows_ref, cols_ref):
    hr, hc = [], []
    for q in range(16):
        hr.append(rows_ref[q, pl.ds(TOP, HEAD), :].astype(jnp.float32)[0:8])
    for q in range(8):
        top = cols_ref[q, pl.ds(TOP, HEAD), :].astype(jnp.float32)
        hc += [top[8:16], top[16:24]]
    hr, hc = jnp.concatenate(hr, 0), jnp.concatenate(hc, 0)
    both = jnp.where((hr > 0) & (hc > 0), 1.0, 0.0)
    line = lax.broadcasted_iota(jnp.int32, (BLK, BLK), 0)
    before = line > lax.broadcasted_iota(jnp.int32, (BLK, BLK), 1)
    rank = jnp.dot(
        jnp.where(before, 1.0, 0.0).astype(jnp.bfloat16),
        both.astype(jnp.bfloat16),
        preferred_element_type=jnp.float32,
    )
    rank = jnp.where(both > 0, rank, -1.0).astype(jnp.int32)
    place_r = (line >> 3) * SLOTS + hr.astype(jnp.int32)
    place_c = (line >> 4) * SLOTS + hc.astype(jnp.int32)
    count = jnp.sum(both, axis=0, keepdims=True).astype(jnp.int32)
    return rank, place_r * FIELD + place_c, count


def write_lists(table_v, lists, done):
    rank, place, count = lists
    most = jnp.max(count, axis=1, keepdims=True)
    lane = lax.broadcasted_iota(jnp.int32, count.shape, 1)
    for p in range(DEPTH):
        one = jnp.sum(jnp.where(rank == done + p, place, 0), axis=0, keepdims=True)
        one = jnp.where(count > done + p, one, IDLE)
        if p == 0:
            length = jnp.where(lane == BLK - 1, most, jnp.maximum(count - done, 0))
            one = one + COUNT * length
        table_v[pl.ds(p, 1), :] = one


IDLE = 16 * SLOTS * FIELD + 1


def length_of(table, cell):
    return table[0, cell] >> 17


LAST_R = 5
LAST_C = 4
SPLIT = 7
SHIFT_Z = 2
SHIFT_X = 1


def span(first, last):
    low = (first + 1) * BLK if first else TOP
    return pl.ds(low, (last + 1) * BLK - low)


def gather_kernel(
    mask_ref,
    x_ref,
    rows_ref,
    cols_ref,
    table_ref,
    mask_s,
    x_v,
    share_ref,
    relay,
    place_v,
    place_s,
    send_sems,
    recv_sems,
    own_sems,
    pack_sems,
    table_v,
):
    row, col, layer = (lax.axis_index(a) for a in ("row", "col", "layer"))
    high, x = row // 4, row % 4
    z, low = col // 2, col % 2

    def along_z(step):
        return 2 * ((z + step) % 4) + low

    def along_x(step):
        return 4 * high + (x + step) % 4

    mate = 2 * z + 1 - low
    far = 4 * (1 - high) + x

    zp, zm = (row, along_z(1), layer), (row, along_z(3), layer)
    xp, xm = (along_x(1), col, layer), (along_x(3), col, layer)
    lo, hi = (row, mate, layer), (far, mate, layer)
    sib = (row, col, 1 - layer)

    barrier = pltpu.get_barrier_semaphore()

    def signal():
        for peer in (zp, zm, xp, xm, lo, hi, sib):
            pl.semaphore_signal(barrier, inc=1, device_id=peer, device_id_type=MESH)

    pack_share(mask_ref, x_ref, mask_s, x_v, share_ref, place_v, place_s, signal, pack_sems)
    pl.semaphore_wait(barrier, 7)

    ALL = span(0, MAXNZ)
    mine = 2 * col + layer
    keep = [
        pltpu.make_async_copy(share_ref.at[ALL], rows_ref.at[mine].at[ALL], own_sems.at[0]),
        pltpu.make_async_copy(share_ref.at[ALL], cols_ref.at[row].at[ALL], own_sems.at[1]),
    ]

    EARLY, EARLY_C = MAXNZ - LAST_R, MAXNZ - LAST_C
    H1, H2 = span(0, HALF), span(HALF, MAXNZ)
    U1, U2, L = span(0, SPLIT), span(SPLIT, EARLY), span(EARLY, MAXNZ)
    V1, V2, V3, V4 = span(0, 4), span(4, SPLIT), span(SPLIT, 10), span(10, EARLY)
    W2, K = span(SPLIT, EARLY_C), span(EARLY_C, MAXNZ)
    T = pl.ds(0, LAST_C * BLK)
    started = []
    waited = set()

    def either(part, act):
        if isinstance(part, tuple):
            flag, held, plain = part
            pl.when(flag)(lambda: act(held))
            pl.when(jnp.logical_not(flag))(lambda: act(plain))
        else:
            act(part)

    def copy_of(k, src, dst, part, into, peer):
        return pltpu.make_async_remote_copy(
            src_ref=src.at[part],
            dst_ref=dst.at[part if into is None else into],
            send_sem=send_sems.at[k],
            recv_sem=recv_sems.at[k],
            device_id=peer,
            device_id_type=MESH,
        )

    def send(src, dst, part, peer, into=None):
        k = len(started)
        either(part, lambda p: copy_of(k, src, dst, p, into, peer).start())
        started.append((part, lambda p: copy_of(k, src, dst, p, into, peer).wait_send()))
        return k

    def arrived(k, dst, part, peer):
        waited.add(k)
        either(part, lambda p: copy_of(k, dst, dst, p, None, peer).wait_recv())

    def halves(place, shift):
        cut = HALF - shift
        pairs = []
        for step in (0, 3, 1, 2):
            flag = (place + step) % 4 == 2
            pairs.append(((flag, span(0, cut), H1), (flag, span(cut, MAXNZ), H2)))
        return pairs

    (A1, A2), (M1, M2), (P1, P2), (F1, F2) = halves(z, SHIFT_Z)
    (B1, B2), (N1, N2), (Q1, Q2), (G1, G2) = halves(x, SHIFT_X)

    def other(q):
        return q + 1 - 2 * (q % 2)

    def r(q):
        return rows_ref.at[2 * q + layer]

    def rsib(q):
        return rows_ref.at[2 * q + 1 - layer]

    def c(q):
        return cols_ref.at[q]

    def across(q):
        return c((q + 4) % 8)

    own_r, own_c = r(col), c(row)
    y_r, y_c = r(mate), c(far)
    zm_r, zp_r, zz_r = (r(along_z(s)) for s in (3, 1, 2))
    ym_r, yp_r, yy_r = (r(other(along_z(s))) for s in (3, 1, 2))
    xm_c, xp_c, xx_c = (c(along_x(s)) for s in (3, 1, 2))
    ym_c, yp_c, yy_c = (across(along_x(s)) for s in (3, 1, 2))

    lo1 = send(share_ref, own_r, U1, lo)
    zp1 = send(share_ref, own_r, A1, zp)
    zm2 = send(share_ref, own_r, A2, zm)
    xp1 = send(share_ref, own_c, B1, xp)
    xm2 = send(share_ref, own_c, B2, xm)
    lo2 = send(share_ref, own_r, U2, lo)
    zp2 = send(share_ref, own_r, A2, zp)
    zm1 = send(share_ref, own_r, A1, zm)
    xp2 = send(share_ref, own_c, B2, xp)
    xm1 = send(share_ref, own_c, B1, xm)
    lo3 = send(share_ref, own_r, L, lo)
    sb0 = send(share_ref, own_r, ALL, sib)
    for copy in keep:
        copy.start()
    rows_ref[16, pl.ds(0, BLK), :] = jnp.zeros((BLK, BLK), rows_ref.dtype)

    arrived(lo1, y_r, U1, lo)
    hi1 = send(y_r, own_c, U1, hi)
    yzp1 = send(y_r, y_r, U1, zp)
    arrived(zp1, zm_r, M1, zm)
    fzp = send(zm_r, zm_r, M1, zp)
    arrived(zm2, zp_r, P2, zp)
    fzm = send(zp_r, zp_r, P2, zm)
    arrived(xp1, xm_c, N1, xm)
    fxp = send(xm_c, xm_c, N1, xp)
    arrived(xm2, xp_c, Q2, xp)
    fxm = send(xp_c, xp_c, Q2, xm)
    txp = send(xp_c, relay.at[0], K, lo, T)
    lzp = send(zp_r, zp_r, L, lo)
    arrived(lo2, y_r, U2, lo)
    hi2 = send(y_r, own_c, U2, hi)
    yzm2 = send(y_r, y_r, U2, zm)
    yzp2 = send(y_r, y_r, U2, zp)
    yzm1 = send(y_r, y_r, U1, zm)
    arrived(hi1, y_c, U1, hi)
    yxp1 = send(y_c, y_c, U1, xp)
    arrived(lo3, y_r, L, lo)
    hi3 = send(y_r, own_c, L, hi)
    sb1 = send(y_r, y_r, ALL, sib)

    arrived(zp2, zm_r, M2, zm)
    arrived(xp2, xm_c, N2, xm)
    txm = send(xm_c, relay.at[1], K, lo, T)
    lzm = send(zm_r, zm_r, L, lo)
    sb2 = send(zm_r, zm_r, ALL, sib)
    arrived(zm1, zp_r, P1, zp)
    sb3 = send(zp_r, zp_r, ALL, sib)
    arrived(hi2, y_c, U2, hi)
    arrived(hi3, y_c, L, hi)
    yxm2 = send(y_c, y_c, W2, xm)
    yxp2 = send(y_c, y_c, W2, xp)
    yxm1 = send(y_c, y_c, U1, xm)
    arrived(txp, relay.at[0], T, lo)
    uxp = send(relay.at[0], xp_c, T, hi, K)
    arrived(fxm, xx_c, G2, xp)
    txx = send(xx_c, relay.at[2], K, lo, T)
    arrived(fzm, zz_r, F2, zp)
    lzz = send(zz_r, zz_r, L, lo)
    arrived(fzp, zz_r, F1, zm)
    sb4 = send(zz_r, zz_r, ALL, sib)
    arrived(txm, relay.at[1], T, lo)
    uxm = send(relay.at[1], xm_c, T, hi, K)

    arrived(yzp1, ym_r, U1, zm)
    gzp = send(ym_r, ym_r, V1, zp)
    gzq = send(ym_r, ym_r, V2, zp)
    arrived(yzm2, yp_r, U2, zp)
    gzm = send(yp_r, yp_r, V3, zm)
    gzn = send(yp_r, yp_r, V4, zm)
    arrived(yxp1, ym_c, U1, xm)
    gxp = send(ym_c, ym_c, V1, xp)
    gxq = send(ym_c, ym_c, V2, xp)
    arrived(yxm2, yp_c, W2, xp)
    gxm = send(yp_c, yp_c, W2, xm)
    sb5 = send(ym_r, ym_r, U1, sib)
    sb6 = send(yp_r, yp_r, U2, sib)
    arrived(lzp, yp_r, L, lo)
    sb12 = send(yp_r, yp_r, L, sib)
    arrived(lzm, ym_r, L, lo)
    sb13 = send(ym_r, ym_r, L, sib)
    arrived(txx, relay.at[2], T, lo)
    uxx = send(relay.at[2], xx_c, T, hi, K)
    arrived(yzm1, yp_r, U1, zp)
    sb14 = send(yp_r, yp_r, U1, sib)
    arrived(yzp2, ym_r, U2, zm)
    sb15 = send(ym_r, ym_r, U2, sib)
    arrived(lzz, yy_r, L, lo)
    sb7 = send(yy_r, yy_r, L, sib)
    for copy in keep:
        copy.wait()
    arrived(xm1, xp_c, Q1, xp)
    arrived(fxp, xx_c, G1, xm)
    arrived(yxm1, yp_c, U1, xp)
    arrived(sb0, rsib(col), ALL, sib)
    arrived(sb1, rsib(mate), ALL, sib)
    arrived(sb2, rsib(along_z(3)), ALL, sib)
    arrived(sb3, rsib(along_z(1)), ALL, sib)
    arrived(gzp, yy_r, V1, zm)
    sb8 = send(yy_r, yy_r, V1, sib)
    arrived(gzm, yy_r, V3, zp)
    sb9 = send(yy_r, yy_r, V3, sib)
    arrived(gxp, yy_c, V1, xm)
    arrived(sb4, rsib(along_z(2)), ALL, sib)
    arrived(sb5, rsib(other(along_z(3))), U1, sib)
    arrived(sb14, rsib(other(along_z(1))), U1, sib)
    arrived(sb8, rsib(other(along_z(2))), V1, sib)
    write_lists(table_v, pair_lists(rows_ref, cols_ref), 0)
    hand = pltpu.make_async_copy(table_v, table_ref, own_sems.at[2])
    hand.start()
    arrived(gzn, yy_r, V4, zp)
    sb10 = send(yy_r, yy_r, V4, sib)
    arrived(gzq, yy_r, V2, zm)
    sb11 = send(yy_r, yy_r, V2, sib)

    arrived(yxp2, ym_c, W2, xm)
    arrived(uxp, yp_c, K, hi)
    arrived(uxm, ym_c, K, hi)
    arrived(uxx, yy_c, K, hi)
    arrived(gxm, yy_c, W2, xp)
    arrived(gxq, yy_c, V2, xm)
    arrived(sb6, rsib(other(along_z(1))), U2, sib)
    arrived(sb12, rsib(other(along_z(1))), L, sib)
    arrived(sb13, rsib(other(along_z(3))), L, sib)
    arrived(sb15, rsib(other(along_z(3))), U2, sib)
    arrived(sb7, rsib(other(along_z(2))), L, sib)
    arrived(sb9, rsib(other(along_z(2))), V3, sib)
    arrived(sb10, rsib(other(along_z(2))), V4, sib)
    arrived(sb11, rsib(other(along_z(2))), V2, sib)
    assert waited == set(range(len(started))) and len(started) == COPIES
    for part, wait in started:
        either(part, wait)
    hand.wait()


COPIES = 58


def gather(block_mask, similarity):
    dtype = similarity.dtype
    cells = block_mask.size
    return pl.pallas_call(
        gather_kernel,
        out_shape=[
            pltpu.VMEM((17, SHARE, BLK), dtype),
            pltpu.VMEM((8, SHARE, BLK), dtype),
            pltpu.SMEM((DEPTH, BLK), jnp.int32),
        ],
        in_specs=[pl.BlockSpec(memory_space=pltpu.HBM)] * 2,
        out_specs=[
            pl.BlockSpec(memory_space=pltpu.VMEM),
            pl.BlockSpec(memory_space=pltpu.VMEM),
            pl.BlockSpec(memory_space=pltpu.SMEM),
        ],
        scratch_shapes=[
            pltpu.SMEM(block_mask.shape[::-1], jnp.int32),
            pltpu.VMEM((cells, BLK, BLK), dtype),
            pltpu.VMEM((SHARE, BLK), dtype),
            pltpu.VMEM((3, LAST_C * BLK, BLK), dtype),
            pltpu.VMEM((8, BLK), jnp.int32),
            pltpu.SMEM((8, BLK), jnp.int32),
            pltpu.SemaphoreType.DMA((COPIES,)),
            pltpu.SemaphoreType.DMA((COPIES,)),
            pltpu.SemaphoreType.DMA((3,)),
            pltpu.SemaphoreType.DMA((8,)),
            pltpu.VMEM((DEPTH, BLK), jnp.int32),
        ],
        compiler_params=pltpu.CompilerParams(
            collective_id=0, has_side_effects=True, vmem_limit_bytes=44 * MIB
        ),
        name="gather",
    )(block_mask.T, similarity)


def group_product(r_ref, c_ref, table, cell, g):
    words = [table[g * GROUP + t, cell] for t in range(GROUP)]
    return sum(
        jnp.dot(
            r_ref[(word >> 8) & 511],
            c_ref[word & 255],
            preferred_element_type=jnp.float32,
        )
        for word in words
    )


def as_blocks(ref):
    return ref.reshape(ref.shape[0] * SLOTS, BLK, BLK)


AT_ONCE = 8


def later_kernel(rows_ref, cols_ref, table_ref, extra_ref, table_v, table_s, list_s, sem):
    r_ref, c_ref = as_blocks(rows_ref), as_blocks(cols_ref)
    cells = extra_ref.shape[0] - 1

    def look(cell, found):
        list_s[found] = cell
        return found + jnp.where(length_of(table_ref, cell) > GROUP, 1, 0)

    found = lax.fori_loop(0, cells, look, jnp.int32(0), unroll=8)
    for t in range(AT_ONCE):
        list_s[found + t] = cells

    @pl.loop(0, (found + AT_ONCE - 1) // AT_ONCE)
    def _(n):
        for t in range(AT_ONCE):
            cell = list_s[n * AT_ONCE + t]
            extra_ref[cell] = group_product(r_ref, c_ref, table_ref, cell, 1)

    def add(table, cell, first):
        @pl.loop(first, (jnp.minimum(length_of(table, cell), DEPTH) + GROUP - 1) // GROUP)
        def _(g):
            extra_ref[cell] += group_product(r_ref, c_ref, table, cell, g)

    most = length_of(table_ref, BLK - 1)

    @pl.when(most > 2 * GROUP)
    def _():
        @pl.loop(0, found)
        def _(n):
            add(table_ref, list_s[n], 2)

    @pl.loop(1, (most + DEPTH - 1) // DEPTH)
    def _(d):
        write_lists(table_v, pair_lists(rows_ref, cols_ref), d * DEPTH)
        copy = pltpu.make_async_copy(table_v, table_s, sem)
        copy.start()
        copy.wait()

        @pl.loop(0, found)
        def _(n):
            add(table_s, list_s[n], 0)


VMEM, SMEM = pl.BlockSpec(memory_space=pltpu.VMEM), pl.BlockSpec(memory_space=pltpu.SMEM)


def later(rows, cols, table, cells):
    return pl.pallas_call(
        later_kernel,
        out_shape=pltpu.VMEM((cells + 1, BLK, BLK), jnp.float32),
        in_specs=[VMEM, VMEM, SMEM],
        out_specs=VMEM,
        scratch_shapes=[
            pltpu.VMEM(table.shape, jnp.int32),
            pltpu.SMEM(table.shape, jnp.int32),
            pltpu.SMEM((BLK,), jnp.int32),
            pltpu.SemaphoreType.DMA(()),
        ],
        compiler_params=pltpu.CompilerParams(vmem_limit_bytes=8 * MIB),
        name="later",
    )(rows, cols, table)


def product_kernel(
    rows_ref, cols_ref, table_ref, extra_ref, out_ref, total_ref, slots, send_sems, recv_sems
):
    row, col, layer = (lax.axis_index(a) for a in ("row", "col", "layer"))
    high, x = row // 4, row % 4
    steps = [(1, 2), (1, 1), (1, 3), (1, 0), (0, 2), (0, 1), (0, 3)]
    peers = [((high + h) % 2 * 4 + (x + d) % 4, col, layer) for h, d in steps]
    barrier = pltpu.get_barrier_semaphore()
    for peer in peers:
        pl.semaphore_signal(barrier, inc=1, device_id=peer, device_id_type=MESH)

    r_ref, c_ref = as_blocks(rows_ref), as_blocks(cols_ref)
    tiles, wide = out_ref.shape[0] // BLK, out_ref.shape[1] // BLK

    def one_row(i, sums):
        lines = pl.ds(pl.multiple_of(i * BLK, BLK), BLK)
        out = []
        for j in range(wide):
            cell = i * wide + j
            value = group_product(r_ref, c_ref, table_ref, cell, 0)
            has_more = jnp.full((BLK, BLK), length_of(table_ref, cell), jnp.int32) > GROUP
            value = value + jnp.where(has_more, extra_ref[cell], 0.0)
            value = value * value
            out_ref[lines, pl.ds(j * BLK, BLK)] = value
            out.append(sums[j] + jnp.sum(value.reshape(BLK // 8, 8, BLK), axis=0))
        return tuple(out)

    sums = tuple(jnp.zeros((8, BLK), jnp.float32) for _ in range(wide))
    sums = lax.fori_loop(0, tiles, one_row, sums, unroll=12)
    slots[row] = jnp.concatenate([jnp.sum(v, axis=0, keepdims=True) for v in sums], 1)
    pl.semaphore_wait(barrier, 7)
    copies = [
        pltpu.make_async_remote_copy(
            src_ref=slots.at[row],
            dst_ref=slots.at[row],
            send_sem=send_sems.at[k],
            recv_sem=recv_sems.at[k],
            device_id=peer,
            device_id_type=MESH,
        )
        for k, peer in enumerate(peers)
    ]
    for copy in copies:
        copy.start()
    for copy in copies:
        copy.wait()
    total = slots[0]
    for q in range(1, 8):
        total = total + slots[q]
    total_ref[...] = total


def product(rows, cols, table, extra, shape):
    lanes = shape[1]
    return pl.pallas_call(
        product_kernel,
        out_shape=[pltpu.VMEM(shape, jnp.float32), pltpu.VMEM((1, lanes), jnp.float32)],
        in_specs=[VMEM, VMEM, SMEM, VMEM],
        out_specs=[VMEM, VMEM],
        scratch_shapes=[
            pltpu.VMEM((8, 1, lanes), jnp.float32),
            pltpu.SemaphoreType.DMA((7,)),
            pltpu.SemaphoreType.DMA((7,)),
        ],
        compiler_params=pltpu.CompilerParams(
            collective_id=1, has_side_effects=True, vmem_limit_bytes=8 * MIB
        ),
        name="product",
    )(rows, cols, table, extra)


STEPS = 6


def scale_kernel(scaling, value_ref, total_ref, out_ref, staged, sems):
    step = staged.shape[1]
    factor = scaling / total_ref[...]
    copies = []
    for t in range(STEPS):
        here = pl.ds(t * step, step)
        staged[t] = value_ref[here, :] * factor
        copy = pltpu.make_async_copy(staged.at[t], out_ref.at[here], sems.at[t])
        copy.start()
        copies.append(copy)
    for copy in copies:
        copy.wait()


def scale(value, total, scaling):
    rows, lanes = value.shape
    return pl.pallas_call(
        functools.partial(scale_kernel, scaling),
        out_shape=jax.ShapeDtypeStruct(value.shape, jnp.float32),
        in_specs=[pl.BlockSpec(memory_space=pltpu.VMEM)] * 2,
        out_specs=pl.BlockSpec(memory_space=pltpu.HBM),
        scratch_shapes=[
            pltpu.VMEM((STEPS, rows // STEPS, lanes), jnp.float32),
            pltpu.SemaphoreType.DMA((STEPS,)),
        ],
        compiler_params=pltpu.CompilerParams(vmem_limit_bytes=16 * MIB),
        name="scale",
    )(value, total)


def body(similarity, block_mask):
    rows, cols, table = gather(block_mask, similarity)
    extra = later(rows, cols, table, block_mask.size)
    value, total = product(rows, cols, table, extra, similarity.shape)
    scaling = similarity.shape[0] * lax.axis_size("row")
    return scale(value, total, float(scaling))


def solution(mesh):
    return jax.shard_map(
        body,
        mesh=mesh,
        in_specs=(P("row", ("col", "layer")), P("row", ("col", "layer"))),
        out_specs=P("row", ("col", "layer")),
        check_vma=False,
    )
```
